512 devices in a mesh: row: 32 (over z, x_hi), col: 16 (over x_lo, y, core).
Axes of the slice: x: 4 (x_hi: 2, x_lo: 2; x = x_hi * 2 + x_lo), y: 4, z: 16, core: 2. Of those that a mesh axis runs over, the one named last changes fastest.
Arguments:
- tokens: bfloat16 [8192, 8192], P('row', 'col'), may hold values from -560 to 560
- norm_gain: bfloat16 [8192], P('col'), may hold values from 0.25 to 1.75
- w_query: bfloat16 [8192, 4096], P('row', 'col'), may hold values from -21 to 21
- w_key: bfloat16 [8192, 512], P('row'), may hold values from -1 to 1
- w_value: bfloat16 [8192, 512], P('row'), may hold values from -0.0625 to 0.0625
Outputs:
- attended: bfloat16 [8192, 4096], P('row', 'col')
The draws below stay inside these ranges and needn't reach their ends.
All inputs are finite; a program needn't handle non-finite values.
Results may differ from the reference program's by a relative error of at most 0.008.
Values may be sent and summed in bfloat16 or wider, within the bound.
No kernel may reach another device: no remote copies, remote signals or barrier semaphores. Data moves between devices by JAX's collectives and lax.ppermute only.
A program may use at most 64 MiB of HBM per device.

```python
import math
import jax
import jax.numpy as jnp
from jax import lax

D = 8192
HEAD = 128
HQ = 32
GROUP = 8
HK = 4
SEQ = 8192


def shared_keys(key):
    return jax.random.truncated_normal(key, -4.0, 4.0, (D, HK * HEAD), jnp.float32) / math.sqrt(D)


def draw_w_key(key, part):
    return shared_keys(key).astype(jnp.bfloat16)


def draw_w_query(key, part):
    key = jax.random.fold_in(key, 7)
    noise_key = jax.random.fold_in(key, 0)
    noise = jax.random.truncated_normal(noise_key, -4.0, 4.0, (D, HQ * HEAD), jnp.float32) / math.sqrt(D)
    result = noise
    return result.astype(jnp.bfloat16)


def draw_tokens(key, part):
    key = jax.random.fold_in(key, 11)
    base_key, row_key, col_key = jax.random.split(key, 3)
    row_scale = jnp.exp(jax.random.uniform(row_key, (SEQ, 1), jnp.float32) * math.log(10.0))
    rough = jax.random.uniform(col_key, (1, D), jnp.float32, -0.3, 0.3)
    col_scale = jnp.exp(math.log(10.0) * jnp.arange(D, dtype=jnp.float32)[None, :] / D + rough)
    base = jax.random.truncated_normal(base_key, -4.0, 4.0, (SEQ, D), jnp.float32)
    return (base * row_scale * col_scale).astype(jnp.bfloat16)


def levels(own_key, dims, pieces, least, largest):
    def one(position, shards_of):
        heights = jax.random.uniform(jax.random.fold_in(jax.random.fold_in(own_key, 6), position), (shards_of,), jnp.float32, least / len(pieces), largest / len(pieces))
        return jnp.repeat(jnp.exp(heights), dims[position] // shards_of).reshape((-1,) + (1,) * (len(dims) - position - 1))

    gain = one(*pieces[0])
    for cut in pieces[1:]:
        gain = gain * one(*cut)
    return gain


def bell_draw(own_key, extent, scale, reach, cuts=(), kind=jnp.bfloat16):
    gain = levels(own_key, extent, cuts, -0.22, 0.18) if cuts else 1.0
    array = jax.random.normal(own_key, extent, jnp.float32) * scale * gain
    return jnp.minimum(jnp.maximum(array, -reach), reach).astype(kind)


def setup_inputs(seed: int = 0) -> dict:
    arg_keys = jax.random.split(jax.random.key(seed), 6)
    tokens = draw_tokens(jax.random.fold_in(arg_keys[5], 71), 0)
    norm_gain = jnp.clip(1.0 + 0.15 * jax.random.normal(arg_keys[1], (D,), jnp.float32), 0.25, 1.75).astype(jnp.bfloat16)
    w_query = draw_w_query(jax.random.fold_in(arg_keys[5], 71), 0)
    w_key = draw_w_key(jax.random.fold_in(arg_keys[5], 71), 0)
    w_value = bell_draw(arg_keys[4], (D, HK * HEAD), D ** -0.5, 0.0625, ((0, 32),))
    return {"tokens": tokens, "norm_gain": norm_gain, "w_query": w_query, "w_key": w_key, "w_value": w_value}


def reference(tokens, norm_gain, w_query, w_key, w_value):
    states = tokens.astype(jnp.float32)
    mean_sq = lax.optimization_barrier(jnp.mean(states * states, axis=1, keepdims=True))
    normed = (states * lax.rsqrt(mean_sq + 1e-05) * norm_gain.astype(jnp.float32)[None, :]).astype(jnp.bfloat16)
    queries = jnp.dot(normed, w_query, preferred_element_type=jnp.float32).astype(jnp.bfloat16)
    keys_all = jnp.dot(normed, w_key, preferred_element_type=jnp.float32).astype(jnp.bfloat16)
    values_all = jnp.dot(normed, w_value, preferred_element_type=jnp.float32).astype(jnp.bfloat16)
    positions = jnp.arange(SEQ, dtype=jnp.int32)
    causal = positions[:, None] >= positions[None, :]
    factor = HEAD ** (-0.5)

    def one_head(head_index):
        kv_index = head_index // GROUP
        q_head = lax.dynamic_slice_in_dim(queries, head_index * HEAD, HEAD, 1)
        k_head = lax.dynamic_slice_in_dim(keys_all, kv_index * HEAD, HEAD, 1)
        v_head = lax.dynamic_slice_in_dim(values_all, kv_index * HEAD, HEAD, 1)
        scores = jnp.dot(q_head, k_head.T, preferred_element_type=jnp.float32) * factor
        masked = jnp.where(causal, scores, -jnp.inf)
        row_max = lax.optimization_barrier(jnp.max(masked, axis=1, keepdims=True))
        weights = jnp.where(causal, jnp.exp(scores - row_max), 0.0)
        totals = lax.optimization_barrier(jnp.sum(weights, axis=1, keepdims=True))
        mixed = jnp.dot(weights.astype(jnp.bfloat16), v_head, preferred_element_type=jnp.float32) / totals
        return mixed.astype(jnp.bfloat16)
    per_head = lax.map(one_head, jnp.arange(HQ, dtype=jnp.int32))
    return jnp.transpose(per_head, (1, 0, 2)).reshape(SEQ, HQ * HEAD)
```

```python
import functools
import math

import jax
import jax.numpy as jnp
from jax import lax
from jax.experimental import pallas as pl
from jax.experimental.pallas import tpu as pltpu
from jax.sharding import Mesh
from jax.sharding import PartitionSpec as P

HEAD = 128
GROUP = 8
EPS = 1e-05
ROW = ("zh", "zl", "xh")
COL = ("xl", "yh", "yl", "core")
F32 = jnp.float32
BF16 = jnp.bfloat16


def gather(x, axes, n):
    return lax.all_to_all(jnp.broadcast_to(x[None], (n, *x.shape)), axes, 0, 0)


def swap(x):
    return lax.ppermute(x, "core", [(0, 1), (1, 0)])


def attend_kernel(place, q_ref, mine_ref, other_ref, out_ref, q_all, m_ref, l_ref, acc_ref):
    z, xh, core = place[0], place[1], place[2]
    rows = q_ref.shape[0]
    scale = HEAD**-0.5 * math.log2(math.e)
    q_all[:rows] = q_ref[:, :HEAD]
    q_all[rows:] = q_ref[:, HEAD:]
    m_ref[...] = jnp.full(m_ref.shape, -1e30, F32)
    l_ref[...] = jnp.zeros(l_ref.shape, F32)
    acc_ref[...] = jnp.zeros(acc_ref.shape, F32)
    chunk = mine_ref.shape[3]
    half = 4 * chunk

    def block(zi, masked):
        zl, zh = lax.rem(zi, 4), lax.div(zi, 4)
        kv = jnp.concatenate(
            [mine_ref[:, zl, zh].reshape(half, 2 * HEAD), other_ref[:, zl, zh].reshape(half, 2 * HEAD)], axis=0
        )
        s = lax.dot_general(q_all[...], kv[:, :HEAD], (((1,), (1,)), ((), ())), preferred_element_type=F32)
        if masked:
            slot = lax.broadcasted_iota(jnp.int32, s.shape, 1)
            within = lax.rem(slot, half)
            owner = jnp.where(slot < half, core, 1 - core)
            key_pos = (lax.div(within, chunk) * 2 + owner) * chunk + lax.rem(within, chunk)
            query_pos = xh * rows + lax.rem(lax.broadcasted_iota(jnp.int32, s.shape, 0), rows)
            s = jnp.where(key_pos <= query_pos, s, -1e30)
        m_old = m_ref[...]
        m_new = jnp.maximum(m_old, jnp.max(s, axis=1, keepdims=True))
        alpha = jnp.exp2((m_old - m_new) * scale)
        total = l_ref[...] * alpha
        weights = []
        for j in range(0, s.shape[1], HEAD):
            w = jnp.exp2((s[:, j : j + HEAD] - m_new) * scale)
            total = total + w
            weights.append(w.astype(BF16))
        p = jnp.concatenate(weights, axis=1)
        l_ref[...] = total
        m_ref[...] = m_new
        acc_ref[...] = acc_ref[...] * alpha + jnp.dot(p, kv[:, HEAD:], preferred_element_type=F32)

    @pl.loop(0, z)
    def _(zi):
        block(zi, False)

    block(z, True)
    total = jnp.sum(l_ref[...], axis=1, keepdims=True)
    result = (acc_ref[...] / total).astype(BF16)
    out_ref[:, :HEAD] = result[:rows]
    out_ref[:, HEAD:] = result[rows:]


def attend(place, q, mine, other):
    rows = q.shape[0]
    vmem = pl.BlockSpec(memory_space=pltpu.VMEM)
    return pl.pallas_call(
        attend_kernel,
        out_shape=jax.ShapeDtypeStruct(q.shape, BF16),
        in_specs=[pl.BlockSpec(memory_space=pltpu.SMEM), vmem, vmem, vmem],
        out_specs=vmem,
        scratch_shapes=[
            pltpu.VMEM((2 * rows, HEAD), BF16),
            pltpu.VMEM((2 * rows, HEAD), F32),
            pltpu.VMEM((2 * rows, HEAD), F32),
            pltpu.VMEM((2 * rows, HEAD), F32),
        ],
        compiler_params=pltpu.CompilerParams(vmem_limit_bytes=40 * 1024 * 1024),
        cost_estimate=pl.CostEstimate(flops=2**31, bytes_accessed=2**22, transcendentals=2**22),
    )(place, q, mine, other)


def on_device(tokens, norm_gain, w_query, w_key, w_value):
    at = lax.axis_index
    z, xh, core = at(("zh", "zl")), at("xh"), at("core")
    rows, feats = tokens.shape
    q_cols = w_query.shape[1]
    half = w_query.shape[0] // 2

    with jax.named_scope("weights"):
        wq = lax.all_to_all(w_query.reshape(2, half, q_cols), "core", 0, 0)
        head = at(("xl", "yh"))
        start = (core * half, head * HEAD)
        wkv = jnp.where(
            at("yl") == 0,
            lax.dynamic_slice(w_key, start, (half, HEAD)),
            lax.dynamic_slice(w_value, start, (half, HEAD)),
        )
        weights = lax.all_gather(
            jnp.concatenate([wkv, wq[0], wq[1]], axis=1), ("zh", "zl"), axis=0, tiled=True
        )

    with jax.named_scope("norm"):
        states = tokens.astype(F32)
        own = jnp.sum(states * states, axis=1).reshape(2, rows // 2)
        mean_sq = jnp.sum(gather(own, COL, 16), axis=0).reshape(rows, 1) / (feats * 16)
        normed = (states * lax.rsqrt(mean_sq + EPS) * norm_gain.astype(F32)[None, :]).astype(BF16)

    with jax.named_scope("spread"):
        quarters = jnp.transpose(normed.reshape(rows, 4, feats // 4), (1, 0, 2))
        quarters = lax.all_to_all(quarters, ("xh", "core"), 0, 0)
        whole = gather(quarters, ("xl", "yh", "yl"), 8)
        whole = whole.reshape(8, 2, 2, rows, feats // 4)
        whole = jnp.transpose(whole, (1, 3, 0, 2, 4)).reshape(2 * rows, 4 * feats)

    with jax.named_scope("project_kv"):
        kv_sum = jnp.dot(whole, weights[:, :HEAD], preferred_element_type=F32)
        parts = lax.all_to_all(kv_sum.reshape(8, rows // 4, HEAD), ("xh", "yl", "core"), 0, 0)
        parts = jnp.sum(parts.reshape(2, 2, 2, rows // 4, HEAD), axis=(0, 2)).astype(BF16)
        kv = jnp.concatenate([parts[0], parts[1]], axis=1)

    with jax.named_scope("gather_kv"):
        kv = gather(gather(kv, "zh", 4), "zl", 4)
        mine = gather(kv, ("xh", "yl"), 4)
        other = swap(mine)

    with jax.named_scope("project_q"):
        q_sum = jnp.dot(whole, weights[:, HEAD:], preferred_element_type=F32)
        q_sum = q_sum.reshape(2 * rows, 2, q_cols)
        q_keep = lax.dynamic_index_in_dim(q_sum, core, 1, keepdims=False)
        q_send = lax.dynamic_index_in_dim(q_sum, 1 - core, 1, keepdims=False)
        q_sum = (q_keep + swap(q_send)).reshape(2, rows, q_cols)
        q_keep = lax.dynamic_index_in_dim(q_sum, xh, 0, keepdims=False)
        q_send = lax.dynamic_index_in_dim(q_sum, 1 - xh, 0, keepdims=False)
        q = (q_keep + lax.ppermute(q_send, "xh", [(0, 1), (1, 0)])).astype(BF16)

    with jax.named_scope("attend"):
        place = jnp.stack([z, xh, core]).astype(jnp.int32)
        return attend(place, q, mine, other)


def solution(mesh):
    fine = Mesh(mesh.devices.reshape(4, 4, 2, 2, 2, 2, 2), ("zh", "zl", "xh", "xl", "yh", "yl", "core"))
    return jax.shard_map(
        on_device,
        mesh=fine,
        in_specs=(P(ROW, COL), P(COL), P(ROW, COL), P(ROW, None), P(ROW, None)),
        out_specs=P(ROW, COL),
        check_vma=False,
    )
```

```python
import functools
import math

import jax
import jax.numpy as jnp
from jax import lax
from jax.experimental import pallas as pl
from jax.experimental.pallas import tpu as pltpu
from jax.sharding import Mesh
from jax.sharding import PartitionSpec as P

HEAD = 128
GROUP = 8
EPS = 1e-05
ROW = ("zh", "zl", "xh")
COL = ("xl", "yh", "yl", "core")
F32 = jnp.float32
BF16 = jnp.bfloat16


def gather(x, axes, n):
    return lax.all_to_all(jnp.broadcast_to(x[None], (n, *x.shape)), axes, 0, 0)


def swap(x):
    return lax.ppermute(x, "core", [(0, 1), (1, 0)])


def attend_kernel(place, q_ref, mine_ref, other_ref, out_ref, q_all, m_ref, l_ref, acc_ref):
    z, xh, core = place[0], place[1], place[2]
    rows = q_ref.shape[0]
    scale = HEAD**-0.5 * math.log2(math.e)
    q_all[:rows] = q_ref[:, :HEAD]
    q_all[rows:] = q_ref[:, HEAD:]
    m_ref[...] = jnp.full(m_ref.shape, -1e30, F32)
    l_ref[...] = jnp.zeros(l_ref.shape, F32)
    acc_ref[...] = jnp.zeros(acc_ref.shape, F32)
    chunk = mine_ref.shape[3]
    half = 4 * chunk

    def block(zi, masked):
        zl, zh = lax.rem(zi, 4), lax.div(zi, 4)
        kv = jnp.concatenate(
            [mine_ref[:, zl, zh].reshape(half, 2 * HEAD), other_ref[:, zl, zh].reshape(half, 2 * HEAD)], axis=0
        )
        s = lax.dot_general(q_all[...], kv[:, :HEAD], (((1,), (1,)), ((), ())), preferred_element_type=F32)
        if masked:
            slot = lax.broadcasted_iota(jnp.int32, s.shape, 1)
            within = lax.rem(slot, half)
            owner = jnp.where(slot < half, core, 1 - core)
            key_pos = (lax.div(within, chunk) * 2 + owner) * chunk + lax.rem(within, chunk)
            query_pos = xh * rows + lax.rem(lax.broadcasted_iota(jnp.int32, s.shape, 0), rows)
            s = jnp.where(key_pos <= query_pos, s, -1e30)
        m_old = m_ref[...]
        m_new = jnp.maximum(m_old, jnp.max(s, axis=1, keepdims=True))
        alpha = jnp.exp2((m_old - m_new) * scale)
        total = l_ref[...] * alpha
        weights = []
        for j in range(0, s.shape[1], HEAD):
            w = jnp.exp2((s[:, j : j + HEAD] - m_new) * scale)
            total = total + w
            weights.append(w.astype(BF16))
        p = jnp.concatenate(weights, axis=1)
        l_ref[...] = total
        m_ref[...] = m_new
        acc_ref[...] = acc_ref[...] * alpha + jnp.dot(p, kv[:, HEAD:], preferred_element_type=F32)

    @pl.loop(0, z)
    def _(zi):
        block(zi, False)

    block(z, True)
    total = jnp.sum(l_ref[...], axis=1, keepdims=True)
    result = (acc_ref[...] / total).astype(BF16)
    out_ref[:, :HEAD] = result[:rows]
    out_ref[:, HEAD:] = result[rows:]


def attend(place, q, mine, other):
    rows = q.shape[0]
    vmem = pl.BlockSpec(memory_space=pltpu.VMEM)
    return pl.pallas_call(
        attend_kernel,
        out_shape=jax.ShapeDtypeStruct(q.shape, BF16),
        in_specs=[pl.BlockSpec(memory_space=pltpu.SMEM), vmem, vmem, vmem],
        out_specs=vmem,
        scratch_shapes=[
            pltpu.VMEM((2 * rows, HEAD), BF16),
            pltpu.VMEM((2 * rows, HEAD), F32),
            pltpu.VMEM((2 * rows, HEAD), F32),
            pltpu.VMEM((2 * rows, HEAD), F32),
        ],
        compiler_params=pltpu.CompilerParams(vmem_limit_bytes=40 * 1024 * 1024),
        cost_estimate=pl.CostEstimate(flops=2**31, bytes_accessed=2**22, transcendentals=2**22),
    )(place, q, mine, other)


def kv_kernel(t_ref, w_ref, out_ref):
    for head in range(out_ref.shape[1]):
        w = jnp.concatenate([w_ref[:, at : at + HEAD] for at in (head * HEAD, head * HEAD + w_ref.shape[1] // 2)], axis=1)
        part = jnp.dot(t_ref[...], w, preferred_element_type=F32)
        out_ref[:, head] = part.reshape(out_ref.shape[0], *out_ref.shape[2:])


def kv_partial(t, w):
    vmem = pl.BlockSpec(memory_space=pltpu.VMEM)
    rows, depth = t.shape
    return pl.pallas_call(
        kv_kernel,
        out_shape=jax.ShapeDtypeStruct((2, 4, 4, rows // 8, 2 * HEAD), F32),
        in_specs=[vmem, vmem],
        out_specs=vmem,
        compiler_params=pltpu.CompilerParams(vmem_limit_bytes=40 * 1024 * 1024),
        cost_estimate=pl.CostEstimate(flops=2 * rows * depth * w.shape[1], bytes_accessed=3 * 2**20, transcendentals=0),
    )(t, w)


def on_device(tokens, norm_gain, w_query, w_key, w_value):
    at = lax.axis_index
    z, xh, core = at(("zh", "zl")), at("xh"), at("core")
    rows, feats = tokens.shape
    half = feats // 2

    with jax.named_scope("weights"):
        wkv = jnp.concatenate([w_key, w_value], axis=1)
        turn = [
            ((a * 2 + x) * 16 + b, (b * 2 + x) * 16 + a) for a in range(16) for x in range(2) for b in range(16)
        ]
        wkv = lax.ppermute(wkv, ROW + COL, turn)
        wq = lax.all_gather(w_query, ("zh", "zl"), axis=0, tiled=True)

    with jax.named_scope("norm"):
        states = tokens.astype(F32)
        own = jnp.sum(states * states, axis=1).reshape(2, rows // 2)
        mean_sq = jnp.sum(gather(own, COL, 16), axis=0).reshape(rows, 1) / (feats * 16)
        normed = (states * lax.rsqrt(mean_sq + EPS) * norm_gain.astype(F32)[None, :]).astype(BF16)

    with jax.named_scope("spread"):
        keep = lax.dynamic_slice_in_dim(normed, xh * half, half, 1)
        send = lax.dynamic_slice_in_dim(normed, (1 - xh) * half, half, 1)
        came = lax.ppermute(send, "xh", [(0, 1), (1, 0)])
        both = jnp.where(xh == 0, jnp.concatenate([keep, came]), jnp.concatenate([came, keep]))
        whole = lax.all_gather(both, COL, axis=1, tiled=True)

    with jax.named_scope("project_kv"):
        kv_sum = kv_partial(both, wkv).reshape(32, rows // 4, 2 * HEAD)
        parts = lax.all_to_all(kv_sum, ("xh",) + COL, 0, 0)
        kv = jnp.sum(parts, axis=0).astype(BF16)

    with jax.named_scope("gather_kv"):
        kv = gather(gather(kv, "zh", 4), "zl", 4)
        mine = gather(kv, ("xh", "yl"), 4)

    with jax.named_scope("project_q"):
        q_sum = jnp.dot(whole, wq, preferred_element_type=F32).reshape(2, rows, -1)
        q_keep = lax.dynamic_index_in_dim(q_sum, xh, 0, keepdims=False)
        q_send = lax.dynamic_index_in_dim(q_sum, 1 - xh, 0, keepdims=False)
        q = (q_keep + lax.ppermute(q_send, "xh", [(0, 1), (1, 0)])).astype(BF16)

    with jax.named_scope("attend"):
        mine, q = lax.optimization_barrier((mine, q))
        place = jnp.stack([z, xh, core]).astype(jnp.int32)
        return attend(place, q, mine, swap(mine))


def solution(mesh):
    fine = Mesh(mesh.devices.reshape(4, 4, 2, 2, 2, 2, 2), ("zh", "zl", "xh", "xl", "yh", "yl", "core"))
    return jax.shard_map(
        on_device,
        mesh=fine,
        in_specs=(P(ROW, COL), P(COL), P(ROW, COL), P(ROW, None), P(ROW, None)),
        out_specs=P(ROW, COL),
        check_vma=False,
    )
```

```python
import functools
import math

import jax
import jax.numpy as jnp
from jax import lax
from jax.experimental import pallas as pl
from jax.experimental.pallas import tpu as pltpu
from jax.sharding import Mesh
from jax.sharding import PartitionSpec as P

HEAD = 128
GROUP = 8
EPS = 1e-05
ROW = ("zh", "zl", "xh")
COL = ("xl", "yh", "yl", "core")
F32 = jnp.float32
BF16 = jnp.bfloat16


def gather(x, axes, n):
    return lax.all_to_all(jnp.broadcast_to(x[None], (n, *x.shape)), axes, 0, 0)


def swap(x):
    return lax.ppermute(x, "core", [(0, 1), (1, 0)])


def attend_kernel(place, q_ref, mine_ref, other_ref, out_ref, q_all, m_ref, l_ref, acc_ref):
    z, xh, core = place[0], place[1], place[2]
    rows = q_ref.shape[0]
    scale = HEAD**-0.5 * math.log2(math.e)
    q_all[:rows] = q_ref[:, :HEAD]
    q_all[rows:] = q_ref[:, HEAD:]
    m_ref[...] = jnp.full(m_ref.shape, -1e30, F32)
    l_ref[...] = jnp.zeros(l_ref.shape, F32)
    acc_ref[...] = jnp.zeros(acc_ref.shape, F32)
    chunk = mine_ref.shape[3]
    half = 4 * chunk

    def block(zi, masked):
        zl, zh = lax.rem(zi, 4), lax.div(zi, 4)
        kv = jnp.concatenate(
            [mine_ref[:, zl, zh].reshape(half, 2 * HEAD), other_ref[:, zl, zh].reshape(half, 2 * HEAD)], axis=0
        )
        s = lax.dot_general(q_all[...], kv[:, :HEAD], (((1,), (1,)), ((), ())), preferred_element_type=F32)
        if masked:
            slot = lax.broadcasted_iota(jnp.int32, s.shape, 1)
            within = lax.rem(slot, half)
            owner = jnp.where(slot < half, core, 1 - core)
            key_pos = (lax.div(within, chunk) * 2 + owner) * chunk + lax.rem(within, chunk)
            query_pos = xh * rows + lax.rem(lax.broadcasted_iota(jnp.int32, s.shape, 0), rows)
            s = jnp.where(key_pos <= query_pos, s, -1e30)
        m_old = m_ref[...]
        m_new = jnp.maximum(m_old, jnp.max(s, axis=1, keepdims=True))
        alpha = jnp.exp2((m_old - m_new) * scale)
        total = l_ref[...] * alpha
        weights = []
        for j in range(0, s.shape[1], HEAD):
            w = jnp.exp2((s[:, j : j + HEAD] - m_new) * scale)
            total = total + w
            weights.append(w.astype(BF16))
        p = jnp.concatenate(weights, axis=1)
        l_ref[...] = total
        m_ref[...] = m_new
        acc_ref[...] = acc_ref[...] * alpha + jnp.dot(p, kv[:, HEAD:], preferred_element_type=F32)

    @pl.loop(0, z)
    def _(zi):
        block(zi, False)

    block(z, True)
    total = jnp.sum(l_ref[...], axis=1, keepdims=True)
    result = (acc_ref[...] / total).astype(BF16)
    out_ref[:, :HEAD] = result[:rows]
    out_ref[:, HEAD:] = result[rows:]


def attend(place, q, mine, other):
    rows = q.shape[0]
    vmem = pl.BlockSpec(memory_space=pltpu.VMEM)
    return pl.pallas_call(
        attend_kernel,
        out_shape=jax.ShapeDtypeStruct(q.shape, BF16),
        in_specs=[pl.BlockSpec(memory_space=pltpu.SMEM), vmem, vmem, vmem],
        out_specs=vmem,
        scratch_shapes=[
            pltpu.VMEM((2 * rows, HEAD), BF16),
            pltpu.VMEM((2 * rows, HEAD), F32),
            pltpu.VMEM((2 * rows, HEAD), F32),
            pltpu.VMEM((2 * rows, HEAD), F32),
        ],
        compiler_params=pltpu.CompilerParams(vmem_limit_bytes=40 * 1024 * 1024),
        cost_estimate=pl.CostEstimate(flops=2**31, bytes_accessed=2**22, transcendentals=2**22),
    )(place, q, mine, other)


def kv_kernel(parts_ref, w_ref, t_ref, kv_ref):
    rows = t_ref.shape[1]
    blocks = parts_ref.shape[1]
    for xh in range(2):
        squares = jnp.zeros((6, HEAD), F32)
        for c in range(blocks):
            squares += parts_ref[xh, c, rows : rows + 6].astype(F32)
        mean_sq = (squares[4:6] + squares[2:4] + squares[0:2]) / (blocks * 4 * HEAD)
        inverse = lax.rsqrt(mean_sq + EPS)
        inverse = jnp.concatenate(
            [jnp.transpose(jnp.broadcast_to(inverse[i : i + 1], (HEAD, HEAD))) for i in range(2)], axis=0
        )
        total = jnp.zeros((rows, HEAD), F32)
        for c in range(0, blocks, 2):
            for d in (c, c + 1):
                gain = parts_ref[xh, d, rows + 6 : rows + 7].astype(F32)
                t = parts_ref[xh, d, :rows].astype(F32) * inverse * gain
                t_ref[xh, :, d * HEAD : (d + 1) * HEAD] = t.astype(BF16)
            w = jnp.concatenate([w_ref[d % 4, d // 4] for d in (c, c + 1)], axis=0)
            total += jnp.dot(t_ref[xh, :, c * HEAD : (c + 2) * HEAD], w, preferred_element_type=F32)
        kv_ref[xh] = total


def project_kv(parts, w, rows):
    vmem = pl.BlockSpec(memory_space=pltpu.VMEM)
    blocks = parts.shape[1]
    return pl.pallas_call(
        kv_kernel,
        out_shape=(
            jax.ShapeDtypeStruct((2, rows, blocks * HEAD), BF16),
            jax.ShapeDtypeStruct((2, rows, HEAD), F32),
        ),
        in_specs=[vmem, vmem],
        out_specs=(vmem, vmem),
        compiler_params=pltpu.CompilerParams(vmem_limit_bytes=40 * 1024 * 1024),
        cost_estimate=pl.CostEstimate(flops=2**28, bytes_accessed=5 * 2**20, transcendentals=0),
    )(parts, w)


def q_kernel(place, mine_ref, other_ref, w_ref, out_ref):
    core = place[2]
    rows = mine_ref.shape[1]
    half = w_ref.shape[1] // 2
    for xh in range(2):
        total = jnp.zeros((rows, w_ref.shape[2]), F32)
        for c in range(w_ref.shape[0]):
            t = jnp.concatenate([ref[xh, :, c * half : (c + 1) * half] for ref in (mine_ref, other_ref)], axis=1)
            w = jnp.concatenate(
                [w_ref[c, pl.ds(pl.multiple_of(at * half, half), half)] for at in (core, 1 - core)], axis=0
            )
            total += jnp.dot(t, w, preferred_element_type=F32)
        out_ref[xh] = total


def project_q(place, mine, other, w):
    vmem = pl.BlockSpec(memory_space=pltpu.VMEM)
    return pl.pallas_call(
        q_kernel,
        out_shape=jax.ShapeDtypeStruct((*mine.shape[:2], w.shape[2]), F32),
        in_specs=[pl.BlockSpec(memory_space=pltpu.SMEM), vmem, vmem, vmem],
        out_specs=vmem,
        compiler_params=pltpu.CompilerParams(vmem_limit_bytes=40 * 1024 * 1024),
        cost_estimate=pl.CostEstimate(flops=2**30, bytes_accessed=6 * 2**20, transcendentals=0),
    )(place, mine, other, w)


def three(x):
    out = []
    for _ in range(3):
        piece = lax.reduce_precision(x, 8, 7)
        out.append(piece.astype(BF16))
        x = x - piece
    return out


def on_device(tokens, norm_gain, w_query, w_key, w_value):
    at = lax.axis_index
    z, xh, core = at(("zh", "zl")), at("xh"), at("core")
    place = jnp.stack([z, xh, core]).astype(jnp.int32)
    rows, feats = tokens.shape
    half = w_key.shape[0] // 2

    with jax.named_scope("weights"):
        wq = lax.all_gather(w_query, ("zh", "zl"), axis=0)
        head = at(("xl", "yh"))
        start = (core * half, head * HEAD)
        wkv = jnp.where(
            at("yl") == 0,
            lax.dynamic_slice(w_key, start, (half, HEAD)),
            lax.dynamic_slice(w_value, start, (half, HEAD)),
        )
        wkv = lax.all_gather(lax.all_gather(wkv, "zh"), "zl")

    with jax.named_scope("spread"):
        states = tokens.astype(F32)
        squares = jnp.concatenate([p.reshape(2, HEAD) for p in three(jnp.sum(states * states, axis=1))])
        quarters = jnp.transpose(tokens.reshape(rows, 4, HEAD), (1, 0, 2))
        extra = jnp.concatenate(
            [
                jnp.broadcast_to(squares[None], (4, 6, HEAD)),
                norm_gain.reshape(4, 1, HEAD),
                jnp.zeros((4, 9, HEAD), BF16),
            ],
            axis=1,
        )
        quarters = jnp.concatenate([quarters, extra], axis=1).reshape(2, 1, 2, rows + 16, HEAD)
        parts = jnp.broadcast_to(quarters, (2, 8, 2, rows + 16, HEAD)).reshape(32, rows + 16, HEAD)
        parts = lax.all_to_all(parts, ("xh",) + COL, 0, 0).reshape(2, 16, rows + 16, HEAD)

    with jax.named_scope("project_kv"):
        whole, kv_sum = project_kv(parts, wkv, rows)
        chunks = lax.all_to_all(kv_sum.reshape(8, rows // 4, HEAD), ("xh", "yl", "core"), 0, 0)
        chunks = jnp.sum(chunks.reshape(2, 2, 2, rows // 4, HEAD), axis=(0, 2)).astype(BF16)
        kv = jnp.concatenate([chunks[0], chunks[1]], axis=1)

    with jax.named_scope("gather_kv"):
        kv = lax.all_gather(lax.all_gather(kv, "zh"), "zl")
        mine = gather(kv, ("xh", "yl"), 4)

    with jax.named_scope("project_q"):
        q_sum = project_q(place, whole, swap(whole), wq)
        q_keep = lax.dynamic_index_in_dim(q_sum, xh, 0, keepdims=False)
        q_send = lax.dynamic_index_in_dim(q_sum, 1 - xh, 0, keepdims=False)
        q = (q_keep + lax.ppermute(q_send, "xh", [(0, 1), (1, 0)])).astype(BF16)

    with jax.named_scope("attend"):
        mine, q = lax.optimization_barrier((mine, q))
        return attend(place, q, mine, swap(mine))


def solution(mesh):
    fine = Mesh(mesh.devices.reshape(4, 4, 2, 2, 2, 2, 2), ("zh", "zl", "xh", "xl", "yh", "yl", "core"))
    return jax.shard_map(
        on_device,
        mesh=fine,
        in_specs=(P(ROW, COL), P(COL), P(ROW, COL), P(ROW, None), P(ROW, None)),
        out_specs=P(ROW, COL),
        check_vma=False,
    )
```

```python
import functools
import math

import jax
import jax.numpy as jnp
from jax import lax
from jax.experimental import pallas as pl
from jax.experimental.pallas import tpu as pltpu
from jax.sharding import Mesh
from jax.sharding import PartitionSpec as P

HEAD = 128
GROUP = 8
EPS = 1e-05
ROW = ("zh", "zl", "xh")
COL = ("xl", "yh", "yl", "core")
F32 = jnp.float32
BF16 = jnp.bfloat16


def gather(x, axes, n):
    return lax.all_to_all(jnp.broadcast_to(x[None], (n, *x.shape)), axes, 0, 0)


def swap(x):
    return lax.ppermute(x, "core", [(0, 1), (1, 0)])


def attend_kernel(place, own_ref, pair_ref, mine_ref, other_ref, out_ref, m_ref, l_ref, acc_ref):
    z, xh, yl, core = place[0], place[1], place[2], place[3]
    rows = own_ref.shape[1]
    scale = HEAD**-0.5 * math.log2(math.e)
    m_ref[...] = jnp.full(m_ref.shape, -1e30, F32)
    l_ref[...] = jnp.zeros(l_ref.shape, F32)
    acc_ref[...] = jnp.zeros(acc_ref.shape, F32)
    chunk = mine_ref.shape[2]
    half = 4 * chunk

    def block(group, masked):
        kv = jnp.concatenate(
            [mine_ref[:, group].reshape(half, 2 * HEAD), other_ref[:, group].reshape(half, 2 * HEAD)], axis=0
        )
        if masked:
            shape = (2 * rows, 2 * half)
            slot = lax.broadcasted_iota(jnp.int32, shape, 1)
            within = lax.rem(slot, half)
            owner = jnp.where(slot < half, core, 1 - core) + 4 * xh + 2 * yl
            key_pos = lax.div(within, chunk) * (2 * rows) + owner * chunk + lax.rem(within, chunk)
            query_pos = lax.rem(z, 4) * (2 * rows) + lax.broadcasted_iota(jnp.int32, shape, 0)
            seen = key_pos <= query_pos
        for head in range(4):
            q_ref = (own_ref, pair_ref)[head // 2]
            at = head % 2 * HEAD
            q = q_ref[:, :, at : at + HEAD].reshape(2 * rows, HEAD)
            s = lax.dot_general(q, kv[:, :HEAD], (((1,), (1,)), ((), ())), preferred_element_type=F32)
            if masked:
                s = jnp.where(seen, s, -1e30)
            m_old = m_ref[head]
            m_new = jnp.maximum(m_old, jnp.max(s, axis=1, keepdims=True))
            alpha = jnp.exp2((m_old - m_new) * scale)
            total = l_ref[head] * alpha
            weights = []
            for j in range(0, s.shape[1], HEAD):
                w = jnp.exp2((s[:, j : j + HEAD] - m_new) * scale)
                total = total + w
                weights.append(w.astype(BF16))
            p = jnp.concatenate(weights, axis=1)
            l_ref[head] = total
            m_ref[head] = m_new
            acc_ref[head] = acc_ref[head] * alpha + jnp.dot(p, kv[:, HEAD:], preferred_element_type=F32)

    mine_group = lax.div(z, 4)

    @pl.loop(0, mine_group)
    def _(group):
        block(group, False)

    block(mine_group, True)
    lane = lax.broadcasted_iota(jnp.int32, (2 * rows, HEAD), 1)
    for side in range(2):
        to = yl if side == 0 else 1 - yl
        stats = jnp.zeros((2 * rows, HEAD), F32)
        for i in range(2):
            head = side * 2 + i
            total = jnp.sum(l_ref[head], axis=1, keepdims=True)
            stats = jnp.where(lane == i, m_ref[head] * scale + jnp.log2(total), stats)
            part = acc_ref[head] / total
            for x in range(2):
                out_ref[2 * x + to, :rows, i * HEAD : (i + 1) * HEAD] = part[x * rows : (x + 1) * rows]
        for x in range(2):
            out_ref[2 * x + to, rows:, :] = jnp.transpose(stats[x * rows : (x + 1) * rows])[:8]


def attend(place, own, pair, mine, other):
    rows, cols = own.shape[1:]
    vmem = pl.BlockSpec(memory_space=pltpu.VMEM)
    return pl.pallas_call(
        attend_kernel,
        out_shape=jax.ShapeDtypeStruct((4, rows + 8, cols), F32),
        in_specs=[pl.BlockSpec(memory_space=pltpu.SMEM), vmem, vmem, vmem, vmem],
        out_specs=vmem,
        scratch_shapes=[pltpu.VMEM((4, 2 * rows, HEAD), F32)] * 3,
        compiler_params=pltpu.CompilerParams(vmem_limit_bytes=40 * 1024 * 1024),
        cost_estimate=pl.CostEstimate(flops=2**31, bytes_accessed=2**22, transcendentals=2**22),
    )(place, own, pair, mine, other)


def merge_kernel(parts_ref, out_ref):
    rows = out_ref.shape[0]
    n = parts_ref.shape[0]
    sums = [parts_ref[i, rows:, :] for i in range(n)]
    most = functools.reduce(jnp.maximum, sums)
    shares = [jnp.exp2(s - most) for s in sums]
    total = functools.reduce(jnp.add, shares)
    columns = [jnp.transpose(jnp.concatenate([s / total] * (HEAD // 8), axis=0)) for s in shares]
    for i in range(2):
        at = slice(i * HEAD, (i + 1) * HEAD)
        out_ref[:, at] = sum(columns[k][:, i : i + 1] * parts_ref[k, :rows, at] for k in range(n)).astype(BF16)


def merge(parts):
    vmem = pl.BlockSpec(memory_space=pltpu.VMEM)
    return pl.pallas_call(
        merge_kernel,
        out_shape=jax.ShapeDtypeStruct((parts.shape[1] - 8, parts.shape[2]), BF16),
        in_specs=[vmem],
        out_specs=vmem,
        compiler_params=pltpu.CompilerParams(vmem_limit_bytes=40 * 1024 * 1024),
    )(parts)


def prep_kernel(tokens_ref, gain_ref, out_ref):
    rows = tokens_ref.shape[0]
    states = tokens_ref[...].astype(F32)
    sums = jnp.sum(states * states, axis=1, keepdims=True)
    left = jnp.transpose(jnp.broadcast_to(sums, (rows, HEAD)))[:1]
    left = jnp.concatenate([left[:, :HEAD], left[:, HEAD:]], axis=0)
    pieces = []
    for _ in range(3):
        piece = left.astype(BF16).astype(F32)
        pieces.append(piece)
        left = left - piece
    for q in range(4):
        at = slice(q * HEAD, (q + 1) * HEAD)
        gain = gain_ref[:, at].astype(F32)
        extra = jnp.concatenate([*pieces, gain, jnp.zeros((9, HEAD), F32)], axis=0).astype(BF16)
        for to in range(out_ref.shape[1]):
            out_ref[q // 2, to, q % 2, :rows] = tokens_ref[:, at]
            out_ref[q // 2, to, q % 2, rows:] = extra


def prep(tokens, gain):
    vmem = pl.BlockSpec(memory_space=pltpu.VMEM)
    return pl.pallas_call(
        prep_kernel,
        out_shape=jax.ShapeDtypeStruct((2, 8, 2, tokens.shape[0] + 16, HEAD), BF16),
        in_specs=[vmem, vmem],
        out_specs=vmem,
        compiler_params=pltpu.CompilerParams(vmem_limit_bytes=40 * 1024 * 1024),
    )(tokens, gain)


def kv_kernel(parts_ref, w_ref, t_ref, kv_ref):
    rows = t_ref.shape[1]
    blocks = parts_ref.shape[1]
    for xh in range(2):
        extra = [parts_ref[xh, c, rows:].astype(F32) for c in range(blocks)]
        squares = functools.reduce(jnp.add, extra)
        mean_sq = (squares[4:6] + squares[2:4] + squares[0:2]) / (blocks * 4 * HEAD)
        inverse = lax.rsqrt(mean_sq + EPS)
        inverse = jnp.concatenate(
            [jnp.transpose(jnp.broadcast_to(inverse[i : i + 1], (HEAD, HEAD))) for i in range(2)], axis=0
        )
        total = jnp.zeros((rows, HEAD), F32)
        for c in range(0, blocks, 2):
            for d in (c, c + 1):
                t = parts_ref[xh, d, :rows].astype(F32) * inverse * extra[d][6:7]
                t_ref[xh, :, d * HEAD : (d + 1) * HEAD] = t.astype(BF16)
            w = jnp.concatenate([w_ref[d % 4, d // 4] for d in (c, c + 1)], axis=0)
            total += jnp.dot(t_ref[xh, :, c * HEAD : (c + 2) * HEAD], w, preferred_element_type=F32)
        kv_ref[xh] = total


def project_kv(parts, w, rows):
    vmem = pl.BlockSpec(memory_space=pltpu.VMEM)
    blocks = parts.shape[1]
    return pl.pallas_call(
        kv_kernel,
        out_shape=(
            jax.ShapeDtypeStruct((2, rows, blocks * HEAD), BF16),
            jax.ShapeDtypeStruct((2, rows, HEAD), F32),
        ),
        in_specs=[vmem, vmem],
        out_specs=(vmem, vmem),
        compiler_params=pltpu.CompilerParams(vmem_limit_bytes=40 * 1024 * 1024),
        cost_estimate=pl.CostEstimate(flops=2**28, bytes_accessed=5 * 2**20, transcendentals=0),
    )(parts, w)


def q_kernel(place, mine_ref, other_ref, w_ref, out_ref):
    core = place[3]
    rows = mine_ref.shape[1]
    half = w_ref.shape[1] // 2
    for xh in range(2):
        total = jnp.zeros((rows, w_ref.shape[2]), F32)
        for c in range(w_ref.shape[0]):
            t = jnp.concatenate([ref[xh, :, c * half : (c + 1) * half] for ref in (mine_ref, other_ref)], axis=1)
            w = jnp.concatenate(
                [w_ref[c, pl.ds(pl.multiple_of(at * half, half), half)] for at in (core, 1 - core)], axis=0
            )
            total += jnp.dot(t, w, preferred_element_type=F32)
        out_ref[xh] = total


def project_q(place, mine, other, w):
    vmem = pl.BlockSpec(memory_space=pltpu.VMEM)
    return pl.pallas_call(
        q_kernel,
        out_shape=jax.ShapeDtypeStruct((*mine.shape[:2], w.shape[2]), F32),
        in_specs=[pl.BlockSpec(memory_space=pltpu.SMEM), vmem, vmem, vmem],
        out_specs=vmem,
        compiler_params=pltpu.CompilerParams(vmem_limit_bytes=40 * 1024 * 1024),
        cost_estimate=pl.CostEstimate(flops=2**30, bytes_accessed=6 * 2**20, transcendentals=0),
    )(place, mine, other, w)


def on_device(tokens, norm_gain, w_query, w_key, w_value):
    at = lax.axis_index
    core = at("core")
    place = jnp.stack([at(("zh", "zl")), at("xh"), at("yl"), core]).astype(jnp.int32)
    rows, feats = tokens.shape
    half = w_key.shape[0] // 2

    with jax.named_scope("weights"):
        wq = lax.all_gather(w_query, ("zh", "zl"), axis=0)
        head = at(("xl", "yh"))
        start = (core * half, head * HEAD)
        wkv = jnp.where(
            at("yl") == 0,
            lax.dynamic_slice(w_key, start, (half, HEAD)),
            lax.dynamic_slice(w_value, start, (half, HEAD)),
        )
        wkv = lax.all_gather(lax.all_gather(wkv, "zh"), "zl")

    with jax.named_scope("spread"):
        parts = prep(tokens, norm_gain.reshape(1, feats))
        parts = lax.all_to_all(parts.reshape(32, rows + 16, HEAD), ("xh",) + COL, 0, 0)
        parts = parts.reshape(2, 16, rows + 16, HEAD)

    with jax.named_scope("project_kv"):
        whole, kv_sum = project_kv(parts, wkv, rows)
        chunks = lax.all_to_all(kv_sum.reshape(8, rows // 4, HEAD), ("xh", "yl", "core"), 0, 0)
        chunks = jnp.sum(chunks.reshape(2, 2, 2, rows // 4, HEAD), axis=(0, 2)).astype(BF16)
        kv = jnp.concatenate([chunks[0], chunks[1]], axis=1)

    with jax.named_scope("gather_kv"):
        kv = gather(gather(kv, "zh", 4), "zl", 4)

    with jax.named_scope("project_q"):
        q = project_q(place, whole, swap(whole), wq)
        q = (q + lax.ppermute(q, "xh", [(0, 1), (1, 0)])).astype(BF16)
        pair = lax.ppermute(q, "yl", [(0, 1), (1, 0)])

    with jax.named_scope("attend"):
        out = attend(place, q, pair, kv, swap(kv))
        return merge(lax.all_to_all(out, ("xh", "yl"), 0, 0))


def solution(mesh):
    fine = Mesh(mesh.devices.reshape(4, 4, 2, 2, 2, 2, 2), ("zh", "zl", "xh", "xl", "yh", "yl", "core"))
    return jax.shard_map(
        on_device,
        mesh=fine,
        in_specs=(P(ROW, COL), P(COL), P(ROW, COL), P(ROW, None), P(ROW, None)),
        out_specs=P(ROW, COL),
        check_vma=False,
    )
```

```python
import functools
import math

import jax
import jax.numpy as jnp
from jax import lax
from jax.experimental import pallas as pl
from jax.experimental.pallas import tpu as pltpu
from jax.sharding import Mesh
from jax.sharding import PartitionSpec as P

HEAD = 128
GROUP = 8
EPS = 1e-05
ROW = ("zh", "zl", "xh")
COL = ("xl", "yh", "yl", "core")
F32 = jnp.float32
BF16 = jnp.bfloat16


def gather(x, axes, n):
    return lax.all_to_all(jnp.broadcast_to(x[None], (n, *x.shape)), axes, 0, 0)


def swap(x):
    return lax.ppermute(x, "core", [(0, 1), (1, 0)])


def attend_kernel(place, own_ref, pair_ref, mine_ref, other_ref, out_ref, m_ref, l_ref, acc_ref):
    z, xh, yl, core = place[0], place[1], place[2], place[3]
    rows = own_ref.shape[1]
    scale = HEAD**-0.5 * math.log2(math.e)
    m_ref[...] = jnp.full(m_ref.shape, -1e30, F32)
    l_ref[...] = jnp.zeros(l_ref.shape, F32)
    acc_ref[...] = jnp.zeros(acc_ref.shape, F32)
    chunk = mine_ref.shape[2]
    half = 4 * chunk

    def block(group, masked):
        kv = jnp.concatenate(
            [mine_ref[:, group].reshape(half, 2 * HEAD), other_ref[:, group].reshape(half, 2 * HEAD)], axis=0
        )
        if masked:
            shape = (2 * rows, 2 * half)
            slot = lax.broadcasted_iota(jnp.int32, shape, 1)
            within = lax.rem(slot, half)
            owner = jnp.where(slot < half, core, 1 - core) + 4 * xh + 2 * yl
            key_pos = lax.div(within, chunk) * (2 * rows) + owner * chunk + lax.rem(within, chunk)
            query_pos = lax.rem(z, 4) * (2 * rows) + lax.broadcasted_iota(jnp.int32, shape, 0)
            seen = key_pos <= query_pos
        for head in range(4):
            q_ref = (own_ref, pair_ref)[head // 2]
            at = head % 2 * HEAD
            q = q_ref[:, :, at : at + HEAD].reshape(2 * rows, HEAD)
            s = lax.dot_general(q, kv[:, :HEAD], (((1,), (1,)), ((), ())), preferred_element_type=F32)
            if masked:
                s = jnp.where(seen, s, -1e30)
            m_old = m_ref[head]
            m_new = jnp.maximum(m_old, jnp.max(s, axis=1, keepdims=True))
            alpha = jnp.exp2((m_old - m_new) * scale)
            total = l_ref[head] * alpha
            weights = []
            for j in range(0, s.shape[1], HEAD):
                w = jnp.exp2((s[:, j : j + HEAD] - m_new) * scale)
                total = total + w
                weights.append(w.astype(BF16))
            p = jnp.concatenate(weights, axis=1)
            l_ref[head] = total
            m_ref[head] = m_new
            acc_ref[head] = acc_ref[head] * alpha + jnp.dot(p, kv[:, HEAD:], preferred_element_type=F32)

    mine_group = lax.div(z, 4)

    @pl.loop(0, mine_group)
    def _(group):
        block(group, False)

    block(mine_group, True)
    lane = lax.broadcasted_iota(jnp.int32, (2 * rows, HEAD), 1)
    for side in range(2):
        to = yl if side == 0 else 1 - yl
        stats = jnp.zeros((2 * rows, HEAD), F32)
        for i in range(2):
            head = side * 2 + i
            total = jnp.sum(l_ref[head], axis=1, keepdims=True)
            stats = jnp.where(lane == i, m_ref[head] * scale + jnp.log2(total), stats)
            part = acc_ref[head] / total
            for x in range(2):
                out_ref[2 * x + to, :rows, i * HEAD : (i + 1) * HEAD] = part[x * rows : (x + 1) * rows]
        for x in range(2):
            out_ref[2 * x + to, rows:, :] = jnp.transpose(stats[x * rows : (x + 1) * rows])[:8]


def attend(place, own, pair, mine, other):
    rows, cols = own.shape[1:]
    vmem = pl.BlockSpec(memory_space=pltpu.VMEM)
    return pl.pallas_call(
        attend_kernel,
        out_shape=jax.ShapeDtypeStruct((4, rows + 8, cols), F32),
        in_specs=[pl.BlockSpec(memory_space=pltpu.SMEM), vmem, vmem, vmem, vmem],
        out_specs=vmem,
        scratch_shapes=[pltpu.VMEM((4, 2 * rows, HEAD), F32)] * 3,
        compiler_params=pltpu.CompilerParams(vmem_limit_bytes=40 * 1024 * 1024),
        cost_estimate=pl.CostEstimate(flops=2**31, bytes_accessed=2**22, transcendentals=2**22),
    )(place, own, pair, mine, other)


def merge_kernel(parts_ref, out_ref):
    rows = out_ref.shape[0]
    n = parts_ref.shape[0]
    sums = [parts_ref[i, rows:, :] for i in range(n)]
    most = functools.reduce(jnp.maximum, sums)
    shares = [jnp.exp2(s - most) for s in sums]
    total = functools.reduce(jnp.add, shares)
    columns = [jnp.transpose(jnp.concatenate([s / total] * (HEAD // 8), axis=0)) for s in shares]
    for i in range(2):
        at = slice(i * HEAD, (i + 1) * HEAD)
        out_ref[:, at] = sum(columns[k][:, i : i + 1] * parts_ref[k, :rows, at] for k in range(n)).astype(BF16)


def merge(parts):
    vmem = pl.BlockSpec(memory_space=pltpu.VMEM)
    return pl.pallas_call(
        merge_kernel,
        out_shape=jax.ShapeDtypeStruct((parts.shape[1] - 8, parts.shape[2]), BF16),
        in_specs=[vmem],
        out_specs=vmem,
        compiler_params=pltpu.CompilerParams(vmem_limit_bytes=40 * 1024 * 1024),
    )(parts)


def prep_kernel(tokens_ref, gain_ref, out_ref):
    rows = tokens_ref.shape[0]
    states = tokens_ref[...].astype(F32)
    sums = jnp.sum(states * states, axis=1, keepdims=True)
    left = jnp.transpose(jnp.broadcast_to(sums, (rows, HEAD)))[:1]
    left = jnp.concatenate([left[:, :HEAD], left[:, HEAD:]], axis=0)
    pieces = []
    for _ in range(3):
        piece = left.astype(BF16).astype(F32)
        pieces.append(piece)
        left = left - piece
    for q in range(4):
        at = slice(q * HEAD, (q + 1) * HEAD)
        gain = gain_ref[:, at].astype(F32)
        extra = jnp.concatenate([*pieces, gain, jnp.zeros((9, HEAD), F32)], axis=0).astype(BF16)
        for to in range(out_ref.shape[1]):
            out_ref[q // 2, to, q % 2, :rows] = tokens_ref[:, at]
            out_ref[q // 2, to, q % 2, rows:] = extra


def prep(tokens, gain):
    vmem = pl.BlockSpec(memory_space=pltpu.VMEM)
    return pl.pallas_call(
        prep_kernel,
        out_shape=jax.ShapeDtypeStruct((2, 8, 2, tokens.shape[0] + 16, HEAD), BF16),
        in_specs=[vmem, vmem],
        out_specs=vmem,
        compiler_params=pltpu.CompilerParams(vmem_limit_bytes=40 * 1024 * 1024),
    )(tokens, gain)


def kv_kernel(parts_ref, w_ref, t_ref, kv_ref):
    rows = t_ref.shape[1]
    blocks = parts_ref.shape[1]
    for xh in range(2):
        extra = [parts_ref[xh, c, rows:].astype(F32) for c in range(blocks)]
        squares = functools.reduce(jnp.add, extra)
        mean_sq = (squares[4:6] + squares[2:4] + squares[0:2]) / (blocks * 4 * HEAD)
        inverse = lax.rsqrt(mean_sq + EPS)
        inverse = jnp.concatenate(
            [jnp.transpose(jnp.broadcast_to(inverse[i : i + 1], (HEAD, HEAD))) for i in range(2)], axis=0
        )
        total = jnp.zeros((rows, HEAD), F32)
        for c in range(0, blocks, 2):
            for d in (c, c + 1):
                t = parts_ref[xh, d, :rows].astype(F32) * inverse * extra[d][6:7]
                t_ref[xh, :, d * HEAD : (d + 1) * HEAD] = t.astype(BF16)
            w = jnp.concatenate([w_ref[d % 4, d // 4] for d in (c, c + 1)], axis=0)
            total += jnp.dot(t_ref[xh, :, c * HEAD : (c + 2) * HEAD], w, preferred_element_type=F32)
        kv_ref[xh] = total


def project_kv(parts, w, rows):
    vmem = pl.BlockSpec(memory_space=pltpu.VMEM)
    blocks = parts.shape[1]
    return pl.pallas_call(
        kv_kernel,
        out_shape=(
            jax.ShapeDtypeStruct((2, rows, blocks * HEAD), BF16),
            jax.ShapeDtypeStruct((2, rows, HEAD), F32),
        ),
        in_specs=[vmem, vmem],
        out_specs=(vmem, vmem),
        compiler_params=pltpu.CompilerParams(vmem_limit_bytes=40 * 1024 * 1024),
        cost_estimate=pl.CostEstimate(flops=2**28, bytes_accessed=5 * 2**20, transcendentals=0),
    )(parts, w)


def q_kernel(place, mine_ref, other_ref, w_ref, out_ref):
    core = place[3]
    rows = mine_ref.shape[1]
    half = w_ref.shape[1] // 2
    for xh in range(2):
        total = jnp.zeros((rows, w_ref.shape[2]), F32)
        for c in range(w_ref.shape[0]):
            t = jnp.concatenate([ref[xh, :, c * half : (c + 1) * half] for ref in (mine_ref, other_ref)], axis=1)
            w = jnp.concatenate(
                [w_ref[c, pl.ds(pl.multiple_of(at * half, half), half)] for at in (core, 1 - core)], axis=0
            )
            total += jnp.dot(t, w, preferred_element_type=F32)
        out_ref[xh] = total


def project_q(place, mine, other, w):
    vmem = pl.BlockSpec(memory_space=pltpu.VMEM)
    return pl.pallas_call(
        q_kernel,
        out_shape=jax.ShapeDtypeStruct((*mine.shape[:2], w.shape[2]), F32),
        in_specs=[pl.BlockSpec(memory_space=pltpu.SMEM), vmem, vmem, vmem],
        out_specs=vmem,
        compiler_params=pltpu.CompilerParams(vmem_limit_bytes=40 * 1024 * 1024),
        cost_estimate=pl.CostEstimate(flops=2**30, bytes_accessed=6 * 2**20, transcendentals=0),
    )(place, mine, other, w)


def on_device(tokens, norm_gain, w_query, w_key, w_value):
    at = lax.axis_index
    core = at("core")
    place = jnp.stack([at(("zh", "zl")), at("xh"), at("yl"), core]).astype(jnp.int32)
    rows, feats = tokens.shape
    half = w_key.shape[0] // 2

    with jax.named_scope("weights"):
        wq = lax.all_gather(w_query, ("zh", "zl"), axis=0)
        head = at(("xl", "yh"))
        start = (core * half, head * HEAD)
        wkv = jnp.where(
            at("yl") == 0,
            lax.dynamic_slice(w_key, start, (half, HEAD)),
            lax.dynamic_slice(w_value, start, (half, HEAD)),
        )
        wkv = lax.all_gather(lax.all_gather(wkv, "zh"), "zl")

    with jax.named_scope("spread"):
        parts = prep(tokens, norm_gain.reshape(1, feats))
        parts = lax.all_to_all(parts.reshape(32, rows + 16, HEAD), ("xh",) + COL, 0, 0)
        parts = parts.reshape(2, 16, rows + 16, HEAD)

    with jax.named_scope("project_kv"):
        whole, kv_sum = project_kv(parts, wkv, rows)
        chunks = lax.all_to_all(kv_sum.reshape(8, rows // 4, HEAD), ("xh", "yl", "core"), 0, 0)
        chunks = jnp.sum(chunks.reshape(2, 2, 2, rows // 4, HEAD), axis=(0, 2)).astype(BF16)
        kv = jnp.concatenate([chunks[0], chunks[1]], axis=1)

    with jax.named_scope("project_q"):
        kv, whole = lax.optimization_barrier((kv, whole))
        q = project_q(place, whole, swap(whole), wq)

    with jax.named_scope("gather_kv"):
        kv, q = lax.optimization_barrier((gather(kv, "zh", 4), q))
        kv = gather(kv, "zl", 4)

    with jax.named_scope("swap_q"):
        q = (q + lax.ppermute(q, "xh", [(0, 1), (1, 0)])).astype(BF16)
        pair = lax.ppermute(q, "yl", [(0, 1), (1, 0)])

    with jax.named_scope("attend"):
        out = attend(place, q, pair, kv, swap(kv))
        return merge(lax.all_to_all(out, ("xh", "yl"), 0, 0))


def solution(mesh):
    fine = Mesh(mesh.devices.reshape(4, 4, 2, 2, 2, 2, 2), ("zh", "zl", "xh", "xl", "yh", "yl", "core"))
    return jax.shard_map(
        on_device,
        mesh=fine,
        in_specs=(P(ROW, COL), P(COL), P(ROW, COL), P(ROW, None), P(ROW, None)),
        out_specs=P(ROW, COL),
        check_vma=False,
    )
```

```python
import functools
import math

import jax
import jax.numpy as jnp
from jax import lax
from jax.experimental import pallas as pl
from jax.experimental.pallas import tpu as pltpu
from jax.sharding import Mesh
from jax.sharding import PartitionSpec as P

HEAD = 128
GROUP = 8
EPS = 1e-05
ROW = ("zh", "zl", "xh")
COL = ("xl", "yh", "yl", "core")
F32 = jnp.float32
BF16 = jnp.bfloat16


def gather(x, axes, n):
    return lax.all_to_all(jnp.broadcast_to(x[None], (n, *x.shape)), axes, 0, 0)


def swap(x):
    return lax.ppermute(x, "core", [(0, 1), (1, 0)])


def three(x):
    pieces = []
    for _ in range(3):
        piece = x.astype(BF16).astype(F32)
        pieces.append(piece)
        x = x - piece
    return pieces


def attend_kernel(place, own_ref, pair_ref, mine_ref, other_ref, out_ref, m_ref, l_ref, acc_ref):
    z, xh, yl, core = place[0], place[1], place[2], place[3]
    rows = own_ref.shape[1]
    scale = HEAD**-0.5 * math.log2(math.e)
    m_ref[...] = jnp.full(m_ref.shape, -1e30, F32)
    l_ref[...] = jnp.zeros(l_ref.shape, F32)
    acc_ref[...] = jnp.zeros(acc_ref.shape, F32)
    chunk = mine_ref.shape[2]
    half = 4 * chunk

    def block(group, masked):
        kv = jnp.concatenate(
            [mine_ref[:, group].reshape(half, 2 * HEAD), other_ref[:, group].reshape(half, 2 * HEAD)], axis=0
        )
        if masked:
            shape = (2 * rows, 2 * half)
            slot = lax.broadcasted_iota(jnp.int32, shape, 1)
            within = lax.rem(slot, half)
            owner = jnp.where(slot < half, core, 1 - core) + 4 * xh + 2 * yl
            key_pos = lax.div(within, chunk) * (2 * rows) + owner * chunk + lax.rem(within, chunk)
            query_pos = lax.rem(z, 4) * (2 * rows) + lax.broadcasted_iota(jnp.int32, shape, 0)
            seen = key_pos <= query_pos
        for head in range(4):
            q_ref = (own_ref, pair_ref)[head // 2]
            at = head % 2 * HEAD
            q = q_ref[:, :, at : at + HEAD].reshape(2 * rows, HEAD)
            s = lax.dot_general(q, kv[:, :HEAD], (((1,), (1,)), ((), ())), preferred_element_type=F32)
            if masked:
                s = jnp.where(seen, s, -1e30)
            m_old = m_ref[head]
            m_new = jnp.maximum(m_old, jnp.max(s, axis=1, keepdims=True))
            alpha = jnp.exp2((m_old - m_new) * scale)
            total = l_ref[head] * alpha
            weights = []
            for j in range(0, s.shape[1], HEAD):
                w = jnp.exp2((s[:, j : j + HEAD] - m_new) * scale)
                total = total + w
                weights.append(w.astype(BF16))
            p = jnp.concatenate(weights, axis=1)
            l_ref[head] = total
            m_ref[head] = m_new
            acc_ref[head] = acc_ref[head] * alpha + jnp.dot(p, kv[:, HEAD:], preferred_element_type=F32)

    mine_group = lax.div(z, 4)

    @pl.loop(0, mine_group)
    def _(group):
        block(group, False)

    block(mine_group, True)
    lane = lax.broadcasted_iota(jnp.int32, (2 * rows, HEAD), 1)
    for side in range(2):
        to = yl if side == 0 else 1 - yl
        stats = jnp.zeros((2 * rows, HEAD), F32)
        for i in range(2):
            head = side * 2 + i
            total = jnp.sum(l_ref[head], axis=1, keepdims=True)
            stats = jnp.where(lane == i, m_ref[head] * scale + jnp.log2(total), stats)
            part = (acc_ref[head] / total).astype(BF16)
            for x in range(2):
                out_ref[2 * x + to, :rows, i * HEAD : (i + 1) * HEAD] = part[x * rows : (x + 1) * rows]
        for x in range(2):
            sums = three(jnp.transpose(stats[x * rows : (x + 1) * rows])[:2])
            sums = jnp.concatenate([*sums, jnp.zeros((10, 2 * HEAD), F32)], axis=0)
            out_ref[2 * x + to, rows:, :] = sums.astype(BF16)


def attend(place, own, pair, mine, other):
    rows, cols = own.shape[1:]
    vmem = pl.BlockSpec(memory_space=pltpu.VMEM)
    return pl.pallas_call(
        attend_kernel,
        out_shape=jax.ShapeDtypeStruct((4, rows + 16, cols), BF16),
        in_specs=[pl.BlockSpec(memory_space=pltpu.SMEM), vmem, vmem, vmem, vmem],
        out_specs=vmem,
        scratch_shapes=[pltpu.VMEM((4, 2 * rows, HEAD), F32)] * 3,
        compiler_params=pltpu.CompilerParams(vmem_limit_bytes=40 * 1024 * 1024),
        cost_estimate=pl.CostEstimate(flops=2**31, bytes_accessed=2**22, transcendentals=2**22),
    )(place, own, pair, mine, other)


def merge_kernel(parts_ref, out_ref):
    rows = out_ref.shape[0]
    n = parts_ref.shape[0]
    sums = [parts_ref[i, rows:, :].astype(F32) for i in range(n)]
    sums = [s[0:2] + s[2:4] + s[4:6] for s in sums]
    most = functools.reduce(jnp.maximum, sums)
    shares = [jnp.exp2(s - most) for s in sums]
    total = functools.reduce(jnp.add, shares)
    columns = [jnp.transpose(jnp.concatenate([s / total] * (HEAD // 2), axis=0)) for s in shares]
    for i in range(2):
        at = slice(i * HEAD, (i + 1) * HEAD)
        out_ref[:, at] = sum(columns[k][:, i : i + 1] * parts_ref[k, :rows, at].astype(F32) for k in range(n)).astype(BF16)


def merge(parts):
    vmem = pl.BlockSpec(memory_space=pltpu.VMEM)
    return pl.pallas_call(
        merge_kernel,
        out_shape=jax.ShapeDtypeStruct((parts.shape[1] - 16, parts.shape[2]), BF16),
        in_specs=[vmem],
        out_specs=vmem,
        compiler_params=pltpu.CompilerParams(vmem_limit_bytes=40 * 1024 * 1024),
    )(parts)


def prep_kernel(tokens_ref, gain_ref, out_ref, block_ref, sems):
    rows = tokens_ref.shape[0]
    states = tokens_ref[...].astype(F32)
    sums = jnp.sum(states * states, axis=1, keepdims=True)
    left = jnp.transpose(jnp.broadcast_to(sums, (rows, HEAD)))[:1]
    pieces = three(jnp.concatenate([left[:, :HEAD], left[:, HEAD:]], axis=0))
    for q in range(4):
        at = slice(q * HEAD, (q + 1) * HEAD)
        gain = gain_ref[:, at].astype(F32)
        extra = jnp.concatenate([*pieces, gain, jnp.zeros((9, HEAD), F32)], axis=0)
        block_ref[q // 2, q % 2, :rows] = tokens_ref[:, at]
        block_ref[q // 2, q % 2, rows:] = extra.astype(BF16)
    copies = [
        pltpu.make_async_copy(block_ref, out_ref.at[:, to], sems.at[to]) for to in range(out_ref.shape[1])
    ]
    for copy in copies:
        copy.start()
    for copy in copies:
        copy.wait()


def prep(tokens, gain):
    vmem = pl.BlockSpec(memory_space=pltpu.VMEM)
    rows = tokens.shape[0] + 16
    return pl.pallas_call(
        prep_kernel,
        out_shape=jax.ShapeDtypeStruct((2, 8, 2, rows, HEAD), BF16),
        in_specs=[vmem, vmem],
        out_specs=pl.BlockSpec(memory_space=pltpu.HBM),
        scratch_shapes=[pltpu.VMEM((2, 2, rows, HEAD), BF16), pltpu.SemaphoreType.DMA((8,))],
        compiler_params=pltpu.CompilerParams(vmem_limit_bytes=60 * 1024 * 1024),
    )(tokens, gain)


def kv_kernel(parts_ref, w_ref, out_ref, kv_ref, t_ref, sems):
    rows = t_ref.shape[1]
    blocks = parts_ref.shape[1]
    copies = [pltpu.make_async_copy(t_ref.at[xh], out_ref.at[xh], sems.at[xh]) for xh in range(2)]
    for xh in range(2):
        extra = [parts_ref[xh, c, rows:].astype(F32) for c in range(blocks)]
        squares = functools.reduce(jnp.add, extra)
        mean_sq = (squares[4:6] + squares[2:4] + squares[0:2]) / (blocks * 4 * HEAD)
        inverse = lax.rsqrt(mean_sq + EPS)
        inverse = jnp.concatenate(
            [jnp.transpose(jnp.broadcast_to(inverse[i : i + 1], (HEAD, HEAD))) for i in range(2)], axis=0
        )
        total = jnp.zeros((rows, HEAD), F32)
        for c in range(0, blocks, 2):
            for d in (c, c + 1):
                t = parts_ref[xh, d, :rows].astype(F32) * inverse * extra[d][6:7]
                t_ref[xh, :, d * HEAD : (d + 1) * HEAD] = t.astype(BF16)
            w = jnp.concatenate([w_ref[d % 4, d // 4] for d in (c, c + 1)], axis=0)
            total += jnp.dot(t_ref[xh, :, c * HEAD : (c + 2) * HEAD], w, preferred_element_type=F32)
        kv_ref[xh] = total
        copies[xh].start()
    for copy in copies:
        copy.wait()


def project_kv(parts, w, rows):
    vmem = pl.BlockSpec(memory_space=pltpu.VMEM)
    blocks = parts.shape[1]
    return pl.pallas_call(
        kv_kernel,
        out_shape=(
            jax.ShapeDtypeStruct((2, rows, blocks * HEAD), BF16),
            jax.ShapeDtypeStruct((2, rows, HEAD), F32),
        ),
        in_specs=[vmem, vmem],
        out_specs=(pl.BlockSpec(memory_space=pltpu.HBM), vmem),
        scratch_shapes=[pltpu.VMEM((2, rows, blocks * HEAD), BF16), pltpu.SemaphoreType.DMA((2,))],
        compiler_params=pltpu.CompilerParams(vmem_limit_bytes=40 * 1024 * 1024),
        cost_estimate=pl.CostEstimate(flops=2**28, bytes_accessed=5 * 2**20, transcendentals=0),
    )(parts, w)


def q_kernel(place, mine_ref, other_ref, w_ref, out_ref):
    core = place[3]
    rows = mine_ref.shape[1]
    half = mine_ref.shape[2] // w_ref.shape[0]
    for xh in range(2):
        total = jnp.zeros((rows, w_ref.shape[2]), F32)
        for c in range(w_ref.shape[0]):
            t = jnp.concatenate([ref[xh, :, c * half : (c + 1) * half] for ref in (mine_ref, other_ref)], axis=1)
            w = jnp.concatenate(
                [w_ref[c, pl.ds(pl.multiple_of(at * half, half), half)] for at in (core, 1 - core)], axis=0
            )
            total += jnp.dot(t, w, preferred_element_type=F32)
        out_ref[xh] = total


def project_q(place, mine, other, w):
    vmem = pl.BlockSpec(memory_space=pltpu.VMEM)
    return pl.pallas_call(
        q_kernel,
        out_shape=jax.ShapeDtypeStruct((*mine.shape[:2], w.shape[2]), F32),
        in_specs=[pl.BlockSpec(memory_space=pltpu.SMEM), vmem, vmem, vmem],
        out_specs=vmem,
        compiler_params=pltpu.CompilerParams(vmem_limit_bytes=40 * 1024 * 1024),
        cost_estimate=pl.CostEstimate(flops=2**30, bytes_accessed=6 * 2**20, transcendentals=0),
    )(place, mine, other, w)


def on_device(tokens, norm_gain, w_query, w_key, w_value):
    at = lax.axis_index
    core = at("core")
    place = jnp.stack([at(("zh", "zl")), at("xh"), at("yl"), core]).astype(jnp.int32)
    rows, feats = tokens.shape
    half = w_key.shape[0] // 2

    with jax.named_scope("weights"):
        wq = lax.all_gather(jnp.pad(w_query, ((0, 64), (0, 0))), ("zh", "zl"), axis=0)
        head = at(("xl", "yh"))
        start = (core * half, head * HEAD)
        wkv = jnp.where(
            at("yl") == 0,
            lax.dynamic_slice(w_key, start, (half, HEAD)),
            lax.dynamic_slice(w_value, start, (half, HEAD)),
        )
        wkv = lax.all_gather(lax.all_gather(wkv, "zh"), "zl")

    with jax.named_scope("spread"):
        parts = prep(tokens, norm_gain.reshape(1, feats))
        parts = lax.all_to_all(parts.reshape(32, rows + 16, HEAD), ("xh",) + COL, 0, 0)
        parts = parts.reshape(2, 16, rows + 16, HEAD)

    with jax.named_scope("project_kv"):
        whole, kv_sum = project_kv(parts, wkv, rows)
        chunks = lax.all_to_all(kv_sum.reshape(8, rows // 4, HEAD), ("xh", "yl", "core"), 0, 0)
        chunks = jnp.sum(chunks.reshape(2, 2, 2, rows // 4, HEAD), axis=(0, 2)).astype(BF16)
        kv = jnp.concatenate([chunks[0], chunks[1]], axis=1)

    with jax.named_scope("project_q"):
        kv, whole = lax.optimization_barrier((kv, whole))
        q = project_q(place, whole, swap(whole), wq)

    with jax.named_scope("gather_kv"):
        kv, q = lax.optimization_barrier((gather(kv, "zh", 4), q))
        kv = gather(kv, "zl", 4)

    with jax.named_scope("swap_q"):
        q = (q + lax.ppermute(q, "xh", [(0, 1), (1, 0)])).astype(BF16)
        pair = lax.ppermute(q, "yl", [(0, 1), (1, 0)])

    with jax.named_scope("attend"):
        out = attend(place, q, pair, kv, swap(kv))
        return merge(lax.all_to_all(out, ("xh", "yl"), 0, 0))


def solution(mesh):
    fine = Mesh(mesh.devices.reshape(4, 4, 2, 2, 2, 2, 2), ("zh", "zl", "xh", "xl", "yh", "yl", "core"))
    return jax.shard_map(
        on_device,
        mesh=fine,
        in_specs=(P(ROW, COL), P(COL), P(ROW, COL), P(ROW, None), P(ROW, None)),
        out_specs=P(ROW, COL),
        check_vma=False,
    )
```

```python
import functools
import math

import jax
import jax.numpy as jnp
from jax import lax
from jax.experimental import pallas as pl
from jax.experimental.pallas import tpu as pltpu
from jax.sharding import Mesh
from jax.sharding import PartitionSpec as P

HEAD = 128
GROUP = 8
EPS = 1e-05
ROW = ("zh", "zl", "xh")
COL = ("xl", "yh", "yl", "core")
F32 = jnp.float32
BF16 = jnp.bfloat16


def gather(x, axes, n):
    return lax.all_to_all(jnp.broadcast_to(x[None], (n, *x.shape)), axes, 0, 0)


def swap(x):
    return lax.ppermute(x, "core", [(0, 1), (1, 0)])


def three(x):
    pieces = []
    for _ in range(3):
        piece = x.astype(BF16).astype(F32)
        pieces.append(piece)
        x = x - piece
    return pieces


def attend_kernel(place, q0_ref, q1_ref, q2_ref, q3_ref, mine_ref, other_ref, out_ref, m_ref, l_ref, acc_ref):
    z, xh, yl, core = place[0], place[1], place[2], place[3]
    rows = q0_ref.shape[0]
    scale = HEAD**-0.5 * math.log2(math.e)
    m_ref[...] = jnp.full(m_ref.shape, -1e30, F32)
    l_ref[...] = jnp.zeros(l_ref.shape, F32)
    acc_ref[...] = jnp.zeros(acc_ref.shape, F32)
    chunk = mine_ref.shape[2]
    half = 4 * chunk

    def block(group, masked):
        kv = jnp.concatenate(
            [mine_ref[:, group].reshape(half, 2 * HEAD), other_ref[:, group].reshape(half, 2 * HEAD)], axis=0
        )
        if masked:
            shape = (2 * rows, 2 * half)
            slot = lax.broadcasted_iota(jnp.int32, shape, 1)
            within = lax.rem(slot, half)
            owner = jnp.where(slot < half, core, 1 - core) + 4 * xh + 2 * yl
            key_pos = lax.div(within, chunk) * (2 * rows) + owner * chunk + lax.rem(within, chunk)
            query = lax.broadcasted_iota(jnp.int32, shape, 0)
            query = lax.rem(query + xh * rows, 2 * rows)
            query_pos = lax.rem(z, 4) * (2 * rows) + query
            seen = key_pos <= query_pos
        for head in range(4):
            at = slice(head % 2 * HEAD, (head % 2 + 1) * HEAD)
            q = jnp.concatenate([ref[:, at] for ref in ((q0_ref, q1_ref), (q2_ref, q3_ref))[head // 2]], axis=0)
            s = lax.dot_general(q, kv[:, :HEAD], (((1,), (1,)), ((), ())), preferred_element_type=F32)
            if masked:
                s = jnp.where(seen, s, -1e30)
            m_old = m_ref[head]
            m_new = jnp.maximum(m_old, jnp.max(s, axis=1, keepdims=True))
            alpha = jnp.exp2((m_old - m_new) * scale)
            total = l_ref[head] * alpha
            weights = []
            for j in range(0, s.shape[1], HEAD):
                w = jnp.exp2((s[:, j : j + HEAD] - m_new) * scale)
                total = total + w
                weights.append(w.astype(BF16))
            p = jnp.concatenate(weights, axis=1)
            l_ref[head] = total
            m_ref[head] = m_new
            acc_ref[head] = acc_ref[head] * alpha + jnp.dot(p, kv[:, HEAD:], preferred_element_type=F32)

    mine_group = lax.div(z, 4)

    @pl.loop(0, mine_group)
    def _(group):
        block(group, False)

    block(mine_group, True)
    lane = lax.broadcasted_iota(jnp.int32, (2 * rows, HEAD), 1)
    for side in range(2):
        to = yl if side == 0 else 1 - yl
        stats = jnp.zeros((2 * rows, HEAD), F32)
        for i in range(2):
            head = side * 2 + i
            total = jnp.sum(l_ref[head], axis=1, keepdims=True)
            stats = jnp.where(lane == i, m_ref[head] * scale + jnp.log2(total), stats)
            part = (acc_ref[head] / total).astype(BF16)
            for x in range(2):
                out_ref[2 * (x ^ xh) + to, :rows, i * HEAD : (i + 1) * HEAD] = part[x * rows : (x + 1) * rows]
        for x in range(2):
            sums = three(jnp.transpose(stats[x * rows : (x + 1) * rows])[:2])
            sums = jnp.concatenate([*sums, jnp.zeros((10, 2 * HEAD), F32)], axis=0)
            out_ref[2 * (x ^ xh) + to, rows:, :] = sums.astype(BF16)


def attend(place, queries, mine, other):
    rows, cols = queries[0].shape
    vmem = pl.BlockSpec(memory_space=pltpu.VMEM)
    return pl.pallas_call(
        attend_kernel,
        out_shape=jax.ShapeDtypeStruct((4, rows + 16, cols), BF16),
        in_specs=[pl.BlockSpec(memory_space=pltpu.SMEM)] + [vmem] * 6,
        out_specs=vmem,
        scratch_shapes=[pltpu.VMEM((4, 2 * rows, HEAD), F32)] * 3,
        compiler_params=pltpu.CompilerParams(vmem_limit_bytes=40 * 1024 * 1024),
        cost_estimate=pl.CostEstimate(flops=2**31, bytes_accessed=2**22, transcendentals=2**22),
    )(place, *queries, mine, other)


def merge_kernel(parts_ref, out_ref):
    rows = out_ref.shape[0]
    n = parts_ref.shape[0]
    sums = [parts_ref[i, rows:, :].astype(F32) for i in range(n)]
    sums = [s[0:2] + s[2:4] + s[4:6] for s in sums]
    most = functools.reduce(jnp.maximum, sums)
    shares = [jnp.exp2(s - most) for s in sums]
    total = functools.reduce(jnp.add, shares)
    columns = [jnp.transpose(jnp.concatenate([s / total] * (HEAD // 2), axis=0)) for s in shares]
    for i in range(2):
        at = slice(i * HEAD, (i + 1) * HEAD)
        out_ref[:, at] = sum(columns[k][:, i : i + 1] * parts_ref[k, :rows, at].astype(F32) for k in range(n)).astype(BF16)


def merge(parts):
    vmem = pl.BlockSpec(memory_space=pltpu.VMEM)
    return pl.pallas_call(
        merge_kernel,
        out_shape=jax.ShapeDtypeStruct((parts.shape[1] - 16, parts.shape[2]), BF16),
        in_specs=[vmem],
        out_specs=vmem,
        compiler_params=pltpu.CompilerParams(vmem_limit_bytes=40 * 1024 * 1024),
    )(parts)


def prep_kernel(tokens_ref, gain_ref, w_ref, out_ref, padded_ref, block_ref, sems):
    rows = tokens_ref.shape[0]
    states = tokens_ref[...].astype(F32)
    sums = jnp.sum(states * states, axis=1, keepdims=True)
    left = jnp.transpose(jnp.broadcast_to(sums, (rows, HEAD)))[:1]
    pieces = three(jnp.concatenate([left[:, :HEAD], left[:, HEAD:]], axis=0))
    for q in range(4):
        at = slice(q * HEAD, (q + 1) * HEAD)
        gain = gain_ref[at].astype(F32).reshape(1, HEAD)
        extra = jnp.concatenate([*pieces, gain, jnp.zeros((9, HEAD), F32)], axis=0)
        block_ref[q // 2, q % 2, :rows] = tokens_ref[:, at]
        block_ref[q // 2, q % 2, rows:] = extra.astype(BF16)
    copies = [
        pltpu.make_async_copy(block_ref, out_ref.at[:, to], sems.at[to]) for to in range(out_ref.shape[1])
    ]
    for copy in copies:
        copy.start()
    depth = w_ref.shape[0]
    padded_ref[:depth] = w_ref[...]
    padded_ref[depth:] = jnp.zeros((padded_ref.shape[0] - depth, w_ref.shape[1]), BF16)
    for copy in copies:
        copy.wait()


def prep(tokens, gain, w):
    vmem = pl.BlockSpec(memory_space=pltpu.VMEM)
    rows = tokens.shape[0] + 16
    return pl.pallas_call(
        prep_kernel,
        out_shape=(
            jax.ShapeDtypeStruct((2, 8, 2, rows, HEAD), BF16),
            jax.ShapeDtypeStruct((w.shape[0] + 64, w.shape[1]), BF16),
        ),
        in_specs=[vmem, vmem, vmem],
        out_specs=(pl.BlockSpec(memory_space=pltpu.HBM), vmem),
        scratch_shapes=[pltpu.VMEM((2, 2, rows, HEAD), BF16), pltpu.SemaphoreType.DMA((8,))],
        compiler_params=pltpu.CompilerParams(vmem_limit_bytes=60 * 1024 * 1024),
    )(tokens, gain, w)


def kv_kernel(parts_ref, w_ref, out_ref, kv_ref, t_ref, sems):
    rows = t_ref.shape[1]
    blocks = parts_ref.shape[1]
    copies = [pltpu.make_async_copy(t_ref.at[xh], out_ref.at[xh], sems.at[xh]) for xh in range(2)]
    for xh in range(2):
        extra = [parts_ref[xh, c, rows:].astype(F32) for c in range(blocks)]
        squares = functools.reduce(jnp.add, extra)
        mean_sq = (squares[4:6] + squares[2:4] + squares[0:2]) / (blocks * 4 * HEAD)
        inverse = lax.rsqrt(mean_sq + EPS)
        inverse = jnp.concatenate(
            [jnp.transpose(jnp.broadcast_to(inverse[i : i + 1], (HEAD, HEAD))) for i in range(2)], axis=0
        )
        total = jnp.zeros((rows, HEAD), F32)
        for c in range(0, blocks, 2):
            for d in (c, c + 1):
                t = parts_ref[xh, d, :rows].astype(F32) * inverse * extra[d][6:7]
                t_ref[xh, :, d * HEAD : (d + 1) * HEAD] = t.astype(BF16)
            w = jnp.concatenate([w_ref[d % 4, d // 4] for d in (c, c + 1)], axis=0)
            total += jnp.dot(t_ref[xh, :, c * HEAD : (c + 2) * HEAD], w, preferred_element_type=F32)
        kv_ref[xh] = total
        copies[xh].start()
    for copy in copies:
        copy.wait()


def project_kv(parts, w, rows):
    vmem = pl.BlockSpec(memory_space=pltpu.VMEM)
    blocks = parts.shape[1]
    return pl.pallas_call(
        kv_kernel,
        out_shape=(
            jax.ShapeDtypeStruct((2, rows, blocks * HEAD), BF16),
            jax.ShapeDtypeStruct((2, rows, HEAD), F32),
        ),
        in_specs=[vmem, vmem],
        out_specs=(pl.BlockSpec(memory_space=pltpu.HBM), vmem),
        scratch_shapes=[pltpu.VMEM((2, rows, blocks * HEAD), BF16), pltpu.SemaphoreType.DMA((2,))],
        compiler_params=pltpu.CompilerParams(vmem_limit_bytes=40 * 1024 * 1024),
        cost_estimate=pl.CostEstimate(flops=2**28, bytes_accessed=5 * 2**20, transcendentals=0),
    )(parts, w)


def q_kernel(place, mine_ref, other_ref, w_ref, keep_ref, send_ref):
    xh, core = place[1], place[3]
    rows = mine_ref.shape[1]
    half = mine_ref.shape[2] // w_ref.shape[0]
    for out_ref, x in ((send_ref, 1 - xh), (keep_ref, xh)):
        total = jnp.zeros((rows, w_ref.shape[2]), F32)
        for c in range(w_ref.shape[0]):
            t = jnp.concatenate([ref[x, :, c * half : (c + 1) * half] for ref in (mine_ref, other_ref)], axis=1)
            w = jnp.concatenate(
                [w_ref[c, pl.ds(pl.multiple_of(at * half, half), half)] for at in (core, 1 - core)], axis=0
            )
            total += jnp.dot(t, w, preferred_element_type=F32)
        out_ref[...] = total.astype(out_ref.dtype)


def project_q(place, mine, other, w):
    vmem = pl.BlockSpec(memory_space=pltpu.VMEM)
    return pl.pallas_call(
        q_kernel,
        out_shape=[jax.ShapeDtypeStruct((mine.shape[1], w.shape[2]), kind) for kind in (F32, BF16)],
        in_specs=[pl.BlockSpec(memory_space=pltpu.SMEM), vmem, vmem, vmem],
        out_specs=[vmem, vmem],
        compiler_params=pltpu.CompilerParams(vmem_limit_bytes=40 * 1024 * 1024),
        cost_estimate=pl.CostEstimate(flops=2**30, bytes_accessed=6 * 2**20, transcendentals=0),
    )(place, mine, other, w)


def on_device(tokens, norm_gain, w_query, w_key, w_value):
    at = lax.axis_index
    core = at("core")
    place = jnp.stack([at(("zh", "zl")), at("xh"), at("yl"), core]).astype(jnp.int32)
    rows, feats = tokens.shape
    half = w_key.shape[0] // 2

    with jax.named_scope("prep"):
        parts, padded = prep(tokens, norm_gain, w_query)

    with jax.named_scope("weights"):
        wq = lax.all_gather(padded, ("zh", "zl"), axis=0)
        start = (core * half, at(("xl", "yh")) * HEAD)
        wkv = jnp.where(
            at("yl") == 0,
            lax.dynamic_slice(w_key, start, (half, HEAD)),
            lax.dynamic_slice(w_value, start, (half, HEAD)),
        )
        wkv = lax.all_gather(lax.all_gather(wkv, "zh"), "zl")

    with jax.named_scope("spread"):
        parts = lax.all_to_all(parts.reshape(32, rows + 16, HEAD), ("xh",) + COL, 0, 0)
        parts = parts.reshape(2, 16, rows + 16, HEAD)

    with jax.named_scope("project_kv"):
        whole, kv_sum = project_kv(parts, wkv, rows)
        chunks = lax.all_to_all(kv_sum.reshape(8, rows // 4, HEAD), ("xh", "yl", "core"), 0, 0)
        chunks = jnp.sum(chunks.reshape(2, 2, 2, rows // 4, HEAD), axis=(0, 2)).astype(BF16)
        kv = jnp.concatenate([chunks[0], chunks[1]], axis=1)

    with jax.named_scope("project_q"):
        kv, whole = lax.optimization_barrier((kv, whole))
        q_keep, q_send = project_q(place, whole, swap(whole), wq)
        q = (q_keep + lax.ppermute(q_send, "xh", [(0, 1), (1, 0)]).astype(F32)).astype(BF16)

    with jax.named_scope("gather_kv"):
        kv, q = lax.optimization_barrier((gather(kv, "zh", 4), q))
        kv = gather(kv, "zl", 4)

    with jax.named_scope("swap_q"):
        queries = (
            q,
            lax.ppermute(q, "xh", [(0, 1), (1, 0)]),
            lax.ppermute(q, "yl", [(0, 1), (1, 0)]),
            lax.ppermute(q, ("xh", "yl"), [(0, 3), (1, 2), (2, 1), (3, 0)]),
        )

    with jax.named_scope("attend"):
        kv, queries = lax.optimization_barrier((kv, queries))
        out = attend(place, queries, kv, swap(kv))
        return merge(lax.all_to_all(out, ("xh", "yl"), 0, 0))


def solution(mesh):
    fine = Mesh(mesh.devices.reshape(4, 4, 2, 2, 2, 2, 2), ("zh", "zl", "xh", "xl", "yh", "yl", "core"))
    return jax.shard_map(
        on_device,
        mesh=fine,
        in_specs=(P(ROW, COL), P(COL), P(ROW, COL), P(ROW, None), P(ROW, None)),
        out_specs=P(ROW, COL),
        check_vma=False,
    )
```

```python
import functools
import math

import jax
import jax.numpy as jnp
from jax import lax
from jax.experimental import pallas as pl
from jax.experimental.pallas import tpu as pltpu
from jax.sharding import Mesh
from jax.sharding import PartitionSpec as P

HEAD = 128
GROUP = 8
EPS = 1e-05
ROW = ("zh", "zl", "xh")
COL = ("xl", "yh", "yl", "core")
F32 = jnp.float32
BF16 = jnp.bfloat16


def gather(x, axes, n):
    return lax.all_to_all(jnp.broadcast_to(x[None], (n, *x.shape)), axes, 0, 0)


def swap(x):
    return lax.ppermute(x, "core", [(0, 1), (1, 0)])


def three(x):
    pieces = []
    for _ in range(3):
        piece = x.astype(BF16).astype(F32)
        pieces.append(piece)
        x = x - piece
    return pieces


def attend_kernel(side, place, q_ref, mine_ref, other_ref, *refs):
    out_ref, m_ref, l_ref, acc_ref = refs[-4:]
    z, xh, yl, core = place[0], place[1], place[2], place[3]
    rows = q_ref.shape[1]
    scale = HEAD**-0.5 * math.log2(math.e)
    m_ref[...] = jnp.full(m_ref.shape, -1e30, F32)
    l_ref[...] = jnp.zeros(l_ref.shape, F32)
    acc_ref[...] = jnp.zeros(acc_ref.shape, F32)
    chunk = mine_ref.shape[2]
    half = 4 * chunk

    def block(group, masked):
        kv = jnp.concatenate(
            [mine_ref[:, group].reshape(half, 2 * HEAD), other_ref[:, group].reshape(half, 2 * HEAD)], axis=0
        )
        if masked:
            shape = (2 * rows, 2 * half)
            slot = lax.broadcasted_iota(jnp.int32, shape, 1)
            within = lax.rem(slot, half)
            owner = jnp.where(slot < half, core, 1 - core) + 4 * xh + 2 * yl
            key_pos = lax.div(within, chunk) * (2 * rows) + owner * chunk + lax.rem(within, chunk)
            query_pos = lax.rem(z, 4) * (2 * rows) + lax.broadcasted_iota(jnp.int32, shape, 0)
            seen = key_pos <= query_pos
        for head in range(2):
            q = q_ref[:, :, head * HEAD : (head + 1) * HEAD].reshape(2 * rows, HEAD)
            s = lax.dot_general(q, kv[:, :HEAD], (((1,), (1,)), ((), ())), preferred_element_type=F32)
            if masked:
                s = jnp.where(seen, s, -1e30)
            m_old = m_ref[head]
            m_new = jnp.maximum(m_old, jnp.max(s, axis=1, keepdims=True))
            alpha = jnp.exp2((m_old - m_new) * scale)
            total = l_ref[head] * alpha
            weights = []
            for j in range(0, s.shape[1], HEAD):
                w = jnp.exp2((s[:, j : j + HEAD] - m_new) * scale)
                total = total + w
                weights.append(w.astype(BF16))
            p = jnp.concatenate(weights, axis=1)
            l_ref[head] = total
            m_ref[head] = m_new
            acc_ref[head] = acc_ref[head] * alpha + jnp.dot(p, kv[:, HEAD:], preferred_element_type=F32)

    last = lax.div(z, 4)

    @pl.loop(0, last)
    def _(group):
        block(group, False)

    block(last, True)
    lane = lax.broadcasted_iota(jnp.int32, (2 * rows, HEAD), 1)
    to = yl if side == 0 else 1 - yl
    stats = jnp.zeros((2 * rows, HEAD), F32)
    for head in range(2):
        total = jnp.sum(l_ref[head], axis=1, keepdims=True)
        stats = jnp.where(lane == head, m_ref[head] * scale + jnp.log2(total), stats)
        part = (acc_ref[head] / total).astype(BF16)
        for x in range(2):
            out_ref[2 * x + to, :rows, head * HEAD : (head + 1) * HEAD] = part[x * rows : (x + 1) * rows]
    for x in range(2):
        sums = three(jnp.transpose(stats[x * rows : (x + 1) * rows])[:2])
        sums = jnp.concatenate([*sums, jnp.zeros((10, 2 * HEAD), F32)], axis=0)
        out_ref[2 * x + to, rows:, :] = sums.astype(BF16)


def attend(side, place, q, mine, other, *first):
    rows, cols = q.shape[1:]
    vmem = pl.BlockSpec(memory_space=pltpu.VMEM)
    return pl.pallas_call(
        functools.partial(attend_kernel, side),
        out_shape=jax.ShapeDtypeStruct((4, rows + 16, cols), BF16),
        in_specs=[pl.BlockSpec(memory_space=pltpu.SMEM)] + [vmem] * (3 + len(first)),
        out_specs=vmem,
        scratch_shapes=[pltpu.VMEM((2, 2 * rows, HEAD), F32)] * 3,
        input_output_aliases={4: 0} if first else {},
        compiler_params=pltpu.CompilerParams(vmem_limit_bytes=40 * 1024 * 1024),
        cost_estimate=pl.CostEstimate(flops=2**30, bytes_accessed=2**22, transcendentals=2**21),
    )(place, q, mine, other, *first)


def merge_kernel(parts_ref, out_ref):
    rows = out_ref.shape[0]
    n = parts_ref.shape[0]
    sums = [parts_ref[i, rows:, :].astype(F32) for i in range(n)]
    sums = [s[0:2] + s[2:4] + s[4:6] for s in sums]
    most = functools.reduce(jnp.maximum, sums)
    shares = [jnp.exp2(s - most) for s in sums]
    total = functools.reduce(jnp.add, shares)
    columns = [jnp.transpose(jnp.concatenate([s / total] * (HEAD // 2), axis=0)) for s in shares]
    for i in range(2):
        at = slice(i * HEAD, (i + 1) * HEAD)
        out_ref[:, at] = sum(columns[k][:, i : i + 1] * parts_ref[k, :rows, at].astype(F32) for k in range(n)).astype(BF16)


def merge(parts):
    vmem = pl.BlockSpec(memory_space=pltpu.VMEM)
    return pl.pallas_call(
        merge_kernel,
        out_shape=jax.ShapeDtypeStruct((parts.shape[1] - 16, parts.shape[2]), BF16),
        in_specs=[vmem],
        out_specs=vmem,
        compiler_params=pltpu.CompilerParams(vmem_limit_bytes=40 * 1024 * 1024),
    )(parts)


def prep_kernel(tokens_ref, gain_ref, w_ref, out_ref, padded_ref, block_ref, sems):
    rows = tokens_ref.shape[0]
    states = tokens_ref[...].astype(F32)
    sums = jnp.sum(states * states, axis=1, keepdims=True)
    left = jnp.transpose(jnp.broadcast_to(sums, (rows, HEAD)))[:1]
    pieces = three(jnp.concatenate([left[:, :HEAD], left[:, HEAD:]], axis=0))
    for q in range(4):
        at = slice(q * HEAD, (q + 1) * HEAD)
        gain = gain_ref[at].astype(F32).reshape(1, HEAD)
        extra = jnp.concatenate([*pieces, gain, jnp.zeros((9, HEAD), F32)], axis=0)
        block_ref[q // 2, q % 2, :rows] = tokens_ref[:, at]
        block_ref[q // 2, q % 2, rows:] = extra.astype(BF16)
    copies = [
        pltpu.make_async_copy(block_ref, out_ref.at[:, to], sems.at[to]) for to in range(out_ref.shape[1])
    ]
    for copy in copies:
        copy.start()
    depth = w_ref.shape[0]
    padded_ref[:depth] = w_ref[...]
    padded_ref[depth:] = jnp.zeros((padded_ref.shape[0] - depth, w_ref.shape[1]), BF16)
    for copy in copies:
        copy.wait()


def prep(tokens, gain, w):
    vmem = pl.BlockSpec(memory_space=pltpu.VMEM)
    rows = tokens.shape[0] + 16
    return pl.pallas_call(
        prep_kernel,
        out_shape=(
            jax.ShapeDtypeStruct((2, 8, 2, rows, HEAD), BF16),
            jax.ShapeDtypeStruct((w.shape[0] + 64, w.shape[1]), BF16),
        ),
        in_specs=[vmem, vmem, vmem],
        out_specs=(pl.BlockSpec(memory_space=pltpu.HBM), vmem),
        scratch_shapes=[pltpu.VMEM((2, 2, rows, HEAD), BF16), pltpu.SemaphoreType.DMA((8,))],
        compiler_params=pltpu.CompilerParams(vmem_limit_bytes=60 * 1024 * 1024),
    )(tokens, gain, w)


def kv_kernel(parts_ref, w_ref, out_ref, kv_ref, t_ref, sems):
    rows = t_ref.shape[1]
    blocks = parts_ref.shape[1]
    copies = [pltpu.make_async_copy(t_ref.at[xh], out_ref.at[xh], sems.at[xh]) for xh in range(2)]
    for xh in range(2):
        extra = [parts_ref[xh, c, rows:].astype(F32) for c in range(blocks)]
        squares = functools.reduce(jnp.add, extra)
        mean_sq = (squares[4:6] + squares[2:4] + squares[0:2]) / (blocks * 4 * HEAD)
        inverse = lax.rsqrt(mean_sq + EPS)
        inverse = jnp.concatenate(
            [jnp.transpose(jnp.broadcast_to(inverse[i : i + 1], (HEAD, HEAD))) for i in range(2)], axis=0
        )
        total = jnp.zeros((rows, HEAD), F32)
        for c in range(0, blocks, 2):
            for d in (c, c + 1):
                t = parts_ref[xh, d, :rows].astype(F32) * inverse * extra[d][6:7]
                t_ref[xh, :, d * HEAD : (d + 1) * HEAD] = t.astype(BF16)
            w = jnp.concatenate([w_ref[d % 4, d // 4] for d in (c, c + 1)], axis=0)
            total += jnp.dot(t_ref[xh, :, c * HEAD : (c + 2) * HEAD], w, preferred_element_type=F32)
        kv_ref[xh] = total
        copies[xh].start()
    for copy in copies:
        copy.wait()


def project_kv(parts, w, rows):
    vmem = pl.BlockSpec(memory_space=pltpu.VMEM)
    blocks = parts.shape[1]
    return pl.pallas_call(
        kv_kernel,
        out_shape=(
            jax.ShapeDtypeStruct((2, rows, blocks * HEAD), BF16),
            jax.ShapeDtypeStruct((2, rows, HEAD), F32),
        ),
        in_specs=[vmem, vmem],
        out_specs=(pl.BlockSpec(memory_space=pltpu.HBM), vmem),
        scratch_shapes=[pltpu.VMEM((2, rows, blocks * HEAD), BF16), pltpu.SemaphoreType.DMA((2,))],
        compiler_params=pltpu.CompilerParams(vmem_limit_bytes=40 * 1024 * 1024),
        cost_estimate=pl.CostEstimate(flops=2**28, bytes_accessed=5 * 2**20, transcendentals=0),
    )(parts, w)


def q_kernel(place, mine_ref, other_ref, w_ref, out_ref):
    core = place[3]
    rows = mine_ref.shape[1]
    half = mine_ref.shape[2] // w_ref.shape[0]
    for x in range(2):
        total = jnp.zeros((rows, w_ref.shape[2]), F32)
        for c in range(w_ref.shape[0]):
            t = jnp.concatenate([ref[x, :, c * half : (c + 1) * half] for ref in (mine_ref, other_ref)], axis=1)
            w = jnp.concatenate(
                [w_ref[c, pl.ds(pl.multiple_of(at * half, half), half)] for at in (core, 1 - core)], axis=0
            )
            total += jnp.dot(t, w, preferred_element_type=F32)
        out_ref[x] = total


def project_q(place, mine, other, w):
    vmem = pl.BlockSpec(memory_space=pltpu.VMEM)
    return pl.pallas_call(
        q_kernel,
        out_shape=jax.ShapeDtypeStruct((*mine.shape[:2], w.shape[2]), F32),
        in_specs=[pl.BlockSpec(memory_space=pltpu.SMEM), vmem, vmem, vmem],
        out_specs=vmem,
        compiler_params=pltpu.CompilerParams(vmem_limit_bytes=40 * 1024 * 1024),
        cost_estimate=pl.CostEstimate(flops=2**30, bytes_accessed=6 * 2**20, transcendentals=0),
    )(place, mine, other, w)


def on_device(tokens, norm_gain, w_query, w_key, w_value):
    at = lax.axis_index
    core = at("core")
    place = jnp.stack([at(("zh", "zl")), at("xh"), at("yl"), core]).astype(jnp.int32)
    rows, feats = tokens.shape
    half = w_key.shape[0] // 2

    with jax.named_scope("prep"):
        parts, padded = prep(tokens, norm_gain, w_query)

    with jax.named_scope("weights"):
        wq = lax.all_gather(padded, ("zh", "zl"), axis=0)
        start = (core * half, at(("xl", "yh")) * HEAD)
        wkv = jnp.where(
            at("yl") == 0,
            lax.dynamic_slice(w_key, start, (half, HEAD)),
            lax.dynamic_slice(w_value, start, (half, HEAD)),
        )
        wkv = lax.all_gather(lax.all_gather(wkv, "zh"), "zl")

    with jax.named_scope("spread"):
        parts = lax.all_to_all(parts.reshape(32, rows + 16, HEAD), ("xh",) + COL, 0, 0)
        parts = parts.reshape(2, 16, rows + 16, HEAD)

    with jax.named_scope("project_kv"):
        whole, kv_sum = project_kv(parts, wkv, rows)
        chunks = lax.all_to_all(kv_sum.reshape(8, rows // 4, HEAD), ("xh", "yl", "core"), 0, 0)
        chunks = jnp.sum(chunks.reshape(2, 2, 2, rows // 4, HEAD), axis=(0, 2)).astype(BF16)
        kv = jnp.concatenate([chunks[0], chunks[1]], axis=1)

    with jax.named_scope("gather_kv"):
        kv, wq = lax.optimization_barrier((lax.all_gather(kv, "zh"), wq))
        kv = gather(kv, "zl", 4)

    with jax.named_scope("project_q"):
        q = project_q(place, whole, swap(whole), wq)
        q = (q + lax.ppermute(q, "xh", [(0, 1), (1, 0)])).astype(BF16)
        pair = lax.ppermute(q, "yl", [(0, 1), (1, 0)])

    with jax.named_scope("attend"):
        swapped = swap(kv)
        out = attend(0, place, q, kv, swapped)
        out = attend(1, place, pair, kv, swapped, out)
        return merge(lax.all_to_all(out, ("xh", "yl"), 0, 0))


def solution(mesh):
    fine = Mesh(mesh.devices.reshape(4, 4, 2, 2, 2, 2, 2), ("zh", "zl", "xh", "xl", "yh", "yl", "core"))
    return jax.shard_map(
        on_device,
        mesh=fine,
        in_specs=(P(ROW, COL), P(COL), P(ROW, COL), P(ROW, None), P(ROW, None)),
        out_specs=P(ROW, COL),
        check_vma=False,
    )
```

```python
import functools
import math

import jax
import jax.numpy as jnp
from jax import lax
from jax.experimental import pallas as pl
from jax.experimental.pallas import tpu as pltpu
from jax.sharding import Mesh
from jax.sharding import PartitionSpec as P

HEAD = 128
GROUP = 8
EPS = 1e-05
ROW = ("zh", "zl", "xh")
COL = ("xl", "yh", "yl", "core")
F32 = jnp.float32
BF16 = jnp.bfloat16


def gather(x, axes, n):
    return lax.all_to_all(jnp.broadcast_to(x[None], (n, *x.shape)), axes, 0, 0)


def swap(x):
    return lax.ppermute(x, "core", [(0, 1), (1, 0)])


def three(x):
    pieces = []
    for _ in range(3):
        piece = x.astype(BF16).astype(F32)
        pieces.append(piece)
        x = x - piece
    return pieces


def attend_kernel(side, place, q_ref, mine_ref, other_ref, *refs):
    out_ref = refs[-1]
    z, xh, yl, core = place[0], place[1], place[2], place[3]
    rows = q_ref.shape[1]
    scale = HEAD**-0.5 * math.log2(math.e)
    chunk = mine_ref.shape[2]
    half = 4 * chunk
    to = yl if side == 0 else 1 - yl
    lane = lax.broadcasted_iota(jnp.int32, (rows, HEAD), 1)

    def block(group):
        return jnp.concatenate(
            [ref[:, group].reshape(half, 2 * HEAD) for ref in (mine_ref, other_ref)], axis=0
        )

    def run(last, x):
        shape = (rows, 2 * half)
        slot = lax.broadcasted_iota(jnp.int32, shape, 1)
        within = lax.rem(slot, half)
        owner = jnp.where(slot < half, core, 1 - core) + 4 * xh + 2 * yl
        key_pos = lax.div(within, chunk) * (2 * rows) + owner * chunk + lax.rem(within, chunk)
        query_pos = lax.rem(z, 4) * (2 * rows) + x * rows + lax.broadcasted_iota(jnp.int32, shape, 0)
        seen = key_pos <= query_pos
        stats = jnp.zeros((rows, HEAD), F32)
        for head in range(2):
            q = q_ref[x, :, head * HEAD : (head + 1) * HEAD]
            scores = [
                lax.dot_general(q, block(g)[:, :HEAD], (((1,), (1,)), ((), ())), preferred_element_type=F32)
                for g in range(last + 1)
            ]
            scores[last] = jnp.where(seen, scores[last], -1e30)
            pieces = [part[:, j : j + HEAD] for part in scores for j in range(0, 2 * half, HEAD)]
            most = jnp.max(functools.reduce(jnp.maximum, pieces), axis=1, keepdims=True)
            total = jnp.zeros((rows, HEAD), F32)
            acc = jnp.zeros((rows, HEAD), F32)
            for g in range(last + 1):
                weights = []
                for j in range(0, 2 * half, HEAD):
                    w = jnp.exp2((scores[g][:, j : j + HEAD] - most) * scale)
                    total = total + w
                    weights.append(w.astype(BF16))
                p = jnp.concatenate(weights, axis=1)
                acc = acc + jnp.dot(p, block(g)[:, HEAD:], preferred_element_type=F32)
            total = jnp.sum(total, axis=1, keepdims=True)
            stats = jnp.where(lane == head, most * scale + jnp.log2(total), stats)
            out_ref[2 * x + to, :rows, head * HEAD : (head + 1) * HEAD] = (acc / total).astype(BF16)
        sums = three(jnp.transpose(stats)[:2])
        sums = jnp.concatenate([*sums, jnp.zeros((10, rows), F32)], axis=0)
        out_ref[2 * x + to, rows:, :] = sums.astype(BF16)

    for last in range(4):

        @pl.when(lax.div(z, 4) == last)
        def _():
            for x in range(2):
                run(last, x)


def attend(side, place, q, mine, other, *first):
    rows, cols = q.shape[1:]
    vmem = pl.BlockSpec(memory_space=pltpu.VMEM)
    return pl.pallas_call(
        functools.partial(attend_kernel, side),
        out_shape=jax.ShapeDtypeStruct((4, rows + 16, cols), BF16),
        in_specs=[pl.BlockSpec(memory_space=pltpu.SMEM)] + [vmem] * (3 + len(first)),
        out_specs=vmem,
        input_output_aliases={4: 0} if first else {},
        compiler_params=pltpu.CompilerParams(vmem_limit_bytes=40 * 1024 * 1024),
        cost_estimate=pl.CostEstimate(flops=2**30, bytes_accessed=2**22, transcendentals=2**21),
    )(place, q, mine, other, *first)


def merge_kernel(parts_ref, out_ref):
    rows = out_ref.shape[0]
    n = parts_ref.shape[0]
    sums = [parts_ref[i, rows:, :].astype(F32) for i in range(n)]
    sums = [s[0:2] + s[2:4] + s[4:6] for s in sums]
    most = functools.reduce(jnp.maximum, sums)
    shares = [jnp.exp2(s - most) for s in sums]
    total = functools.reduce(jnp.add, shares)
    columns = [jnp.transpose(jnp.concatenate([s / total] * (HEAD // 2), axis=0)) for s in shares]
    for i in range(2):
        at = slice(i * HEAD, (i + 1) * HEAD)
        out_ref[:, at] = sum(columns[k][:, i : i + 1] * parts_ref[k, :rows, at].astype(F32) for k in range(n)).astype(BF16)


def merge(parts):
    vmem = pl.BlockSpec(memory_space=pltpu.VMEM)
    return pl.pallas_call(
        merge_kernel,
        out_shape=jax.ShapeDtypeStruct((parts.shape[1] - 16, parts.shape[2]), BF16),
        in_specs=[vmem],
        out_specs=vmem,
        compiler_params=pltpu.CompilerParams(vmem_limit_bytes=40 * 1024 * 1024),
    )(parts)


def prep_kernel(
    place, tokens_ref, gain_ref, query_ref, key_ref, value_ref, out_ref, padded_ref, own_ref, block_ref, zeros_ref, sems
):
    rows = tokens_ref.shape[0]
    n = out_ref.shape[1]
    depth = query_ref.shape[0]
    yl, core, head = place[2], place[3], place[4]
    zeros_ref[...] = jnp.zeros(zeros_ref.shape, BF16)
    at = (pl.ds(pl.multiple_of(core * HEAD, HEAD), HEAD), pl.ds(pl.multiple_of(head * HEAD, HEAD), HEAD))
    keys = pltpu.make_async_copy(key_ref.at[at], own_ref, sems.at[2 * n])
    values = pltpu.make_async_copy(value_ref.at[at], own_ref, sems.at[2 * n + 1])
    pads = [
        pltpu.make_async_copy(query_ref, padded_ref.at[:depth], sems.at[2 * n + 2]),
        pltpu.make_async_copy(zeros_ref, padded_ref.at[depth:], sems.at[2 * n + 3]),
    ]
    for q in range(4):
        block_ref[q // 2, q % 2, :rows] = tokens_ref[:, q * HEAD : (q + 1) * HEAD]
    body = [
        pltpu.make_async_copy(block_ref.at[:, :, :rows], out_ref.at[:, to, :, :rows], sems.at[to]) for to in range(n)
    ]
    tail = [
        pltpu.make_async_copy(block_ref.at[:, :, rows:], out_ref.at[:, to, :, rows:], sems.at[n + to]) for to in range(n)
    ]
    for copy in (*pads, *body):
        copy.start()

    @pl.when(yl == 0)
    def _():
        keys.start()

    @pl.when(yl == 1)
    def _():
        values.start()

    states = tokens_ref[...].astype(F32)
    sums = jnp.sum(states * states, axis=1, keepdims=True)
    left = jnp.transpose(jnp.broadcast_to(sums, (rows, HEAD)))[:1]
    pieces = three(jnp.concatenate([left[:, :HEAD], left[:, HEAD:]], axis=0))
    for q in range(4):
        gain = gain_ref[q * HEAD : (q + 1) * HEAD].astype(F32).reshape(1, HEAD)
        extra = jnp.concatenate([*pieces, gain, jnp.zeros((9, HEAD), F32)], axis=0)
        block_ref[q // 2, q % 2, rows:] = extra.astype(BF16)
    for copy in tail:
        copy.start()

    @pl.when(yl == 0)
    def _():
        keys.wait()

    @pl.when(yl == 1)
    def _():
        values.wait()

    for copy in (*pads, *body, *tail):
        copy.wait()


def prep(place, tokens, gain, w_query, w_key, w_value):
    vmem = pl.BlockSpec(memory_space=pltpu.VMEM)
    hbm = pl.BlockSpec(memory_space=pltpu.HBM)
    rows = tokens.shape[0] + 16
    depth, cols = w_query.shape
    return pl.pallas_call(
        prep_kernel,
        out_shape=(
            jax.ShapeDtypeStruct((2, 8, 2, rows, HEAD), BF16),
            jax.ShapeDtypeStruct((depth + 64, cols), BF16),
            jax.ShapeDtypeStruct((HEAD, HEAD), BF16),
        ),
        in_specs=[pl.BlockSpec(memory_space=pltpu.SMEM), vmem, vmem, hbm, hbm, hbm],
        out_specs=(hbm, hbm, hbm),
        scratch_shapes=[
            pltpu.VMEM((2, 2, rows, HEAD), BF16),
            pltpu.VMEM((64, cols), BF16),
            pltpu.SemaphoreType.DMA((20,)),
        ],
        compiler_params=pltpu.CompilerParams(vmem_limit_bytes=60 * 1024 * 1024),
    )(place, tokens, gain, w_query, w_key, w_value)


def kv_kernel(parts_ref, w_ref, out_ref, kv_ref, t_ref, sems):
    rows = t_ref.shape[1]
    blocks = parts_ref.shape[1]
    copies = [pltpu.make_async_copy(t_ref.at[xh], out_ref.at[xh], sems.at[xh]) for xh in range(2)]
    for xh in range(2):
        extra = [parts_ref[xh, c, rows:].astype(F32) for c in range(blocks)]
        squares = functools.reduce(jnp.add, extra)
        mean_sq = (squares[4:6] + squares[2:4] + squares[0:2]) / (blocks * 4 * HEAD)
        inverse = lax.rsqrt(mean_sq + EPS)
        inverse = jnp.concatenate(
            [jnp.transpose(jnp.broadcast_to(inverse[i : i + 1], (HEAD, HEAD))) for i in range(2)], axis=0
        )
        total = jnp.zeros((rows, HEAD), F32)
        for c in range(0, blocks, 2):
            for d in (c, c + 1):
                t = parts_ref[xh, d, :rows].astype(F32) * inverse * extra[d][6:7]
                t_ref[xh, :, d * HEAD : (d + 1) * HEAD] = t.astype(BF16)
            w = jnp.concatenate([w_ref[d % 4, d // 4] for d in (c, c + 1)], axis=0)
            total += jnp.dot(t_ref[xh, :, c * HEAD : (c + 2) * HEAD], w, preferred_element_type=F32)
        kv_ref[xh] = total
        copies[xh].start()
    for copy in copies:
        copy.wait()


def project_kv(parts, w, rows):
    vmem = pl.BlockSpec(memory_space=pltpu.VMEM)
    blocks = parts.shape[1]
    return pl.pallas_call(
        kv_kernel,
        out_shape=(
            jax.ShapeDtypeStruct((2, rows, blocks * HEAD), BF16),
            jax.ShapeDtypeStruct((2, rows, HEAD), F32),
        ),
        in_specs=[vmem, vmem],
        out_specs=(pl.BlockSpec(memory_space=pltpu.HBM), vmem),
        scratch_shapes=[pltpu.VMEM((2, rows, blocks * HEAD), BF16), pltpu.SemaphoreType.DMA((2,))],
        compiler_params=pltpu.CompilerParams(vmem_limit_bytes=40 * 1024 * 1024),
        cost_estimate=pl.CostEstimate(flops=2**28, bytes_accessed=5 * 2**20, transcendentals=0),
    )(parts, w)


def q_kernel(place, mine_ref, other_ref, w_ref, out_ref):
    core = place[3]
    rows = mine_ref.shape[1]
    half = mine_ref.shape[2] // w_ref.shape[0]
    for x in range(2):
        total = jnp.zeros((rows, w_ref.shape[2]), F32)
        for c in range(w_ref.shape[0]):
            t = jnp.concatenate([ref[x, :, c * half : (c + 1) * half] for ref in (mine_ref, other_ref)], axis=1)
            w = jnp.concatenate(
                [w_ref[c, pl.ds(pl.multiple_of(at * half, half), half)] for at in (core, 1 - core)], axis=0
            )
            total += jnp.dot(t, w, preferred_element_type=F32)
        out_ref[x] = total


def project_q(place, mine, other, w):
    vmem = pl.BlockSpec(memory_space=pltpu.VMEM)
    return pl.pallas_call(
        q_kernel,
        out_shape=jax.ShapeDtypeStruct((*mine.shape[:2], w.shape[2]), F32),
        in_specs=[pl.BlockSpec(memory_space=pltpu.SMEM), vmem, vmem, vmem],
        out_specs=vmem,
        compiler_params=pltpu.CompilerParams(vmem_limit_bytes=40 * 1024 * 1024),
        cost_estimate=pl.CostEstimate(flops=2**30, bytes_accessed=6 * 2**20, transcendentals=0),
    )(place, mine, other, w)


def on_device(tokens, norm_gain, w_query, w_key, w_value):
    at = lax.axis_index
    place = jnp.stack([at(("zh", "zl")), at("xh"), at("yl"), at("core"), at(("xl", "yh"))]).astype(jnp.int32)
    rows = tokens.shape[0]

    with jax.named_scope("prep"):
        parts, padded, wkv = prep(place, tokens, norm_gain, w_query, w_key, w_value)

    with jax.named_scope("weights"):
        wq = lax.all_gather(padded, ("zh", "zl"), axis=0)
        wkv = lax.all_gather(lax.all_gather(wkv, "zh"), "zl")

    with jax.named_scope("spread"):
        parts = lax.all_to_all(parts.reshape(32, rows + 16, HEAD), ("xh",) + COL, 0, 0)
        parts = parts.reshape(2, 16, rows + 16, HEAD)

    with jax.named_scope("project_kv"):
        whole, kv_sum = project_kv(parts, wkv, rows)
        chunks = lax.all_to_all(kv_sum.reshape(8, rows // 4, HEAD), ("xh", "yl", "core"), 0, 0)
        chunks = jnp.sum(chunks.reshape(2, 2, 2, rows // 4, HEAD), axis=(0, 2)).astype(BF16)
        kv = jnp.concatenate([chunks[0], chunks[1]], axis=1)

    with jax.named_scope("gather_kv"):
        kv, wq = lax.optimization_barrier((lax.all_gather(kv, "zh"), wq))
        kv = gather(kv, "zl", 4)

    with jax.named_scope("project_q"):
        q = project_q(place, whole, swap(whole), wq)
        q = (q + lax.ppermute(q, "xh", [(0, 1), (1, 0)])).astype(BF16)
        pair = lax.ppermute(q, "yl", [(0, 1), (1, 0)])

    with jax.named_scope("attend"):
        swapped = swap(kv)
        out = attend(0, place, q, kv, swapped)
        out = attend(1, place, pair, kv, swapped, out)
        return merge(lax.all_to_all(out, ("xh", "yl"), 0, 0))


def solution(mesh):
    fine = Mesh(mesh.devices.reshape(4, 4, 2, 2, 2, 2, 2), ("zh", "zl", "xh", "xl", "yh", "yl", "core"))
    return jax.shard_map(
        on_device,
        mesh=fine,
        in_specs=(P(ROW, COL), P(COL), P(ROW, COL), P(ROW, None), P(ROW, None)),
        out_specs=P(ROW, COL),
        check_vma=False,
    )
```

```python
import functools
import math

import jax
import jax.numpy as jnp
from jax import lax
from jax.experimental import pallas as pl
from jax.experimental.pallas import tpu as pltpu
from jax.sharding import Mesh
from jax.sharding import PartitionSpec as P

HEAD = 128
GROUP = 8
EPS = 1e-05
ROW = ("zh", "zl", "xh")
COL = ("xl", "yh", "yl", "core")
F32 = jnp.float32
BF16 = jnp.bfloat16


def gather(x, axes, n):
    return lax.all_to_all(jnp.broadcast_to(x[None], (n, *x.shape)), axes, 0, 0)


def swap(x):
    return lax.ppermute(x, "core", [(0, 1), (1, 0)])


def three(x):
    pieces = []
    for _ in range(3):
        piece = x.astype(BF16).astype(F32)
        pieces.append(piece)
        x = x - piece
    return pieces


def attend_kernel(side, place, q_ref, mine_ref, other_ref, *refs):
    out_ref = refs[-1]
    z, xh, yl, core = place[0], place[1], place[2], place[3]
    rows = q_ref.shape[1]
    scale = HEAD**-0.5 * math.log2(math.e)
    chunk = mine_ref.shape[1]
    half = 4 * chunk
    to = yl if side == 0 else 1 - yl
    lane = lax.broadcasted_iota(jnp.int32, (rows, HEAD), 1)

    def block(group):
        return jnp.concatenate(
            [ref[4 * group : 4 * group + 4].reshape(half, 2 * HEAD) for ref in (mine_ref, other_ref)], axis=0
        )

    def run(last, x):
        shape = (rows, 2 * half)
        slot = lax.broadcasted_iota(jnp.int32, shape, 1)
        within = lax.rem(slot, half)
        owner = jnp.where(slot < half, core, 1 - core) + 4 * xh + 2 * yl
        key_pos = lax.div(within, chunk) * (2 * rows) + owner * chunk + lax.rem(within, chunk)
        query_pos = lax.rem(z, 4) * (2 * rows) + x * rows + lax.broadcasted_iota(jnp.int32, shape, 0)
        seen = key_pos <= query_pos
        stats = jnp.zeros((rows, HEAD), F32)
        for head in range(2):
            q = q_ref[x, :, head * HEAD : (head + 1) * HEAD]
            scores = [
                lax.dot_general(q, block(g)[:, :HEAD], (((1,), (1,)), ((), ())), preferred_element_type=F32)
                for g in range(last + 1)
            ]
            scores[last] = jnp.where(seen, scores[last], -1e30)
            pieces = [part[:, j : j + HEAD] for part in scores for j in range(0, 2 * half, HEAD)]
            most = jnp.max(functools.reduce(jnp.maximum, pieces), axis=1, keepdims=True)
            total = jnp.zeros((rows, HEAD), F32)
            acc = jnp.zeros((rows, HEAD), F32)
            for g in range(last + 1):
                weights = []
                for j in range(0, 2 * half, HEAD):
                    w = jnp.exp2((scores[g][:, j : j + HEAD] - most) * scale)
                    total = total + w
                    weights.append(w.astype(BF16))
                p = jnp.concatenate(weights, axis=1)
                acc = acc + jnp.dot(p, block(g)[:, HEAD:], preferred_element_type=F32)
            total = jnp.sum(total, axis=1, keepdims=True)
            stats = jnp.where(lane == head, most * scale + jnp.log2(total), stats)
            out_ref[2 * x + to, :rows, head * HEAD : (head + 1) * HEAD] = (acc / total).astype(BF16)
        sums = three(jnp.transpose(stats)[:2])
        sums = jnp.concatenate([*sums, jnp.zeros((10, rows), F32)], axis=0)
        out_ref[2 * x + to, rows:, :] = sums.astype(BF16)

    for last in range(4):

        @pl.when(lax.div(z, 4) == last)
        def _():
            for x in range(2):
                run(last, x)


def attend(side, place, q, mine, other, *first):
    rows, cols = q.shape[1:]
    vmem = pl.BlockSpec(memory_space=pltpu.VMEM)
    return pl.pallas_call(
        functools.partial(attend_kernel, side),
        out_shape=jax.ShapeDtypeStruct((4, rows + 16, cols), BF16),
        in_specs=[pl.BlockSpec(memory_space=pltpu.SMEM)] + [vmem] * (3 + len(first)),
        out_specs=vmem,
        input_output_aliases={4: 0} if first else {},
        compiler_params=pltpu.CompilerParams(vmem_limit_bytes=40 * 1024 * 1024),
        cost_estimate=pl.CostEstimate(flops=2**30, bytes_accessed=2**22, transcendentals=2**21),
    )(place, q, mine, other, *first)


def merge_kernel(parts_ref, out_ref):
    rows = out_ref.shape[0]
    n = parts_ref.shape[0]
    sums = [parts_ref[i, rows:, :].astype(F32) for i in range(n)]
    sums = [s[0:2] + s[2:4] + s[4:6] for s in sums]
    most = functools.reduce(jnp.maximum, sums)
    shares = [jnp.exp2(s - most) for s in sums]
    total = functools.reduce(jnp.add, shares)
    columns = [jnp.transpose(jnp.concatenate([s / total] * (HEAD // 2), axis=0)) for s in shares]
    for i in range(2):
        at = slice(i * HEAD, (i + 1) * HEAD)
        out_ref[:, at] = sum(columns[k][:, i : i + 1] * parts_ref[k, :rows, at].astype(F32) for k in range(n)).astype(BF16)


def merge(parts):
    vmem = pl.BlockSpec(memory_space=pltpu.VMEM)
    return pl.pallas_call(
        merge_kernel,
        out_shape=jax.ShapeDtypeStruct((parts.shape[1] - 16, parts.shape[2]), BF16),
        in_specs=[vmem],
        out_specs=vmem,
        compiler_params=pltpu.CompilerParams(vmem_limit_bytes=40 * 1024 * 1024),
    )(parts)


def prep_kernel(tokens_ref, gain_ref, w_ref, out_ref, padded_ref, block_ref, sems):
    rows = tokens_ref.shape[0]
    states = tokens_ref[...].astype(F32)
    sums = jnp.sum(states * states, axis=1, keepdims=True)
    left = jnp.transpose(jnp.broadcast_to(sums, (rows, HEAD)))[:1]
    pieces = three(jnp.concatenate([left[:, :HEAD], left[:, HEAD:]], axis=0))
    for q in range(4):
        at = slice(q * HEAD, (q + 1) * HEAD)
        gain = gain_ref[at].astype(F32).reshape(1, HEAD)
        extra = jnp.concatenate([*pieces, gain, jnp.zeros((9, HEAD), F32)], axis=0)
        block_ref[q // 2, q % 2, :rows] = tokens_ref[:, at]
        block_ref[q // 2, q % 2, rows:] = extra.astype(BF16)
    copies = [
        pltpu.make_async_copy(block_ref, out_ref.at[:, to], sems.at[to]) for to in range(out_ref.shape[1])
    ]
    for copy in copies:
        copy.start()
    depth = w_ref.shape[0]
    padded_ref[:depth] = w_ref[...]
    padded_ref[depth:] = jnp.zeros((padded_ref.shape[0] - depth, w_ref.shape[1]), BF16)
    for copy in copies:
        copy.wait()


def prep(tokens, gain, w):
    vmem = pl.BlockSpec(memory_space=pltpu.VMEM)
    rows = tokens.shape[0] + 16
    return pl.pallas_call(
        prep_kernel,
        out_shape=(
            jax.ShapeDtypeStruct((2, 8, 2, rows, HEAD), BF16),
            jax.ShapeDtypeStruct((w.shape[0] + 64, w.shape[1]), BF16),
        ),
        in_specs=[vmem, vmem, vmem],
        out_specs=(pl.BlockSpec(memory_space=pltpu.HBM), vmem),
        scratch_shapes=[pltpu.VMEM((2, 2, rows, HEAD), BF16), pltpu.SemaphoreType.DMA((8,))],
        compiler_params=pltpu.CompilerParams(vmem_limit_bytes=60 * 1024 * 1024),
    )(tokens, gain, w)


def kv_kernel(parts_ref, w_ref, out_ref, kv_ref, t_ref, sems):
    rows = t_ref.shape[1]
    blocks = parts_ref.shape[1]
    copies = [pltpu.make_async_copy(t_ref.at[xh], out_ref.at[xh], sems.at[xh]) for xh in range(2)]
    for xh in range(2):
        extra = [parts_ref[xh, c, rows:].astype(F32) for c in range(blocks)]
        squares = functools.reduce(jnp.add, extra)
        mean_sq = (squares[4:6] + squares[2:4] + squares[0:2]) / (blocks * 4 * HEAD)
        inverse = lax.rsqrt(mean_sq + EPS)
        inverse = jnp.concatenate(
            [jnp.transpose(jnp.broadcast_to(inverse[i : i + 1], (HEAD, HEAD))) for i in range(2)], axis=0
        )
        total = jnp.zeros((rows, HEAD), F32)
        for c in range(0, blocks, 2):
            for d in (c, c + 1):
                t = parts_ref[xh, d, :rows].astype(F32) * inverse * extra[d][6:7]
                t_ref[xh, :, d * HEAD : (d + 1) * HEAD] = t.astype(BF16)
            w = jnp.concatenate([w_ref[d % 4, d // 4] for d in (c, c + 1)], axis=0)
            total += jnp.dot(t_ref[xh, :, c * HEAD : (c + 2) * HEAD], w, preferred_element_type=F32)
        kv_ref[xh] = total
        copies[xh].start()
    for copy in copies:
        copy.wait()


def project_kv(parts, w, rows):
    vmem = pl.BlockSpec(memory_space=pltpu.VMEM)
    blocks = parts.shape[1]
    return pl.pallas_call(
        kv_kernel,
        out_shape=(
            jax.ShapeDtypeStruct((2, rows, blocks * HEAD), BF16),
            jax.ShapeDtypeStruct((2, rows, HEAD), F32),
        ),
        in_specs=[vmem, vmem],
        out_specs=(pl.BlockSpec(memory_space=pltpu.HBM), vmem),
        scratch_shapes=[pltpu.VMEM((2, rows, blocks * HEAD), BF16), pltpu.SemaphoreType.DMA((2,))],
        compiler_params=pltpu.CompilerParams(vmem_limit_bytes=40 * 1024 * 1024),
        cost_estimate=pl.CostEstimate(flops=2**28, bytes_accessed=5 * 2**20, transcendentals=0),
    )(parts, w)


def q_kernel(place, mine_ref, other_ref, w_ref, out_ref):
    core = place[3]
    rows = mine_ref.shape[1]
    half = mine_ref.shape[2] // w_ref.shape[0]
    for x in range(2):
        total = jnp.zeros((rows, w_ref.shape[2]), F32)
        for c in range(w_ref.shape[0]):
            t = jnp.concatenate([ref[x, :, c * half : (c + 1) * half] for ref in (mine_ref, other_ref)], axis=1)
            w = jnp.concatenate(
                [w_ref[c, pl.ds(pl.multiple_of(at * half, half), half)] for at in (core, 1 - core)], axis=0
            )
            total += jnp.dot(t, w, preferred_element_type=F32)
        out_ref[x] = total


def project_q(place, mine, other, w):
    vmem = pl.BlockSpec(memory_space=pltpu.VMEM)
    return pl.pallas_call(
        q_kernel,
        out_shape=jax.ShapeDtypeStruct((*mine.shape[:2], w.shape[2]), F32),
        in_specs=[pl.BlockSpec(memory_space=pltpu.SMEM), vmem, vmem, vmem],
        out_specs=vmem,
        compiler_params=pltpu.CompilerParams(vmem_limit_bytes=40 * 1024 * 1024),
        cost_estimate=pl.CostEstimate(flops=2**30, bytes_accessed=6 * 2**20, transcendentals=0),
    )(place, mine, other, w)


def on_device(tokens, norm_gain, w_query, w_key, w_value):
    at = lax.axis_index
    core = at("core")
    place = jnp.stack([at(("zh", "zl")), at("xh"), at("yl"), core]).astype(jnp.int32)
    rows, feats = tokens.shape
    half = w_key.shape[0] // 2

    with jax.named_scope("prep"):
        parts, padded = prep(tokens, norm_gain, w_query)

    with jax.named_scope("weights"):
        wq = lax.all_gather(padded, ("zh", "zl"), axis=0)
        start = (core * half, at(("xl", "yh")) * HEAD)
        wkv = jnp.where(
            at("yl") == 0,
            lax.dynamic_slice(w_key, start, (half, HEAD)),
            lax.dynamic_slice(w_value, start, (half, HEAD)),
        )
        wkv = lax.all_gather(lax.all_gather(wkv, "zh"), "zl")

    with jax.named_scope("spread"):
        parts = lax.all_to_all(parts.reshape(32, rows + 16, HEAD), ("xh",) + COL, 0, 0)
        parts = parts.reshape(2, 16, rows + 16, HEAD)

    with jax.named_scope("project_kv"):
        whole, kv_sum = project_kv(parts, wkv, rows)
        chunks = lax.all_to_all(kv_sum.reshape(8, rows // 4, HEAD), ("xh", "yl", "core"), 0, 0)
        chunks = jnp.sum(chunks.reshape(2, 2, 2, rows // 4, HEAD), axis=(0, 2)).astype(BF16)
        kv = jnp.concatenate([chunks[0], chunks[1]], axis=1)

    with jax.named_scope("gather_kv"):
        kv = gather(kv, ("zh", "zl"), 16)

    with jax.named_scope("project_q"):
        q = project_q(place, whole, swap(whole), wq)
        q = (q + lax.ppermute(q, "xh", [(0, 1), (1, 0)])).astype(BF16)
        pair = lax.ppermute(q, "yl", [(0, 1), (1, 0)])

    with jax.named_scope("attend"):
        swapped = swap(kv)
        out = attend(0, place, q, kv, swapped)
        out = attend(1, place, pair, kv, swapped, out)
        return merge(lax.all_to_all(out, ("xh", "yl"), 0, 0))


def solution(mesh):
    fine = Mesh(mesh.devices.reshape(4, 4, 2, 2, 2, 2, 2), ("zh", "zl", "xh", "xl", "yh", "yl", "core"))
    return jax.shard_map(
        on_device,
        mesh=fine,
        in_specs=(P(ROW, COL), P(COL), P(ROW, COL), P(ROW, None), P(ROW, None)),
        out_specs=P(ROW, COL),
        check_vma=False,
    )
```

```python
import functools
import math

import jax
import jax.numpy as jnp
from jax import lax
from jax.experimental import pallas as pl
from jax.experimental.pallas import tpu as pltpu
from jax.sharding import Mesh
from jax.sharding import PartitionSpec as P

HEAD = 128
GROUP = 8
EPS = 1e-05
ROW = ("zh", "zl", "xh")
COL = ("xl", "yh", "yl", "core")
F32 = jnp.float32
BF16 = jnp.bfloat16


def gather(x, axes, n):
    return lax.all_to_all(jnp.broadcast_to(x[None], (n, *x.shape)), axes, 0, 0)


def swap(x):
    return lax.ppermute(x, "core", [(0, 1), (1, 0)])


def three(x):
    pieces = []
    for _ in range(3):
        piece = x.astype(BF16).astype(F32)
        pieces.append(piece)
        x = x - piece
    return pieces


def attend_kernel(place, own_ref, pair_ref, mine_ref, other_ref, out_ref):
    z, xh, yl, core = place[0], place[1], place[2], place[3]
    rows = own_ref.shape[1]
    scale = HEAD**-0.5 * math.log2(math.e)
    chunk = mine_ref.shape[1]
    half = 4 * chunk
    lane = lax.broadcasted_iota(jnp.int32, (rows, HEAD), 1)

    def block(group):
        return jnp.concatenate(
            [ref[4 * group : 4 * group + 4].reshape(half, 2 * HEAD) for ref in (mine_ref, other_ref)], axis=0
        )

    def run(last, x):
        shape = (rows, 2 * half)
        slot = lax.broadcasted_iota(jnp.int32, shape, 1)
        within = lax.rem(slot, half)
        owner = jnp.where(slot < half, core, 1 - core) + 4 * xh + 2 * yl
        key_pos = lax.div(within, chunk) * (2 * rows) + owner * chunk + lax.rem(within, chunk)
        query_pos = lax.rem(z, 4) * (2 * rows) + x * rows + lax.broadcasted_iota(jnp.int32, shape, 0)
        seen = key_pos <= query_pos
        for q_ref, to in ((own_ref, yl), (pair_ref, 1 - yl)):
            share(last, x, seen, q_ref, to)

    def share(last, x, seen, q_ref, to):
        stats = jnp.zeros((rows, HEAD), F32)
        for head in range(2):
            q = q_ref[x, :, head * HEAD : (head + 1) * HEAD]
            scores = [
                lax.dot_general(q, block(g)[:, :HEAD], (((1,), (1,)), ((), ())), preferred_element_type=F32)
                for g in range(last + 1)
            ]
            scores[last] = jnp.where(seen, scores[last], -1e30)
            pieces = [part[:, j : j + HEAD] for part in scores for j in range(0, 2 * half, HEAD)]
            most = jnp.max(functools.reduce(jnp.maximum, pieces), axis=1, keepdims=True)
            total = jnp.zeros((rows, HEAD), F32)
            acc = jnp.zeros((rows, HEAD), F32)
            for g in range(last + 1):
                weights = []
                for j in range(0, 2 * half, HEAD):
                    w = jnp.exp2((scores[g][:, j : j + HEAD] - most) * scale)
                    total = total + w
                    weights.append(w.astype(BF16))
                p = jnp.concatenate(weights, axis=1)
                acc = acc + jnp.dot(p, block(g)[:, HEAD:], preferred_element_type=F32)
            total = jnp.sum(total, axis=1, keepdims=True)
            stats = jnp.where(lane == head, most * scale + jnp.log2(total), stats)
            out_ref[2 * x + to, :rows, head * HEAD : (head + 1) * HEAD] = (acc / total).astype(BF16)
        sums = three(jnp.transpose(stats)[:2])
        sums = jnp.concatenate([*sums, jnp.zeros((10, rows), F32)], axis=0)
        out_ref[2 * x + to, rows:, :] = sums.astype(BF16)

    for last in range(4):

        @pl.when(lax.div(z, 4) == last)
        def _():
            for x in range(2):
                run(last, x)


def attend(place, own, pair, mine, other):
    rows, cols = own.shape[1:]
    vmem = pl.BlockSpec(memory_space=pltpu.VMEM)
    return pl.pallas_call(
        attend_kernel,
        out_shape=jax.ShapeDtypeStruct((4, rows + 16, cols), BF16),
        in_specs=[pl.BlockSpec(memory_space=pltpu.SMEM), vmem, vmem, vmem, vmem],
        out_specs=vmem,
        compiler_params=pltpu.CompilerParams(vmem_limit_bytes=40 * 1024 * 1024),
        cost_estimate=pl.CostEstimate(flops=2**31, bytes_accessed=2**22, transcendentals=2**22),
    )(place, own, pair, mine, other)


def merge_kernel(parts_ref, out_ref):
    rows = out_ref.shape[0]
    n = parts_ref.shape[0]
    sums = [parts_ref[i, rows:, :].astype(F32) for i in range(n)]
    sums = [s[0:2] + s[2:4] + s[4:6] for s in sums]
    most = functools.reduce(jnp.maximum, sums)
    shares = [jnp.exp2(s - most) for s in sums]
    total = functools.reduce(jnp.add, shares)
    columns = [jnp.transpose(jnp.concatenate([s / total] * (HEAD // 2), axis=0)) for s in shares]
    for i in range(2):
        at = slice(i * HEAD, (i + 1) * HEAD)
        out_ref[:, at] = sum(columns[k][:, i : i + 1] * parts_ref[k, :rows, at].astype(F32) for k in range(n)).astype(BF16)


def merge(parts):
    vmem = pl.BlockSpec(memory_space=pltpu.VMEM)
    return pl.pallas_call(
        merge_kernel,
        out_shape=jax.ShapeDtypeStruct((parts.shape[1] - 16, parts.shape[2]), BF16),
        in_specs=[vmem],
        out_specs=vmem,
        compiler_params=pltpu.CompilerParams(vmem_limit_bytes=40 * 1024 * 1024),
    )(parts)


def prep_kernel(tokens_ref, gain_ref, w_ref, out_ref, padded_ref, block_ref, sems):
    rows = tokens_ref.shape[0]
    states = tokens_ref[...].astype(F32)
    sums = jnp.sum(states * states, axis=1, keepdims=True)
    left = jnp.transpose(jnp.broadcast_to(sums, (rows, HEAD)))[:1]
    pieces = three(jnp.concatenate([left[:, :HEAD], left[:, HEAD:]], axis=0))
    for q in range(4):
        at = slice(q * HEAD, (q + 1) * HEAD)
        gain = gain_ref[at].astype(F32).reshape(1, HEAD)
        extra = jnp.concatenate([*pieces, gain, jnp.zeros((9, HEAD), F32)], axis=0)
        block_ref[q // 2, q % 2, :rows] = tokens_ref[:, at]
        block_ref[q // 2, q % 2, rows:] = extra.astype(BF16)
    copies = [
        pltpu.make_async_copy(block_ref, out_ref.at[:, to], sems.at[to]) for to in range(out_ref.shape[1])
    ]
    for copy in copies:
        copy.start()
    depth = w_ref.shape[0]
    padded_ref[:depth] = w_ref[...]
    padded_ref[depth:] = jnp.zeros((padded_ref.shape[0] - depth, w_ref.shape[1]), BF16)
    for copy in copies:
        copy.wait()


def prep(tokens, gain, w):
    vmem = pl.BlockSpec(memory_space=pltpu.VMEM)
    rows = tokens.shape[0] + 16
    return pl.pallas_call(
        prep_kernel,
        out_shape=(
            jax.ShapeDtypeStruct((2, 8, 2, rows, HEAD), BF16),
            jax.ShapeDtypeStruct((w.shape[0] + 64, w.shape[1]), BF16),
        ),
        in_specs=[vmem, vmem, vmem],
        out_specs=(pl.BlockSpec(memory_space=pltpu.HBM), vmem),
        scratch_shapes=[pltpu.VMEM((2, 2, rows, HEAD), BF16), pltpu.SemaphoreType.DMA((8,))],
        compiler_params=pltpu.CompilerParams(vmem_limit_bytes=60 * 1024 * 1024),
    )(tokens, gain, w)


def kv_kernel(parts_ref, w_ref, out_ref, kv_ref, t_ref, sems):
    rows = t_ref.shape[1]
    blocks = parts_ref.shape[1]
    copies = [pltpu.make_async_copy(t_ref.at[xh], out_ref.at[xh], sems.at[xh]) for xh in range(2)]
    for xh in range(2):
        extra = [parts_ref[xh, c, rows:].astype(F32) for c in range(blocks)]
        squares = functools.reduce(jnp.add, extra)
        mean_sq = (squares[4:6] + squares[2:4] + squares[0:2]) / (blocks * 4 * HEAD)
        inverse = lax.rsqrt(mean_sq + EPS)
        inverse = jnp.concatenate(
            [jnp.transpose(jnp.broadcast_to(inverse[i : i + 1], (HEAD, HEAD))) for i in range(2)], axis=0
        )
        total = jnp.zeros((rows, HEAD), F32)
        for c in range(0, blocks, 2):
            for d in (c, c + 1):
                t = parts_ref[xh, d, :rows].astype(F32) * inverse * extra[d][6:7]
                t_ref[xh, :, d * HEAD : (d + 1) * HEAD] = t.astype(BF16)
            w = jnp.concatenate([w_ref[d % 4, d // 4] for d in (c, c + 1)], axis=0)
            total += jnp.dot(t_ref[xh, :, c * HEAD : (c + 2) * HEAD], w, preferred_element_type=F32)
        kv_ref[xh] = total
        copies[xh].start()
    for copy in copies:
        copy.wait()


def project_kv(parts, w, rows):
    vmem = pl.BlockSpec(memory_space=pltpu.VMEM)
    blocks = parts.shape[1]
    return pl.pallas_call(
        kv_kernel,
        out_shape=(
            jax.ShapeDtypeStruct((2, rows, blocks * HEAD), BF16),
            jax.ShapeDtypeStruct((2, rows, HEAD), F32),
        ),
        in_specs=[vmem, vmem],
        out_specs=(pl.BlockSpec(memory_space=pltpu.HBM), vmem),
        scratch_shapes=[pltpu.VMEM((2, rows, blocks * HEAD), BF16), pltpu.SemaphoreType.DMA((2,))],
        compiler_params=pltpu.CompilerParams(vmem_limit_bytes=40 * 1024 * 1024),
        cost_estimate=pl.CostEstimate(flops=2**28, bytes_accessed=5 * 2**20, transcendentals=0),
    )(parts, w)


def q_kernel(place, mine_ref, other_ref, w_ref, out_ref):
    core = place[3]
    rows = mine_ref.shape[1]
    half = mine_ref.shape[2] // w_ref.shape[0]
    for x in range(2):
        total = jnp.zeros((rows, w_ref.shape[2]), F32)
        for c in range(w_ref.shape[0]):
            t = jnp.concatenate([ref[x, :, c * half : (c + 1) * half] for ref in (mine_ref, other_ref)], axis=1)
            w = jnp.concatenate(
                [w_ref[c, pl.ds(pl.multiple_of(at * half, half), half)] for at in (core, 1 - core)], axis=0
            )
            total += jnp.dot(t, w, preferred_element_type=F32)
        out_ref[x] = total


def project_q(place, mine, other, w):
    vmem = pl.BlockSpec(memory_space=pltpu.VMEM)
    return pl.pallas_call(
        q_kernel,
        out_shape=jax.ShapeDtypeStruct((*mine.shape[:2], w.shape[2]), F32),
        in_specs=[pl.BlockSpec(memory_space=pltpu.SMEM), vmem, vmem, vmem],
        out_specs=vmem,
        compiler_params=pltpu.CompilerParams(vmem_limit_bytes=40 * 1024 * 1024),
        cost_estimate=pl.CostEstimate(flops=2**30, bytes_accessed=6 * 2**20, transcendentals=0),
    )(place, mine, other, w)


def on_device(tokens, norm_gain, w_query, w_key, w_value):
    at = lax.axis_index
    core = at("core")
    place = jnp.stack([at(("zh", "zl")), at("xh"), at("yl"), core]).astype(jnp.int32)
    rows, feats = tokens.shape
    half = w_key.shape[0] // 2

    with jax.named_scope("prep"):
        parts, padded = prep(tokens, norm_gain, w_query)

    with jax.named_scope("weights"):
        wq = lax.all_gather(padded, ("zh", "zl"), axis=0)
        start = (core * half, at(("xl", "yh")) * HEAD)
        wkv = jnp.where(
            at("yl") == 0,
            lax.dynamic_slice(w_key, start, (half, HEAD)),
            lax.dynamic_slice(w_value, start, (half, HEAD)),
        )
        wkv = lax.all_gather(lax.all_gather(wkv, "zh"), "zl")

    with jax.named_scope("spread"):
        parts = lax.all_to_all(parts.reshape(32, rows + 16, HEAD), ("xh",) + COL, 0, 0)
        parts = parts.reshape(2, 16, rows + 16, HEAD)

    with jax.named_scope("project_kv"):
        whole, kv_sum = project_kv(parts, wkv, rows)
        chunks = lax.all_to_all(kv_sum.reshape(8, rows // 4, HEAD), ("xh", "yl", "core"), 0, 0)
        chunks = jnp.sum(chunks.reshape(2, 2, 2, rows // 4, HEAD), axis=(0, 2)).astype(BF16)
        kv = jnp.concatenate([chunks[0], chunks[1]], axis=1)

    with jax.named_scope("gather_kv"):
        kv = gather(kv, ("zh", "zl"), 16)

    with jax.named_scope("project_q"):
        q = project_q(place, whole, swap(whole), wq)
        q = (q + lax.ppermute(q, "xh", [(0, 1), (1, 0)])).astype(BF16)
        pair = lax.ppermute(q, "yl", [(0, 1), (1, 0)])

    with jax.named_scope("attend"):
        kv, pair = lax.optimization_barrier((kv, pair))
        out = attend(place, q, pair, kv, swap(kv))
        return merge(lax.all_to_all(out, ("xh", "yl"), 0, 0))


def solution(mesh):
    fine = Mesh(mesh.devices.reshape(4, 4, 2, 2, 2, 2, 2), ("zh", "zl", "xh", "xl", "yh", "yl", "core"))
    return jax.shard_map(
        on_device,
        mesh=fine,
        in_specs=(P(ROW, COL), P(COL), P(ROW, COL), P(ROW, None), P(ROW, None)),
        out_specs=P(ROW, COL),
        check_vma=False,
    )
```

```python
import functools
import math

import jax
import jax.numpy as jnp
from jax import lax
from jax.experimental import pallas as pl
from jax.experimental.pallas import tpu as pltpu
from jax.sharding import Mesh
from jax.sharding import PartitionSpec as P

HEAD = 128
GROUP = 8
EPS = 1e-05
ROW = ("zh", "zl", "xh")
COL = ("xl", "yh", "yl", "core")
F32 = jnp.float32
BF16 = jnp.bfloat16


def gather(x, axes, n):
    return lax.all_to_all(jnp.broadcast_to(x[None], (n, *x.shape)), axes, 0, 0)


def swap(x):
    return lax.ppermute(x, "core", [(0, 1), (1, 0)])


def three(x):
    pieces = []
    for _ in range(3):
        piece = x.astype(BF16).astype(F32)
        pieces.append(piece)
        x = x - piece
    return pieces


def attend_kernel(side, place, q_ref, mine_ref, other_ref, *refs):
    out_ref = refs[-1]
    z, xh, yl, core = place[0], place[1], place[2], place[3]
    rows = q_ref.shape[1]
    scale = HEAD**-0.5 * math.log2(math.e)
    chunk = mine_ref.shape[1]
    half = 4 * chunk
    to = yl if side == 0 else 1 - yl
    lane = lax.broadcasted_iota(jnp.int32, (rows, HEAD), 1)

    def block(group):
        return jnp.concatenate(
            [ref[4 * group : 4 * group + 4].reshape(half, 2 * HEAD) for ref in (mine_ref, other_ref)], axis=0
        )

    def run(last, x):
        shape = (rows, 2 * half)
        slot = lax.broadcasted_iota(jnp.int32, shape, 1)
        within = lax.rem(slot, half)
        owner = jnp.where(slot < half, core, 1 - core) + 4 * xh + 2 * yl
        key_pos = lax.div(within, chunk) * (2 * rows) + owner * chunk + lax.rem(within, chunk)
        query_pos = lax.rem(z, 4) * (2 * rows) + x * rows + lax.broadcasted_iota(jnp.int32, shape, 0)
        seen = key_pos <= query_pos
        stats = jnp.zeros((rows, HEAD), F32)
        for head in range(2):
            q = q_ref[x, :, head * HEAD : (head + 1) * HEAD]
            scores = [
                lax.dot_general(q, block(g)[:, :HEAD], (((1,), (1,)), ((), ())), preferred_element_type=F32)
                for g in range(last + 1)
            ]
            scores[last] = jnp.where(seen, scores[last], -1e30)
            pieces = [part[:, j : j + HEAD] for part in scores for j in range(0, 2 * half, HEAD)]
            most = jnp.max(functools.reduce(jnp.maximum, pieces), axis=1, keepdims=True)
            total = jnp.zeros((rows, HEAD), F32)
            acc = jnp.zeros((rows, HEAD), F32)
            for g in range(last + 1):
                weights = []
                for j in range(0, 2 * half, HEAD):
                    w = jnp.exp2((scores[g][:, j : j + HEAD] - most) * scale)
                    total = total + w
                    weights.append(w.astype(BF16))
                p = jnp.concatenate(weights, axis=1)
                acc = acc + jnp.dot(p, block(g)[:, HEAD:], preferred_element_type=F32)
            total = jnp.sum(total, axis=1, keepdims=True)
            stats = jnp.where(lane == head, most * scale + jnp.log2(total), stats)
            out_ref[2 * x + to, :rows, head * HEAD : (head + 1) * HEAD] = (acc / total).astype(BF16)
        sums = three(jnp.transpose(stats)[:2])
        sums = jnp.concatenate([*sums, jnp.zeros((10, rows), F32)], axis=0)
        out_ref[2 * x + to, rows:, :] = sums.astype(BF16)

    for last in range(4):

        @pl.when(lax.div(z, 4) == last)
        def _():
            for x in range(2):
                run(last, x)


def attend(side, place, q, mine, other, *first):
    rows, cols = q.shape[1:]
    vmem = pl.BlockSpec(memory_space=pltpu.VMEM)
    return pl.pallas_call(
        functools.partial(attend_kernel, side),
        out_shape=jax.ShapeDtypeStruct((4, rows + 16, cols), BF16),
        in_specs=[pl.BlockSpec(memory_space=pltpu.SMEM)] + [vmem] * (3 + len(first)),
        out_specs=vmem,
        input_output_aliases={4: 0} if first else {},
        compiler_params=pltpu.CompilerParams(vmem_limit_bytes=40 * 1024 * 1024),
        cost_estimate=pl.CostEstimate(flops=2**30, bytes_accessed=2**22, transcendentals=2**21),
    )(place, q, mine, other, *first)


def merge_kernel(parts_ref, out_ref):
    rows = out_ref.shape[0]
    n = parts_ref.shape[0]
    sums = [parts_ref[i, rows:, :].astype(F32) for i in range(n)]
    sums = [s[0:2] + s[2:4] + s[4:6] for s in sums]
    most = functools.reduce(jnp.maximum, sums)
    shares = [jnp.exp2(s - most) for s in sums]
    total = functools.reduce(jnp.add, shares)
    columns = [jnp.transpose(jnp.concatenate([s / total] * (HEAD // 2), axis=0)) for s in shares]
    for i in range(2):
        at = slice(i * HEAD, (i + 1) * HEAD)
        out_ref[:, at] = sum(columns[k][:, i : i + 1] * parts_ref[k, :rows, at].astype(F32) for k in range(n)).astype(BF16)


def merge(parts):
    vmem = pl.BlockSpec(memory_space=pltpu.VMEM)
    return pl.pallas_call(
        merge_kernel,
        out_shape=jax.ShapeDtypeStruct((parts.shape[1] - 16, parts.shape[2]), BF16),
        in_specs=[vmem],
        out_specs=vmem,
        compiler_params=pltpu.CompilerParams(vmem_limit_bytes=40 * 1024 * 1024),
    )(parts)


def prep_kernel(tokens_ref, gain_ref, w_ref, out_ref, padded_ref, block_ref, sems):
    rows = tokens_ref.shape[0]
    states = tokens_ref[...].astype(F32)
    sums = jnp.sum(states * states, axis=1, keepdims=True)
    left = jnp.transpose(jnp.broadcast_to(sums, (rows, HEAD)))[:1]
    pieces = three(jnp.concatenate([left[:, :HEAD], left[:, HEAD:]], axis=0))
    for q in range(4):
        at = slice(q * HEAD, (q + 1) * HEAD)
        gain = gain_ref[at].astype(F32).reshape(1, HEAD)
        extra = jnp.concatenate([*pieces, gain, jnp.zeros((9, HEAD), F32)], axis=0)
        block_ref[q // 2, q % 2, :rows] = tokens_ref[:, at]
        block_ref[q // 2, q % 2, rows:] = extra.astype(BF16)
    copies = [
        pltpu.make_async_copy(block_ref, out_ref.at[:, to], sems.at[to]) for to in range(out_ref.shape[1])
    ]
    for copy in copies:
        copy.start()
    depth = w_ref.shape[0]
    padded_ref[:depth] = w_ref[...]
    padded_ref[depth:] = jnp.zeros((padded_ref.shape[0] - depth, w_ref.shape[1]), BF16)
    for copy in copies:
        copy.wait()


def prep(tokens, gain, w):
    vmem = pl.BlockSpec(memory_space=pltpu.VMEM)
    rows = tokens.shape[0] + 16
    return pl.pallas_call(
        prep_kernel,
        out_shape=(
            jax.ShapeDtypeStruct((2, 8, 2, rows, HEAD), BF16),
            jax.ShapeDtypeStruct((w.shape[0] + 64, w.shape[1]), BF16),
        ),
        in_specs=[vmem, vmem, vmem],
        out_specs=(pl.BlockSpec(memory_space=pltpu.HBM), vmem),
        scratch_shapes=[pltpu.VMEM((2, 2, rows, HEAD), BF16), pltpu.SemaphoreType.DMA((8,))],
        compiler_params=pltpu.CompilerParams(vmem_limit_bytes=60 * 1024 * 1024),
    )(tokens, gain, w)


def kv_kernel(parts_ref, w_ref, out_ref, kv_ref, t_ref, sems):
    rows = t_ref.shape[1]
    blocks = parts_ref.shape[1]
    copies = [pltpu.make_async_copy(t_ref.at[xh], out_ref.at[xh], sems.at[xh]) for xh in range(2)]
    for xh in range(2):
        extra = [parts_ref[xh, c, rows:].astype(F32) for c in range(blocks)]
        squares = functools.reduce(jnp.add, extra)
        mean_sq = (squares[4:6] + squares[2:4] + squares[0:2]) / (blocks * 4 * HEAD)
        inverse = lax.rsqrt(mean_sq + EPS)
        inverse = jnp.concatenate(
            [jnp.transpose(jnp.broadcast_to(inverse[i : i + 1], (HEAD, HEAD))) for i in range(2)], axis=0
        )
        total = jnp.zeros((rows, HEAD), F32)
        for c in range(0, blocks, 2):
            for d in (c, c + 1):
                t = parts_ref[xh, d, :rows].astype(F32) * inverse * extra[d][6:7]
                t_ref[xh, :, d * HEAD : (d + 1) * HEAD] = t.astype(BF16)
            w = jnp.concatenate([w_ref[d % 4, d // 4] for d in (c, c + 1)], axis=0)
            total += jnp.dot(t_ref[xh, :, c * HEAD : (c + 2) * HEAD], w, preferred_element_type=F32)
        kv_ref[xh] = total
        copies[xh].start()
    for copy in copies:
        copy.wait()


def project_kv(parts, w, rows):
    vmem = pl.BlockSpec(memory_space=pltpu.VMEM)
    blocks = parts.shape[1]
    return pl.pallas_call(
        kv_kernel,
        out_shape=(
            jax.ShapeDtypeStruct((2, rows, blocks * HEAD), BF16),
            jax.ShapeDtypeStruct((2, rows, HEAD), F32),
        ),
        in_specs=[vmem, vmem],
        out_specs=(pl.BlockSpec(memory_space=pltpu.HBM), vmem),
        scratch_shapes=[pltpu.VMEM((2, rows, blocks * HEAD), BF16), pltpu.SemaphoreType.DMA((2,))],
        compiler_params=pltpu.CompilerParams(vmem_limit_bytes=40 * 1024 * 1024),
        cost_estimate=pl.CostEstimate(flops=2**28, bytes_accessed=5 * 2**20, transcendentals=0),
    )(parts, w)


def q_kernel(place, mine_hbm, other_hbm, w_hbm, out_ref, mine_ref, other_ref, w_ref, sems):
    core = place[3]
    blocks, depth = w_ref.shape[:2]
    half = depth // 2
    rows = mine_ref.shape[1]
    step = blocks // 4
    copies = []
    for i in range(4):
        at = pl.ds(i * step, step)
        wide = pl.ds(i * step * half, step * half)
        copies.append(
            [
                pltpu.make_async_copy(mine_hbm.at[:, :, wide], mine_ref.at[:, :, wide], sems.at[3 * i]),
                pltpu.make_async_copy(other_hbm.at[:, :, wide], other_ref.at[:, :, wide], sems.at[3 * i + 1]),
                pltpu.make_async_copy(w_hbm.at[at, :depth], w_ref.at[at], sems.at[3 * i + 2]),
            ]
        )
    for group in copies:
        for copy in group:
            copy.start()
    totals = [jnp.zeros((rows, w_ref.shape[2]), F32) for _ in range(2)]
    for i in range(4):
        for copy in copies[i]:
            copy.wait()
        for c in range(i * step, (i + 1) * step):
            w = jnp.concatenate(
                [w_ref[c, pl.ds(pl.multiple_of(at * half, half), half)] for at in (core, 1 - core)], axis=0
            )
            for x in range(2):
                t = jnp.concatenate([ref[x, :, c * half : (c + 1) * half] for ref in (mine_ref, other_ref)], axis=1)
                totals[x] += jnp.dot(t, w, preferred_element_type=F32)
    for x in range(2):
        out_ref[x] = totals[x]


def project_q(place, mine, other, w):
    vmem = pl.BlockSpec(memory_space=pltpu.VMEM)
    hbm = pl.BlockSpec(memory_space=pltpu.HBM)
    return pl.pallas_call(
        q_kernel,
        out_shape=jax.ShapeDtypeStruct((*mine.shape[:2], w.shape[2]), F32),
        in_specs=[pl.BlockSpec(memory_space=pltpu.SMEM), hbm, hbm, hbm],
        out_specs=vmem,
        scratch_shapes=[
            pltpu.VMEM(mine.shape, BF16),
            pltpu.VMEM(other.shape, BF16),
            pltpu.VMEM((w.shape[0], w.shape[1] - 64, w.shape[2]), BF16),
            pltpu.SemaphoreType.DMA((12,)),
        ],
        compiler_params=pltpu.CompilerParams(vmem_limit_bytes=57 * 1024 * 1024),
        cost_estimate=pl.CostEstimate(flops=2**30, bytes_accessed=6 * 2**20, transcendentals=0),
    )(place, mine, other, w)


def on_device(tokens, norm_gain, w_query, w_key, w_value):
    at = lax.axis_index
    core = at("core")
    place = jnp.stack([at(("zh", "zl")), at("xh"), at("yl"), core]).astype(jnp.int32)
    rows, feats = tokens.shape
    half = w_key.shape[0] // 2

    with jax.named_scope("prep"):
        parts, padded = prep(tokens, norm_gain, w_query)

    with jax.named_scope("weights"):
        wq = lax.all_gather(padded, ("zh", "zl"), axis=0)
        start = (core * half, at(("xl", "yh")) * HEAD)
        wkv = jnp.where(
            at("yl") == 0,
            lax.dynamic_slice(w_key, start, (half, HEAD)),
            lax.dynamic_slice(w_value, start, (half, HEAD)),
        )
        wkv = lax.all_gather(lax.all_gather(wkv, "zh"), "zl")

    with jax.named_scope("spread"):
        parts = lax.all_to_all(parts.reshape(32, rows + 16, HEAD), ("xh",) + COL, 0, 0)
        parts = parts.reshape(2, 16, rows + 16, HEAD)

    with jax.named_scope("project_kv"):
        whole, kv_sum = project_kv(parts, wkv, rows)
        chunks = lax.all_to_all(kv_sum.reshape(8, rows // 4, HEAD), ("xh", "yl", "core"), 0, 0)
        chunks = jnp.sum(chunks.reshape(2, 2, 2, rows // 4, HEAD), axis=(0, 2)).astype(BF16)
        kv = jnp.concatenate([chunks[0], chunks[1]], axis=1)

    with jax.named_scope("gather_kv"):
        kv = gather(kv, ("zh", "zl"), 16)

    with jax.named_scope("project_q"):
        q = project_q(place, whole, swap(whole), wq)
        q = (q + lax.ppermute(q, "xh", [(0, 1), (1, 0)])).astype(BF16)
        pair = lax.ppermute(q, "yl", [(0, 1), (1, 0)])

    with jax.named_scope("attend"):
        kv, q = lax.optimization_barrier((kv, q))
        swapped = swap(kv)
        out = attend(0, place, q, kv, swapped)
        out = attend(1, place, pair, kv, swapped, out)
        return merge(lax.all_to_all(out, ("xh", "yl"), 0, 0))


def solution(mesh):
    fine = Mesh(mesh.devices.reshape(4, 4, 2, 2, 2, 2, 2), ("zh", "zl", "xh", "xl", "yh", "yl", "core"))
    return jax.shard_map(
        on_device,
        mesh=fine,
        in_specs=(P(ROW, COL), P(COL), P(ROW, COL), P(ROW, None), P(ROW, None)),
        out_specs=P(ROW, COL),
        check_vma=False,
    )
```

```python
import functools
import math

import jax
import jax.numpy as jnp
from jax import lax
from jax.experimental import pallas as pl
from jax.experimental.pallas import tpu as pltpu
from jax.sharding import Mesh
from jax.sharding import PartitionSpec as P

HEAD = 128
GROUP = 8
EPS = 1e-05
ROW = ("zh", "zl", "xh")
COL = ("xl", "yh", "yl", "core")
F32 = jnp.float32
BF16 = jnp.bfloat16


def gather(x, axes, n):
    return lax.all_to_all(jnp.broadcast_to(x[None], (n, *x.shape)), axes, 0, 0)


def swap(x):
    return lax.ppermute(x, "core", [(0, 1), (1, 0)])


def three(x):
    pieces = []
    for _ in range(3):
        piece = x.astype(BF16).astype(F32)
        pieces.append(piece)
        x = x - piece
    return pieces


def attend_kernel(side, place, q_ref, mine_ref, other_ref, *refs):
    out_ref = refs[-1]
    z, xh, yl, core = place[0], place[1], place[2], place[3]
    rows = q_ref.shape[1]
    scale = HEAD**-0.5 * math.log2(math.e)
    chunk = mine_ref.shape[2]
    half = 4 * chunk
    to = yl if side == 0 else 1 - yl
    lane = lax.broadcasted_iota(jnp.int32, (rows, HEAD), 1)

    def block(group):
        return jnp.concatenate(
            [ref[:, group].reshape(half, 2 * HEAD) for ref in (mine_ref, other_ref)], axis=0
        )

    def run(last, x):
        shape = (rows, 2 * half)
        slot = lax.broadcasted_iota(jnp.int32, shape, 1)
        within = lax.rem(slot, half)
        owner = jnp.where(slot < half, core, 1 - core) + 4 * xh + 2 * yl
        key_pos = lax.div(within, chunk) * (2 * rows) + owner * chunk + lax.rem(within, chunk)
        query_pos = lax.rem(z, 4) * (2 * rows) + x * rows + lax.broadcasted_iota(jnp.int32, shape, 0)
        seen = key_pos <= query_pos
        stats = jnp.zeros((rows, HEAD), F32)
        for head in range(2):
            q = q_ref[x, :, head * HEAD : (head + 1) * HEAD]
            scores = [
                lax.dot_general(q, block(g)[:, :HEAD], (((1,), (1,)), ((), ())), preferred_element_type=F32)
                for g in range(last + 1)
            ]
            scores[last] = jnp.where(seen, scores[last], -1e30)
            pieces = [part[:, j : j + HEAD] for part in scores for j in range(0, 2 * half, HEAD)]
            most = jnp.max(functools.reduce(jnp.maximum, pieces), axis=1, keepdims=True)
            total = jnp.zeros((rows, HEAD), F32)
            acc = jnp.zeros((rows, HEAD), F32)
            for g in range(last + 1):
                weights = []
                for j in range(0, 2 * half, HEAD):
                    w = jnp.exp2((scores[g][:, j : j + HEAD] - most) * scale)
                    total = total + w
                    weights.append(w.astype(BF16))
                p = jnp.concatenate(weights, axis=1)
                acc = acc + jnp.dot(p, block(g)[:, HEAD:], preferred_element_type=F32)
            total = jnp.sum(total, axis=1, keepdims=True)
            stats = jnp.where(lane == head, most * scale + jnp.log2(total), stats)
            out_ref[2 * x + to, :rows, head * HEAD : (head + 1) * HEAD] = (acc / total).astype(BF16)
        sums = three(jnp.transpose(stats)[:2])
        sums = jnp.concatenate([*sums, jnp.zeros((10, rows), F32)], axis=0)
        out_ref[2 * x + to, rows:, :] = sums.astype(BF16)

    for last in range(4):

        @pl.when(lax.div(z, 4) == last)
        def _():
            for x in range(2):
                run(last, x)


def attend(side, place, q, mine, other, *first):
    rows, cols = q.shape[1:]
    vmem = pl.BlockSpec(memory_space=pltpu.VMEM)
    return pl.pallas_call(
        functools.partial(attend_kernel, side),
        out_shape=jax.ShapeDtypeStruct((4, rows + 16, cols), BF16),
        in_specs=[pl.BlockSpec(memory_space=pltpu.SMEM)] + [vmem] * (3 + len(first)),
        out_specs=vmem,
        input_output_aliases={4: 0} if first else {},
        compiler_params=pltpu.CompilerParams(vmem_limit_bytes=40 * 1024 * 1024),
        cost_estimate=pl.CostEstimate(flops=2**30, bytes_accessed=2**22, transcendentals=2**21),
    )(place, q, mine, other, *first)


def merge_kernel(parts_ref, out_ref):
    rows = out_ref.shape[0]
    n = parts_ref.shape[0]
    sums = [parts_ref[i, rows:, :].astype(F32) for i in range(n)]
    sums = [s[0:2] + s[2:4] + s[4:6] for s in sums]
    most = functools.reduce(jnp.maximum, sums)
    shares = [jnp.exp2(s - most) for s in sums]
    total = functools.reduce(jnp.add, shares)
    columns = [jnp.transpose(jnp.concatenate([s / total] * (HEAD // 2), axis=0)) for s in shares]
    for i in range(2):
        at = slice(i * HEAD, (i + 1) * HEAD)
        out_ref[:, at] = sum(columns[k][:, i : i + 1] * parts_ref[k, :rows, at].astype(F32) for k in range(n)).astype(BF16)


def merge(parts):
    vmem = pl.BlockSpec(memory_space=pltpu.VMEM)
    return pl.pallas_call(
        merge_kernel,
        out_shape=jax.ShapeDtypeStruct((parts.shape[1] - 16, parts.shape[2]), BF16),
        in_specs=[vmem],
        out_specs=vmem,
        compiler_params=pltpu.CompilerParams(vmem_limit_bytes=40 * 1024 * 1024),
    )(parts)


def prep_kernel(tokens_ref, gain_ref, w_ref, out_ref, padded_ref, block_ref, sems):
    rows = tokens_ref.shape[0]
    states = tokens_ref[...].astype(F32)
    sums = jnp.sum(states * states, axis=1, keepdims=True)
    left = jnp.transpose(jnp.broadcast_to(sums, (rows, HEAD)))[:1]
    pieces = three(jnp.concatenate([left[:, :HEAD], left[:, HEAD:]], axis=0))
    for q in range(4):
        at = slice(q * HEAD, (q + 1) * HEAD)
        gain = gain_ref[at].astype(F32).reshape(1, HEAD)
        extra = jnp.concatenate([*pieces, gain, jnp.zeros((9, HEAD), F32)], axis=0)
        block_ref[q // 2, q % 2, :rows] = tokens_ref[:, at]
        block_ref[q // 2, q % 2, rows:] = extra.astype(BF16)
    copies = [
        pltpu.make_async_copy(block_ref, out_ref.at[:, to], sems.at[to]) for to in range(out_ref.shape[1])
    ]
    for copy in copies:
        copy.start()
    depth = w_ref.shape[0]
    padded_ref[:depth] = w_ref[...]
    padded_ref[depth:] = jnp.zeros((padded_ref.shape[0] - depth, w_ref.shape[1]), BF16)
    for copy in copies:
        copy.wait()


def prep(tokens, gain, w):
    vmem = pl.BlockSpec(memory_space=pltpu.VMEM)
    rows = tokens.shape[0] + 16
    return pl.pallas_call(
        prep_kernel,
        out_shape=(
            jax.ShapeDtypeStruct((2, 8, 2, rows, HEAD), BF16),
            jax.ShapeDtypeStruct((w.shape[0] + 64, w.shape[1]), BF16),
        ),
        in_specs=[vmem, vmem, vmem],
        out_specs=(pl.BlockSpec(memory_space=pltpu.HBM), vmem),
        scratch_shapes=[pltpu.VMEM((2, 2, rows, HEAD), BF16), pltpu.SemaphoreType.DMA((8,))],
        compiler_params=pltpu.CompilerParams(vmem_limit_bytes=60 * 1024 * 1024),
    )(tokens, gain, w)


def kv_kernel(parts_ref, w_ref, out_ref, kv_ref, t_ref, sems):
    rows = t_ref.shape[1]
    blocks = parts_ref.shape[1]
    copies = [pltpu.make_async_copy(t_ref.at[xh], out_ref.at[xh], sems.at[xh]) for xh in range(2)]
    for xh in range(2):
        extra = [parts_ref[xh, c, rows:].astype(F32) for c in range(blocks)]
        squares = functools.reduce(jnp.add, extra)
        mean_sq = (squares[4:6] + squares[2:4] + squares[0:2]) / (blocks * 4 * HEAD)
        inverse = lax.rsqrt(mean_sq + EPS)
        inverse = jnp.concatenate(
            [jnp.transpose(jnp.broadcast_to(inverse[i : i + 1], (HEAD, HEAD))) for i in range(2)], axis=0
        )
        total = jnp.zeros((rows, HEAD), F32)
        for c in range(0, blocks, 2):
            for d in (c, c + 1):
                t = parts_ref[xh, d, :rows].astype(F32) * inverse * extra[d][6:7]
                t_ref[xh, :, d * HEAD : (d + 1) * HEAD] = t.astype(BF16)
            w = jnp.concatenate([w_ref[d % 4, d // 4] for d in (c, c + 1)], axis=0)
            total += jnp.dot(t_ref[xh, :, c * HEAD : (c + 2) * HEAD], w, preferred_element_type=F32)
        kv_ref[xh] = total
        copies[xh].start()
    for copy in copies:
        copy.wait()


def project_kv(parts, w, rows):
    vmem = pl.BlockSpec(memory_space=pltpu.VMEM)
    blocks = parts.shape[1]
    return pl.pallas_call(
        kv_kernel,
        out_shape=(
            jax.ShapeDtypeStruct((2, rows, blocks * HEAD), BF16),
            jax.ShapeDtypeStruct((2, rows, HEAD), F32),
        ),
        in_specs=[vmem, vmem],
        out_specs=(pl.BlockSpec(memory_space=pltpu.HBM), vmem),
        scratch_shapes=[pltpu.VMEM((2, rows, blocks * HEAD), BF16), pltpu.SemaphoreType.DMA((2,))],
        compiler_params=pltpu.CompilerParams(vmem_limit_bytes=40 * 1024 * 1024),
        cost_estimate=pl.CostEstimate(flops=2**28, bytes_accessed=5 * 2**20, transcendentals=0),
    )(parts, w)


def q_kernel(place, mine_ref, other_ref, w_ref, out_ref):
    core = place[3]
    rows = mine_ref.shape[1]
    half = mine_ref.shape[2] // w_ref.shape[0]
    for x in range(2):
        total = jnp.zeros((rows, w_ref.shape[2]), F32)
        for c in range(w_ref.shape[0]):
            t = jnp.concatenate([ref[x, :, c * half : (c + 1) * half] for ref in (mine_ref, other_ref)], axis=1)
            w = jnp.concatenate(
                [w_ref[c, pl.ds(pl.multiple_of(at * half, half), half)] for at in (core, 1 - core)], axis=0
            )
            total += jnp.dot(t, w, preferred_element_type=F32)
        out_ref[x] = total


def project_q(place, mine, other, w):
    vmem = pl.BlockSpec(memory_space=pltpu.VMEM)
    return pl.pallas_call(
        q_kernel,
        out_shape=jax.ShapeDtypeStruct((*mine.shape[:2], w.shape[2]), F32),
        in_specs=[pl.BlockSpec(memory_space=pltpu.SMEM), vmem, vmem, vmem],
        out_specs=vmem,
        compiler_params=pltpu.CompilerParams(vmem_limit_bytes=40 * 1024 * 1024),
        cost_estimate=pl.CostEstimate(flops=2**30, bytes_accessed=6 * 2**20, transcendentals=0),
    )(place, mine, other, w)


def on_device(tokens, norm_gain, w_query, w_key, w_value):
    at = lax.axis_index
    core = at("core")
    place = jnp.stack([at(("zh", "zl")), at("xh"), at("yl"), core]).astype(jnp.int32)
    rows, feats = tokens.shape
    half = w_key.shape[0] // 2

    with jax.named_scope("prep"):
        parts, padded = prep(tokens, norm_gain, w_query)

    with jax.named_scope("weights"):
        wq = lax.all_gather(padded, ("zh", "zl"), axis=0)
        start = (core * half, at(("xl", "yh")) * HEAD)
        wkv = jnp.where(
            at("yl") == 0,
            lax.dynamic_slice(w_key, start, (half, HEAD)),
            lax.dynamic_slice(w_value, start, (half, HEAD)),
        )
        wkv = lax.all_gather(lax.all_gather(wkv, "zh"), "zl")

    with jax.named_scope("spread"):
        parts = lax.all_to_all(parts.reshape(32, rows + 16, HEAD), ("xh",) + COL, 0, 0)
        parts = parts.reshape(2, 16, rows + 16, HEAD)

    with jax.named_scope("project_kv"):
        whole, kv_sum = project_kv(parts, wkv, rows)
        chunks = lax.all_to_all(kv_sum.reshape(8, rows // 4, HEAD), ("xh", "yl", "core"), 0, 0)
        chunks = jnp.sum(chunks.reshape(2, 2, 2, rows // 4, HEAD), axis=(0, 2)).astype(BF16)
        kv = jnp.concatenate([chunks[0], chunks[1]], axis=1)

    with jax.named_scope("gather_kv"):
        kv, wq = lax.optimization_barrier((lax.all_gather(kv, "zh"), wq))
        kv = gather(kv, "zl", 4)

    with jax.named_scope("project_q"):
        q = project_q(place, whole, swap(whole), wq)
        q = (q + lax.ppermute(q, "xh", [(0, 1), (1, 0)])).astype(BF16)
        pair = lax.ppermute(q, "yl", [(0, 1), (1, 0)])

    with jax.named_scope("attend"):
        swapped = swap(kv)
        out = attend(0, place, q, kv, swapped)
        out = attend(1, place, pair, kv, swapped, out)
        return merge(lax.all_to_all(out, ("xh", "yl"), 0, 0))


def solution(mesh):
    fine = Mesh(mesh.devices.reshape(4, 4, 2, 2, 2, 2, 2), ("zh", "zl", "xh", "xl", "yh", "yl", "core"))
    return jax.shard_map(
        on_device,
        mesh=fine,
        in_specs=(P(ROW, COL), P(COL), P(ROW, COL), P(ROW, None), P(ROW, None)),
        out_specs=P(ROW, COL),
        check_vma=False,
    )
```

```python
import functools
import math

import jax
import jax.numpy as jnp
from jax import lax
from jax.experimental import pallas as pl
from jax.experimental.pallas import tpu as pltpu
from jax.sharding import Mesh
from jax.sharding import PartitionSpec as P

HEAD = 128
GROUP = 8
EPS = 1e-05
ROW = ("zh", "zl", "xh")
COL = ("xl", "yh", "yl", "core")
F32 = jnp.float32
BF16 = jnp.bfloat16


def gather(x, axes, n):
    return lax.all_to_all(jnp.broadcast_to(x[None], (n, *x.shape)), axes, 0, 0)


def swap(x):
    return lax.ppermute(x, "core", [(0, 1), (1, 0)])


def three(x):
    pieces = []
    for _ in range(3):
        piece = x.astype(BF16).astype(F32)
        pieces.append(piece)
        x = x - piece
    return pieces


def attend_kernel(side, place, q_ref, mine_ref, other_ref, *refs):
    out_ref = refs[-1]
    z, xh, yl, core = place[0], place[1], place[2], place[3]
    rows = q_ref.shape[1]
    scale = HEAD**-0.5 * math.log2(math.e)
    chunk = mine_ref.shape[2]
    half = 4 * chunk
    to = yl if side == 0 else 1 - yl
    lane = lax.broadcasted_iota(jnp.int32, (rows, HEAD), 1)

    def block(group):
        return jnp.concatenate(
            [ref[:, group].reshape(half, 2 * HEAD) for ref in (mine_ref, other_ref)], axis=0
        )

    def run(last, x):
        shape = (rows, 2 * half)
        slot = lax.broadcasted_iota(jnp.int32, shape, 1)
        within = lax.rem(slot, half)
        owner = jnp.where(slot < half, core, 1 - core) + 4 * xh + 2 * yl
        key_pos = lax.div(within, chunk) * (2 * rows) + owner * chunk + lax.rem(within, chunk)
        query_pos = lax.rem(z, 4) * (2 * rows) + x * rows + lax.broadcasted_iota(jnp.int32, shape, 0)
        seen = key_pos <= query_pos
        stats = jnp.zeros((rows, HEAD), F32)
        for head in range(2):
            q = q_ref[x, :, head * HEAD : (head + 1) * HEAD]
            scores = [
                lax.dot_general(q, block(g)[:, :HEAD], (((1,), (1,)), ((), ())), preferred_element_type=F32)
                for g in range(last + 1)
            ]
            scores[last] = jnp.where(seen, scores[last], -1e30)
            pieces = [part[:, j : j + HEAD] for part in scores for j in range(0, 2 * half, HEAD)]
            most = jnp.max(functools.reduce(jnp.maximum, pieces), axis=1, keepdims=True)
            total = jnp.zeros((rows, HEAD), F32)
            acc = jnp.zeros((rows, HEAD), F32)
            for g in range(last + 1):
                weights = []
                for j in range(0, 2 * half, HEAD):
                    w = jnp.exp2((scores[g][:, j : j + HEAD] - most) * scale)
                    total = total + w
                    weights.append(w.astype(BF16))
                p = jnp.concatenate(weights, axis=1)
                acc = acc + jnp.dot(p, block(g)[:, HEAD:], preferred_element_type=F32)
            total = jnp.sum(total, axis=1, keepdims=True)
            stats = jnp.where(lane == head, most * scale + jnp.log2(total), stats)
            out_ref[2 * x + to, :rows, head * HEAD : (head + 1) * HEAD] = (acc / total).astype(BF16)
        sums = three(jnp.transpose(stats)[:2])
        sums = jnp.concatenate([*sums, jnp.zeros((10, rows), F32)], axis=0)
        out_ref[2 * x + to, rows:, :] = sums.astype(BF16)

    for last in range(4):

        @pl.when(lax.div(z, 4) == last)
        def _():
            for x in range(2):
                run(last, x)


def attend(side, place, q, mine, other, *first):
    rows, cols = q.shape[1:]
    vmem = pl.BlockSpec(memory_space=pltpu.VMEM)
    return pl.pallas_call(
        functools.partial(attend_kernel, side),
        out_shape=jax.ShapeDtypeStruct((4, rows + 16, cols), BF16),
        in_specs=[pl.BlockSpec(memory_space=pltpu.SMEM)] + [vmem] * (3 + len(first)),
        out_specs=vmem,
        input_output_aliases={4: 0} if first else {},
        compiler_params=pltpu.CompilerParams(vmem_limit_bytes=40 * 1024 * 1024),
        cost_estimate=pl.CostEstimate(flops=2**30, bytes_accessed=2**22, transcendentals=2**21),
    )(place, q, mine, other, *first)


def merge_kernel(parts_ref, out_ref):
    rows = out_ref.shape[0]
    n = parts_ref.shape[0]
    sums = [parts_ref[i, rows:, :].astype(F32) for i in range(n)]
    sums = [s[0:2] + s[2:4] + s[4:6] for s in sums]
    most = functools.reduce(jnp.maximum, sums)
    shares = [jnp.exp2(s - most) for s in sums]
    total = functools.reduce(jnp.add, shares)
    columns = [jnp.transpose(jnp.concatenate([s / total] * (HEAD // 2), axis=0)) for s in shares]
    for i in range(2):
        at = slice(i * HEAD, (i + 1) * HEAD)
        out_ref[:, at] = sum(columns[k][:, i : i + 1] * parts_ref[k, :rows, at].astype(F32) for k in range(n)).astype(BF16)


def merge(parts):
    vmem = pl.BlockSpec(memory_space=pltpu.VMEM)
    return pl.pallas_call(
        merge_kernel,
        out_shape=jax.ShapeDtypeStruct((parts.shape[1] - 16, parts.shape[2]), BF16),
        in_specs=[vmem],
        out_specs=vmem,
        compiler_params=pltpu.CompilerParams(vmem_limit_bytes=40 * 1024 * 1024),
    )(parts)


def prep_kernel(tokens_ref, gain_ref, w_ref, out_ref, padded_ref, block_ref, sems):
    rows = tokens_ref.shape[0]
    states = tokens_ref[...].astype(F32)
    sums = jnp.sum(states * states, axis=1, keepdims=True)
    left = jnp.transpose(jnp.broadcast_to(sums, (rows, HEAD)))[:1]
    pieces = three(jnp.concatenate([left[:, :HEAD], left[:, HEAD:]], axis=0))
    for q in range(4):
        at = slice(q * HEAD, (q + 1) * HEAD)
        gain = gain_ref[at].astype(F32).reshape(1, HEAD)
        extra = jnp.concatenate([*pieces, gain, jnp.zeros((9, HEAD), F32)], axis=0)
        block_ref[q // 2, q % 2, :rows] = tokens_ref[:, at]
        block_ref[q // 2, q % 2, rows:] = extra.astype(BF16)
    copies = [
        pltpu.make_async_copy(block_ref, out_ref.at[:, to], sems.at[to]) for to in range(out_ref.shape[1])
    ]
    for copy in copies:
        copy.start()
    depth = w_ref.shape[0]
    padded_ref[:depth] = w_ref[...]
    padded_ref[depth:] = jnp.zeros((padded_ref.shape[0] - depth, w_ref.shape[1]), BF16)
    for copy in copies:
        copy.wait()


def prep(tokens, gain, w):
    vmem = pl.BlockSpec(memory_space=pltpu.VMEM)
    rows = tokens.shape[0] + 16
    return pl.pallas_call(
        prep_kernel,
        out_shape=(
            jax.ShapeDtypeStruct((2, 8, 2, rows, HEAD), BF16),
            jax.ShapeDtypeStruct((w.shape[0] + 64, w.shape[1]), BF16),
        ),
        in_specs=[vmem, vmem, vmem],
        out_specs=(pl.BlockSpec(memory_space=pltpu.HBM), vmem),
        scratch_shapes=[pltpu.VMEM((2, 2, rows, HEAD), BF16), pltpu.SemaphoreType.DMA((8,))],
        compiler_params=pltpu.CompilerParams(vmem_limit_bytes=60 * 1024 * 1024),
    )(tokens, gain, w)


def kv_kernel(parts_ref, w_ref, out_ref, kv_ref, t_ref, sems):
    rows = t_ref.shape[1]
    blocks = parts_ref.shape[1]
    copies = [pltpu.make_async_copy(t_ref.at[xh], out_ref.at[xh], sems.at[xh]) for xh in range(2)]
    for xh in range(2):
        extra = [parts_ref[xh, c, rows:].astype(F32) for c in range(blocks)]
        squares = functools.reduce(jnp.add, extra)
        mean_sq = (squares[4:6] + squares[2:4] + squares[0:2]) / (blocks * 4 * HEAD)
        inverse = lax.rsqrt(mean_sq + EPS)
        inverse = jnp.concatenate(
            [jnp.transpose(jnp.broadcast_to(inverse[i : i + 1], (HEAD, HEAD))) for i in range(2)], axis=0
        )
        total = jnp.zeros((rows, HEAD), F32)
        for c in range(0, blocks, 2):
            for d in (c, c + 1):
                t = parts_ref[xh, d, :rows].astype(F32) * inverse * extra[d][6:7]
                t_ref[xh, :, d * HEAD : (d + 1) * HEAD] = t.astype(BF16)
            w = jnp.concatenate([w_ref[d % 4, d // 4] for d in (c, c + 1)], axis=0)
            total += jnp.dot(t_ref[xh, :, c * HEAD : (c + 2) * HEAD], w, preferred_element_type=F32)
        kv_ref[xh] = total
        copies[xh].start()
    for copy in copies:
        copy.wait()


def project_kv(parts, w, rows):
    vmem = pl.BlockSpec(memory_space=pltpu.VMEM)
    blocks = parts.shape[1]
    return pl.pallas_call(
        kv_kernel,
        out_shape=(
            jax.ShapeDtypeStruct((2, rows, blocks * HEAD), BF16),
            jax.ShapeDtypeStruct((2, rows, HEAD), F32),
        ),
        in_specs=[vmem, vmem],
        out_specs=(pl.BlockSpec(memory_space=pltpu.HBM), vmem),
        scratch_shapes=[pltpu.VMEM((2, rows, blocks * HEAD), BF16), pltpu.SemaphoreType.DMA((2,))],
        compiler_params=pltpu.CompilerParams(vmem_limit_bytes=40 * 1024 * 1024),
        cost_estimate=pl.CostEstimate(flops=2**28, bytes_accessed=5 * 2**20, transcendentals=0),
    )(parts, w)


def q_kernel(place, mine_ref, other_ref, w_ref, out_ref):
    core = place[3]
    rows = mine_ref.shape[1]
    half = mine_ref.shape[2] // w_ref.shape[0]
    for x in range(2):
        total = jnp.zeros((rows, w_ref.shape[2]), F32)
        for c in range(w_ref.shape[0]):
            t = jnp.concatenate([ref[x, :, c * half : (c + 1) * half] for ref in (mine_ref, other_ref)], axis=1)
            w = jnp.concatenate(
                [w_ref[c, pl.ds(pl.multiple_of(at * half, half), half)] for at in (core, 1 - core)], axis=0
            )
            total += jnp.dot(t, w, preferred_element_type=F32)
        out_ref[x] = total


def project_q(place, mine, other, w):
    vmem = pl.BlockSpec(memory_space=pltpu.VMEM)
    return pl.pallas_call(
        q_kernel,
        out_shape=jax.ShapeDtypeStruct((*mine.shape[:2], w.shape[2]), F32),
        in_specs=[pl.BlockSpec(memory_space=pltpu.SMEM), vmem, vmem, vmem],
        out_specs=vmem,
        compiler_params=pltpu.CompilerParams(vmem_limit_bytes=40 * 1024 * 1024),
        cost_estimate=pl.CostEstimate(flops=2**30, bytes_accessed=6 * 2**20, transcendentals=0),
    )(place, mine, other, w)


def on_device(tokens, norm_gain, w_query, w_key, w_value):
    at = lax.axis_index
    core = at("core")
    place = jnp.stack([at(("zh", "zl")), at("xh"), at("yl"), core]).astype(jnp.int32)
    rows, feats = tokens.shape
    half = w_key.shape[0] // 2

    with jax.named_scope("prep"):
        parts, padded = prep(tokens, norm_gain, w_query)

    with jax.named_scope("weights"):
        wq = lax.all_gather(padded, ("zh", "zl"), axis=0)
        start = (core * half, at(("xl", "yh")) * HEAD)
        wkv = jnp.where(
            at("yl") == 0,
            lax.dynamic_slice(w_key, start, (half, HEAD)),
            lax.dynamic_slice(w_value, start, (half, HEAD)),
        )
        wkv = lax.all_gather(lax.all_gather(wkv, "zh"), "zl")

    with jax.named_scope("spread"):
        parts = lax.all_to_all(parts.reshape(32, rows + 16, HEAD), ("xh",) + COL, 0, 0)
        parts = parts.reshape(2, 16, rows + 16, HEAD)

    with jax.named_scope("project_kv"):
        whole, kv_sum = project_kv(parts, wkv, rows)
        chunks = lax.all_to_all(kv_sum.reshape(8, rows // 4, HEAD), ("xh", "yl", "core"), 0, 0)
        chunks = jnp.sum(chunks.reshape(2, 2, 2, rows // 4, HEAD), axis=(0, 2)).astype(BF16)
        kv = jnp.concatenate([chunks[0], chunks[1]], axis=1)

    with jax.named_scope("gather_kv"):
        other = swap(whole)
        kv, wq = lax.optimization_barrier((lax.all_gather(kv, "zh"), wq))

    with jax.named_scope("project_q"):
        kv, q = lax.optimization_barrier((kv, project_q(place, whole, other, wq)))
        kv = lax.all_gather(kv, "zl")
        q = (q + lax.ppermute(q, "xh", [(0, 1), (1, 0)])).astype(BF16)
        pair = lax.ppermute(q, "yl", [(0, 1), (1, 0)])

    with jax.named_scope("attend"):
        swapped = swap(kv)
        out = attend(0, place, q, kv, swapped)
        out = attend(1, place, pair, kv, swapped, out)
        return merge(lax.all_to_all(out, ("xh", "yl"), 0, 0))


def solution(mesh):
    fine = Mesh(mesh.devices.reshape(4, 4, 2, 2, 2, 2, 2), ("zh", "zl", "xh", "xl", "yh", "yl", "core"))
    return jax.shard_map(
        on_device,
        mesh=fine,
        in_specs=(P(ROW, COL), P(COL), P(ROW, COL), P(ROW, None), P(ROW, None)),
        out_specs=P(ROW, COL),
        check_vma=False,
    )
```

```python
import functools
import math

import jax
import jax.numpy as jnp
from jax import lax
from jax.experimental import pallas as pl
from jax.experimental.pallas import tpu as pltpu
from jax.sharding import Mesh
from jax.sharding import PartitionSpec as P

HEAD = 128
GROUP = 8
EPS = 1e-05
ROW = ("zh", "zl", "xh")
COL = ("xl", "yh", "yl", "core")
F32 = jnp.float32
BF16 = jnp.bfloat16


def gather(x, axes, n):
    return lax.all_to_all(jnp.broadcast_to(x[None], (n, *x.shape)), axes, 0, 0)


def swap(x):
    return lax.ppermute(x, "core", [(0, 1), (1, 0)])


def three(x):
    pieces = []
    for _ in range(3):
        piece = x.astype(BF16).astype(F32)
        pieces.append(piece)
        x = x - piece
    return pieces


def attend_kernel(side, place, q_ref, mine_ref, other_ref, *refs):
    out_ref, m_ref, l_ref, acc_ref = refs[-4:]
    z, xh, yl, core = place[0], place[1], place[2], place[3]
    rows = q_ref.shape[1]
    scale = HEAD**-0.5 * math.log2(math.e)
    chunk = mine_ref.shape[2]
    half = 4 * chunk

    def block(group, masked):
        kv = jnp.concatenate(
            [mine_ref[:, group].reshape(half, 2 * HEAD), other_ref[:, group].reshape(half, 2 * HEAD)], axis=0
        )
        if masked:
            shape = (2 * rows, 2 * half)
            slot = lax.broadcasted_iota(jnp.int32, shape, 1)
            within = lax.rem(slot, half)
            owner = jnp.where(slot < half, core, 1 - core) + 4 * xh + 2 * yl
            key_pos = lax.div(within, chunk) * (2 * rows) + owner * chunk + lax.rem(within, chunk)
            query_pos = lax.rem(z, 4) * (2 * rows) + lax.broadcasted_iota(jnp.int32, shape, 0)
            seen = key_pos <= query_pos
        for head in range(2):
            q = q_ref[:, :, head * HEAD : (head + 1) * HEAD].reshape(2 * rows, HEAD)
            s = lax.dot_general(q, kv[:, :HEAD], (((1,), (1,)), ((), ())), preferred_element_type=F32)
            if masked:
                s = jnp.where(seen, s, -1e30)
            m_new = jnp.broadcast_to(jnp.max(s, axis=1, keepdims=True), (2 * rows, HEAD))
            total = jnp.zeros((2 * rows, HEAD), F32)
            if not masked:
                m_old = m_ref[head]
                m_new = jnp.maximum(m_old, m_new)
                alpha = jnp.exp2((m_old - m_new) * scale)
                total = l_ref[head] * alpha
            weights = []
            for j in range(0, s.shape[1], HEAD):
                w = jnp.exp2((s[:, j : j + HEAD] - m_new) * scale)
                total = total + w
                weights.append(w.astype(BF16))
            p = jnp.concatenate(weights, axis=1)
            l_ref[head] = total
            m_ref[head] = m_new
            mixed = jnp.dot(p, kv[:, HEAD:], preferred_element_type=F32)
            acc_ref[head] = mixed if masked else acc_ref[head] * alpha + mixed

    last = lax.div(z, 4)

    block(last, True)

    @pl.loop(0, last)
    def _(group):
        block(group, False)

    lane = lax.broadcasted_iota(jnp.int32, (2 * rows, HEAD), 1)
    to = yl if side == 0 else 1 - yl
    stats = jnp.zeros((2 * rows, HEAD), F32)
    for head in range(2):
        total = jnp.sum(l_ref[head], axis=1, keepdims=True)
        stats = jnp.where(lane == head, m_ref[head] * scale + jnp.log2(total), stats)
        part = (acc_ref[head] / total).astype(BF16)
        for x in range(2):
            out_ref[2 * x + to, :rows, head * HEAD : (head + 1) * HEAD] = part[x * rows : (x + 1) * rows]
    for x in range(2):
        sums = three(jnp.transpose(stats[x * rows : (x + 1) * rows])[:2])
        sums = jnp.concatenate([*sums, jnp.zeros((10, 2 * HEAD), F32)], axis=0)
        out_ref[2 * x + to, rows:, :] = sums.astype(BF16)


def attend(side, place, q, mine, other, *first):
    rows, cols = q.shape[1:]
    vmem = pl.BlockSpec(memory_space=pltpu.VMEM)
    return pl.pallas_call(
        functools.partial(attend_kernel, side),
        out_shape=jax.ShapeDtypeStruct((4, rows + 16, cols), BF16),
        in_specs=[pl.BlockSpec(memory_space=pltpu.SMEM)] + [vmem] * (3 + len(first)),
        out_specs=vmem,
        scratch_shapes=[pltpu.VMEM((2, 2 * rows, HEAD), F32)] * 3,
        input_output_aliases={4: 0} if first else {},
        compiler_params=pltpu.CompilerParams(vmem_limit_bytes=40 * 1024 * 1024),
        cost_estimate=pl.CostEstimate(flops=2**30, bytes_accessed=2**22, transcendentals=2**21),
    )(place, q, mine, other, *first)


def merge_kernel(parts_ref, out_ref):
    rows = out_ref.shape[0]
    n = parts_ref.shape[0]
    sums = [parts_ref[i, rows:, :].astype(F32) for i in range(n)]
    sums = [s[0:2] + s[2:4] + s[4:6] for s in sums]
    most = functools.reduce(jnp.maximum, sums)
    shares = [jnp.exp2(s - most) for s in sums]
    total = functools.reduce(jnp.add, shares)
    columns = [jnp.transpose(jnp.concatenate([s / total] * (HEAD // 2), axis=0)) for s in shares]
    for i in range(2):
        at = slice(i * HEAD, (i + 1) * HEAD)
        out_ref[:, at] = sum(columns[k][:, i : i + 1] * parts_ref[k, :rows, at].astype(F32) for k in range(n)).astype(BF16)


def merge(parts):
    vmem = pl.BlockSpec(memory_space=pltpu.VMEM)
    return pl.pallas_call(
        merge_kernel,
        out_shape=jax.ShapeDtypeStruct((parts.shape[1] - 16, parts.shape[2]), BF16),
        in_specs=[vmem],
        out_specs=vmem,
        compiler_params=pltpu.CompilerParams(vmem_limit_bytes=40 * 1024 * 1024),
    )(parts)


def prep_kernel(tokens_ref, gain_ref, w_ref, out_ref, padded_ref, block_ref, sems):
    rows = tokens_ref.shape[0]
    states = tokens_ref[...].astype(F32)
    sums = jnp.sum(states * states, axis=1, keepdims=True)
    left = jnp.transpose(jnp.broadcast_to(sums, (rows, HEAD)))[:1]
    pieces = three(jnp.concatenate([left[:, :HEAD], left[:, HEAD:]], axis=0))
    for q in range(4):
        at = slice(q * HEAD, (q + 1) * HEAD)
        gain = gain_ref[at].astype(F32).reshape(1, HEAD)
        extra = jnp.concatenate([*pieces, gain, jnp.zeros((9, HEAD), F32)], axis=0)
        block_ref[q // 2, q % 2, :rows] = tokens_ref[:, at]
        block_ref[q // 2, q % 2, rows:] = extra.astype(BF16)
    copies = [
        pltpu.make_async_copy(block_ref, out_ref.at[:, to], sems.at[to]) for to in range(out_ref.shape[1])
    ]
    for copy in copies:
        copy.start()
    depth = w_ref.shape[0]
    padded_ref[:depth] = w_ref[...]
    padded_ref[depth:] = jnp.zeros((padded_ref.shape[0] - depth, w_ref.shape[1]), BF16)
    for copy in copies:
        copy.wait()


def prep(tokens, gain, w):
    vmem = pl.BlockSpec(memory_space=pltpu.VMEM)
    rows = tokens.shape[0] + 16
    return pl.pallas_call(
        prep_kernel,
        out_shape=(
            jax.ShapeDtypeStruct((2, 8, 2, rows, HEAD), BF16),
            jax.ShapeDtypeStruct((w.shape[0] + 64, w.shape[1]), BF16),
        ),
        in_specs=[vmem, vmem, vmem],
        out_specs=(pl.BlockSpec(memory_space=pltpu.HBM), vmem),
        scratch_shapes=[pltpu.VMEM((2, 2, rows, HEAD), BF16), pltpu.SemaphoreType.DMA((8,))],
        compiler_params=pltpu.CompilerParams(vmem_limit_bytes=60 * 1024 * 1024),
    )(tokens, gain, w)


def kv_kernel(parts_ref, w_ref, out_ref, kv_ref, t_ref, sems):
    rows = t_ref.shape[1]
    blocks = parts_ref.shape[1]
    copies = [pltpu.make_async_copy(t_ref.at[xh], out_ref.at[xh], sems.at[xh]) for xh in range(2)]
    for xh in range(2):
        extra = [parts_ref[xh, c, rows:].astype(F32) for c in range(blocks)]
        squares = functools.reduce(jnp.add, extra)
        mean_sq = (squares[4:6] + squares[2:4] + squares[0:2]) / (blocks * 4 * HEAD)
        inverse = lax.rsqrt(mean_sq + EPS)
        inverse = jnp.concatenate(
            [jnp.transpose(jnp.broadcast_to(inverse[i : i + 1], (HEAD, HEAD))) for i in range(2)], axis=0
        )
        total = jnp.zeros((rows, HEAD), F32)
        for c in range(0, blocks, 2):
            for d in (c, c + 1):
                t = parts_ref[xh, d, :rows].astype(F32) * inverse * extra[d][6:7]
                t_ref[xh, :, d * HEAD : (d + 1) * HEAD] = t.astype(BF16)
            w = jnp.concatenate([w_ref[d % 4, d // 4] for d in (c, c + 1)], axis=0)
            total += jnp.dot(t_ref[xh, :, c * HEAD : (c + 2) * HEAD], w, preferred_element_type=F32)
        kv_ref[xh] = total
        copies[xh].start()
    for copy in copies:
        copy.wait()


def project_kv(parts, w, rows):
    vmem = pl.BlockSpec(memory_space=pltpu.VMEM)
    blocks = parts.shape[1]
    return pl.pallas_call(
        kv_kernel,
        out_shape=(
            jax.ShapeDtypeStruct((2, rows, blocks * HEAD), BF16),
            jax.ShapeDtypeStruct((2, rows, HEAD), F32),
        ),
        in_specs=[vmem, vmem],
        out_specs=(pl.BlockSpec(memory_space=pltpu.HBM), vmem),
        scratch_shapes=[pltpu.VMEM((2, rows, blocks * HEAD), BF16), pltpu.SemaphoreType.DMA((2,))],
        compiler_params=pltpu.CompilerParams(vmem_limit_bytes=40 * 1024 * 1024),
        cost_estimate=pl.CostEstimate(flops=2**28, bytes_accessed=5 * 2**20, transcendentals=0),
    )(parts, w)


def q_kernel(place, mine_ref, other_ref, w_ref, out_ref):
    core = place[3]
    rows = mine_ref.shape[1]
    half = mine_ref.shape[2] // w_ref.shape[0]
    for x in range(2):
        total = jnp.zeros((rows, w_ref.shape[2]), F32)
        for c in range(w_ref.shape[0]):
            t = jnp.concatenate([ref[x, :, c * half : (c + 1) * half] for ref in (mine_ref, other_ref)], axis=1)
            w = jnp.concatenate(
                [w_ref[c, pl.ds(pl.multiple_of(at * half, half), half)] for at in (core, 1 - core)], axis=0
            )
            total += jnp.dot(t, w, preferred_element_type=F32)
        out_ref[x] = total


def project_q(place, mine, other, w):
    vmem = pl.BlockSpec(memory_space=pltpu.VMEM)
    return pl.pallas_call(
        q_kernel,
        out_shape=jax.ShapeDtypeStruct((*mine.shape[:2], w.shape[2]), F32),
        in_specs=[pl.BlockSpec(memory_space=pltpu.SMEM), vmem, vmem, vmem],
        out_specs=vmem,
        compiler_params=pltpu.CompilerParams(vmem_limit_bytes=40 * 1024 * 1024),
        cost_estimate=pl.CostEstimate(flops=2**30, bytes_accessed=6 * 2**20, transcendentals=0),
    )(place, mine, other, w)


def on_device(tokens, norm_gain, w_query, w_key, w_value):
    at = lax.axis_index
    core = at("core")
    place = jnp.stack([at(("zh", "zl")), at("xh"), at("yl"), core]).astype(jnp.int32)
    rows, feats = tokens.shape
    half = w_key.shape[0] // 2

    with jax.named_scope("prep"):
        parts, padded = prep(tokens, norm_gain, w_query)

    with jax.named_scope("weights"):
        wq = lax.all_gather(padded, ("zh", "zl"), axis=0)
        start = (core * half, at(("xl", "yh")) * HEAD)
        wkv = jnp.where(
            at("yl") == 0,
            lax.dynamic_slice(w_key, start, (half, HEAD)),
            lax.dynamic_slice(w_value, start, (half, HEAD)),
        )
        wkv = lax.all_gather(lax.all_gather(wkv, "zh"), "zl")

    with jax.named_scope("spread"):
        parts = lax.all_to_all(parts.reshape(32, rows + 16, HEAD), ("xh",) + COL, 0, 0)
        parts = parts.reshape(2, 16, rows + 16, HEAD)

    with jax.named_scope("project_kv"):
        whole, kv_sum = project_kv(parts, wkv, rows)
        chunks = lax.all_to_all(kv_sum.reshape(8, rows // 4, HEAD), ("xh", "yl", "core"), 0, 0)
        chunks = jnp.sum(chunks.reshape(2, 2, 2, rows // 4, HEAD), axis=(0, 2)).astype(BF16)
        kv = jnp.concatenate([chunks[0], chunks[1]], axis=1)

    with jax.named_scope("gather_kv"):
        kv, wq = lax.optimization_barrier((lax.all_gather(kv, "zh"), wq))
        kv = gather(kv, "zl", 4)

    with jax.named_scope("project_q"):
        q = project_q(place, whole, swap(whole), wq)
        q = (q + lax.ppermute(q, "xh", [(0, 1), (1, 0)])).astype(BF16)
        pair = lax.ppermute(q, "yl", [(0, 1), (1, 0)])

    with jax.named_scope("attend"):
        swapped = swap(kv)
        out = attend(0, place, q, kv, swapped)
        out = attend(1, place, pair, kv, swapped, out)
        return merge(lax.all_to_all(out, ("xh", "yl"), 0, 0))


def solution(mesh):
    fine = Mesh(mesh.devices.reshape(4, 4, 2, 2, 2, 2, 2), ("zh", "zl", "xh", "xl", "yh", "yl", "core"))
    return jax.shard_map(
        on_device,
        mesh=fine,
        in_specs=(P(ROW, COL), P(COL), P(ROW, COL), P(ROW, None), P(ROW, None)),
        out_specs=P(ROW, COL),
        check_vma=False,
    )
```

```python
import functools
import math

import jax
import jax.numpy as jnp
from jax import lax
from jax.experimental import pallas as pl
from jax.experimental.pallas import tpu as pltpu
from jax.sharding import Mesh
from jax.sharding import PartitionSpec as P

HEAD = 128
GROUP = 8
EPS = 1e-05
ROW = ("zh", "zl", "xh")
COL = ("xl", "yh", "yl", "core")
F32 = jnp.float32
BF16 = jnp.bfloat16


def gather(x, axes, n):
    return lax.all_to_all(jnp.broadcast_to(x[None], (n, *x.shape)), axes, 0, 0)


def swap(x):
    return lax.ppermute(x, "core", [(0, 1), (1, 0)])


def three(x):
    pieces = []
    for _ in range(3):
        piece = x.astype(BF16).astype(F32)
        pieces.append(piece)
        x = x - piece
    return pieces


def attend_kernel(side, place, q_ref, mine_ref, other_ref, *refs):
    out_ref, m_ref, l_ref, acc_ref = refs[-4:]
    z, xh, yl, core = place[0], place[1], place[2], place[3]
    rows = q_ref.shape[1]
    scale = HEAD**-0.5 * math.log2(math.e)
    m_ref[...] = jnp.full(m_ref.shape, -1e30, F32)
    l_ref[...] = jnp.zeros(l_ref.shape, F32)
    acc_ref[...] = jnp.zeros(acc_ref.shape, F32)
    chunk = mine_ref.shape[2]
    half = 4 * chunk

    def block(group, masked):
        kv = jnp.concatenate(
            [mine_ref[:, group].reshape(half, 2 * HEAD), other_ref[:, group].reshape(half, 2 * HEAD)], axis=0
        )
        if masked:
            shape = (2 * rows, 2 * half)
            slot = lax.broadcasted_iota(jnp.int32, shape, 1)
            within = lax.rem(slot, half)
            owner = jnp.where(slot < half, core, 1 - core) + 4 * xh + 2 * yl
            key_pos = lax.div(within, chunk) * (2 * rows) + owner * chunk + lax.rem(within, chunk)
            query_pos = lax.rem(z, 4) * (2 * rows) + lax.broadcasted_iota(jnp.int32, shape, 0)
            seen = key_pos <= query_pos
        for head in range(2):
            q = q_ref[:, :, head * HEAD : (head + 1) * HEAD].reshape(2 * rows, HEAD)
            s = lax.dot_general(q, kv[:, :HEAD], (((1,), (1,)), ((), ())), preferred_element_type=F32)
            if masked:
                s = jnp.where(seen, s, -1e30)
            m_old = m_ref[head]
            m_new = jnp.maximum(m_old, jnp.max(s, axis=1, keepdims=True))
            alpha = jnp.exp2((m_old - m_new) * scale)
            total = l_ref[head] * alpha
            weights = []
            for j in range(0, s.shape[1], HEAD):
                w = jnp.exp2((s[:, j : j + HEAD] - m_new) * scale)
                total = total + w
                weights.append(w.astype(BF16))
            p = jnp.concatenate(weights, axis=1)
            l_ref[head] = total
            m_ref[head] = m_new
            acc_ref[head] = acc_ref[head] * alpha + jnp.dot(p, kv[:, HEAD:], preferred_element_type=F32)

    last = lax.div(z, 4)

    @pl.loop(0, last)
    def _(group):
        block(group, False)

    block(last, True)
    lane = lax.broadcasted_iota(jnp.int32, (2 * rows, HEAD), 1)
    to = yl if side == 0 else 1 - yl
    stats = jnp.zeros((2 * rows, HEAD), F32)
    for head in range(2):
        total = jnp.sum(l_ref[head], axis=1, keepdims=True)
        stats = jnp.where(lane == head, m_ref[head] * scale + jnp.log2(total), stats)
        part = (acc_ref[head] / total).astype(BF16)
        for x in range(2):
            out_ref[2 * x + to, :rows, head * HEAD : (head + 1) * HEAD] = part[x * rows : (x + 1) * rows]
    for x in range(2):
        sums = three(jnp.transpose(stats[x * rows : (x + 1) * rows])[:2])
        sums = jnp.concatenate([*sums, jnp.zeros((10, 2 * HEAD), F32)], axis=0)
        out_ref[2 * x + to, rows:, :] = sums.astype(BF16)


def attend(side, place, q, mine, other, *first):
    rows, cols = q.shape[1:]
    vmem = pl.BlockSpec(memory_space=pltpu.VMEM)
    return pl.pallas_call(
        functools.partial(attend_kernel, side),
        out_shape=jax.ShapeDtypeStruct((4, rows + 16, cols), BF16),
        in_specs=[pl.BlockSpec(memory_space=pltpu.SMEM)] + [vmem] * (3 + len(first)),
        out_specs=vmem,
        scratch_shapes=[pltpu.VMEM((2, 2 * rows, HEAD), F32)] * 3,
        input_output_aliases={4: 0} if first else {},
        compiler_params=pltpu.CompilerParams(vmem_limit_bytes=40 * 1024 * 1024),
        cost_estimate=pl.CostEstimate(flops=2**30, bytes_accessed=2**22, transcendentals=2**21),
    )(place, q, mine, other, *first)


def merge_kernel(parts_ref, out_ref):
    rows = out_ref.shape[0]
    n = parts_ref.shape[0]
    sums = [parts_ref[i, rows:, :].astype(F32) for i in range(n)]
    sums = [s[0:2] + s[2:4] + s[4:6] for s in sums]
    most = functools.reduce(jnp.maximum, sums)
    shares = [jnp.exp2(s - most) for s in sums]
    total = functools.reduce(jnp.add, shares)
    columns = [jnp.transpose(jnp.concatenate([s / total] * (HEAD // 2), axis=0)) for s in shares]
    for i in range(2):
        at = slice(i * HEAD, (i + 1) * HEAD)
        out_ref[:, at] = sum(columns[k][:, i : i + 1] * parts_ref[k, :rows, at].astype(F32) for k in range(n)).astype(BF16)


def merge(parts):
    vmem = pl.BlockSpec(memory_space=pltpu.VMEM)
    return pl.pallas_call(
        merge_kernel,
        out_shape=jax.ShapeDtypeStruct((parts.shape[1] - 16, parts.shape[2]), BF16),
        in_specs=[vmem],
        out_specs=vmem,
        compiler_params=pltpu.CompilerParams(vmem_limit_bytes=40 * 1024 * 1024),
    )(parts)


def prep_kernel(tokens_ref, gain_ref, w_ref, out_ref, padded_ref, block_ref, sems):
    rows = tokens_ref.shape[0]
    states = tokens_ref[...].astype(F32)
    sums = jnp.sum(states * states, axis=1, keepdims=True)
    left = jnp.transpose(jnp.broadcast_to(sums, (rows, HEAD)))[:1]
    pieces = three(jnp.concatenate([left[:, :HEAD], left[:, HEAD:]], axis=0))
    for q in range(4):
        at = slice(q * HEAD, (q + 1) * HEAD)
        gain = gain_ref[at].astype(F32).reshape(1, HEAD)
        extra = jnp.concatenate([*pieces, gain, jnp.zeros((9, HEAD), F32)], axis=0)
        block_ref[q // 2, q % 2, :rows] = tokens_ref[:, at]
        block_ref[q // 2, q % 2, rows:] = extra.astype(BF16)
    copies = [
        pltpu.make_async_copy(block_ref, out_ref.at[:, to], sems.at[to]) for to in range(out_ref.shape[1])
    ]
    for copy in copies:
        copy.start()
    depth = w_ref.shape[0]
    padded_ref[:depth] = w_ref[...]
    padded_ref[depth:] = jnp.zeros((padded_ref.shape[0] - depth, w_ref.shape[1]), BF16)
    for copy in copies:
        copy.wait()


def prep(tokens, gain, w):
    vmem = pl.BlockSpec(memory_space=pltpu.VMEM)
    rows = tokens.shape[0] + 16
    return pl.pallas_call(
        prep_kernel,
        out_shape=(
            jax.ShapeDtypeStruct((2, 8, 2, rows, HEAD), BF16),
            jax.ShapeDtypeStruct((w.shape[0] + 64, w.shape[1]), BF16),
        ),
        in_specs=[vmem, vmem, vmem],
        out_specs=(pl.BlockSpec(memory_space=pltpu.HBM), vmem),
        scratch_shapes=[pltpu.VMEM((2, 2, rows, HEAD), BF16), pltpu.SemaphoreType.DMA((8,))],
        compiler_params=pltpu.CompilerParams(vmem_limit_bytes=60 * 1024 * 1024),
    )(tokens, gain, w)


def kv_kernel(parts_ref, w_ref, out_ref, kv_ref, t_ref, sems):
    rows = t_ref.shape[1]
    blocks = parts_ref.shape[1]
    copies = [pltpu.make_async_copy(t_ref.at[xh], out_ref.at[xh], sems.at[xh]) for xh in range(2)]
    for xh in range(2):
        extra = [parts_ref[xh, c, rows:].astype(F32) for c in range(blocks)]
        squares = functools.reduce(jnp.add, extra)
        mean_sq = (squares[4:6] + squares[2:4] + squares[0:2]) / (blocks * 4 * HEAD)
        inverse = lax.rsqrt(mean_sq + EPS)
        inverse = jnp.concatenate(
            [jnp.transpose(jnp.broadcast_to(inverse[i : i + 1], (HEAD, HEAD))) for i in range(2)], axis=0
        )
        total = jnp.zeros((rows, HEAD), F32)
        for c in range(0, blocks, 2):
            for d in (c, c + 1):
                t = parts_ref[xh, d, :rows].astype(F32) * inverse * extra[d][6:7]
                t_ref[xh, :, d * HEAD : (d + 1) * HEAD] = t.astype(BF16)
            w = jnp.concatenate([w_ref[d % 4, d // 4] for d in (c, c + 1)], axis=0)
            total += jnp.dot(t_ref[xh, :, c * HEAD : (c + 2) * HEAD], w, preferred_element_type=F32)
        kv_ref[xh] = total
        copies[xh].start()
    for copy in copies:
        copy.wait()


def project_kv(parts, w, rows):
    vmem = pl.BlockSpec(memory_space=pltpu.VMEM)
    blocks = parts.shape[1]
    return pl.pallas_call(
        kv_kernel,
        out_shape=(
            jax.ShapeDtypeStruct((2, rows, blocks * HEAD), BF16),
            jax.ShapeDtypeStruct((2, rows, HEAD), F32),
        ),
        in_specs=[vmem, vmem],
        out_specs=(pl.BlockSpec(memory_space=pltpu.HBM), vmem),
        scratch_shapes=[pltpu.VMEM((2, rows, blocks * HEAD), BF16), pltpu.SemaphoreType.DMA((2,))],
        compiler_params=pltpu.CompilerParams(vmem_limit_bytes=40 * 1024 * 1024),
        cost_estimate=pl.CostEstimate(flops=2**28, bytes_accessed=5 * 2**20, transcendentals=0),
    )(parts, w)


def q_kernel(place, mine_ref, other_ref, w_ref, out_ref):
    core = place[3]
    rows = mine_ref.shape[1]
    half = mine_ref.shape[2] // w_ref.shape[0]
    for x in range(2):
        total = jnp.zeros((rows, w_ref.shape[2]), F32)
        for c in range(w_ref.shape[0]):
            t = jnp.concatenate([ref[x, :, c * half : (c + 1) * half] for ref in (mine_ref, other_ref)], axis=1)
            w = jnp.concatenate(
                [w_ref[c, pl.ds(pl.multiple_of(at * half, half), half)] for at in (core, 1 - core)], axis=0
            )
            total += jnp.dot(t, w, preferred_element_type=F32)
        out_ref[x] = total


def project_q(place, mine, other, w):
    vmem = pl.BlockSpec(memory_space=pltpu.VMEM)
    return pl.pallas_call(
        q_kernel,
        out_shape=jax.ShapeDtypeStruct((*mine.shape[:2], w.shape[2]), F32),
        in_specs=[pl.BlockSpec(memory_space=pltpu.SMEM), vmem, vmem, vmem],
        out_specs=vmem,
        compiler_params=pltpu.CompilerParams(vmem_limit_bytes=40 * 1024 * 1024),
        cost_estimate=pl.CostEstimate(flops=2**30, bytes_accessed=6 * 2**20, transcendentals=0),
    )(place, mine, other, w)


def on_device(tokens, norm_gain, w_query, w_key, w_value):
    at = lax.axis_index
    core = at("core")
    place = jnp.stack([at(("zh", "zl")), at("xh"), at("yl"), core]).astype(jnp.int32)
    rows, feats = tokens.shape
    half = w_key.shape[0] // 2

    with jax.named_scope("prep"):
        parts, padded = prep(tokens, norm_gain, w_query)

    with jax.named_scope("weights"):
        wq = lax.all_gather(padded, ("zh", "zl"), axis=0)
        start = (core * half, at(("xl", "yh")) * HEAD)
        wkv = jnp.where(
            at("yl") == 0,
            lax.dynamic_slice(w_key, start, (half, HEAD)),
            lax.dynamic_slice(w_value, start, (half, HEAD)),
        )
        wkv = lax.all_gather(lax.all_gather(wkv, "zh"), "zl")

    with jax.named_scope("spread"):
        parts = lax.all_to_all(parts.reshape(32, rows + 16, HEAD), ("xh",) + COL, 0, 0)
        parts = parts.reshape(2, 16, rows + 16, HEAD)

    with jax.named_scope("project_kv"):
        whole, kv_sum = project_kv(parts, wkv, rows)
        chunks = lax.all_to_all(kv_sum.reshape(8, rows // 4, HEAD), ("xh", "yl", "core"), 0, 0)
        chunks = jnp.sum(chunks.reshape(2, 2, 2, rows // 4, HEAD), axis=(0, 2)).astype(BF16)
        kv = jnp.concatenate([chunks[0], chunks[1]], axis=1)

    with jax.named_scope("gather_kv"):
        kv, whole = lax.optimization_barrier((kv, whole))
        other = swap(whole)
        kv, wq = lax.optimization_barrier((lax.all_gather(kv, "zh"), wq))
        kv = gather(kv, "zl", 4)

    with jax.named_scope("project_q"):
        q = project_q(place, whole, other, wq)
        q = (q + lax.ppermute(q, "xh", [(0, 1), (1, 0)])).astype(BF16)
        pair = lax.ppermute(q, "yl", [(0, 1), (1, 0)])

    with jax.named_scope("attend"):
        swapped = swap(kv)
        out = attend(0, place, q, kv, swapped)
        out = attend(1, place, pair, kv, swapped, out)
        return merge(lax.all_to_all(out, ("xh", "yl"), 0, 0))


def solution(mesh):
    fine = Mesh(mesh.devices.reshape(4, 4, 2, 2, 2, 2, 2), ("zh", "zl", "xh", "xl", "yh", "yl", "core"))
    return jax.shard_map(
        on_device,
        mesh=fine,
        in_specs=(P(ROW, COL), P(COL), P(ROW, COL), P(ROW, None), P(ROW, None)),
        out_specs=P(ROW, COL),
        check_vma=False,
    )
```
